32 devices in a mesh: grp: 2 (over x), row: 16 (over z, y, core).
Axes of the slice: x: 2, y: 2, z: 4, core: 2. Of those that a mesh axis runs over, the one named last changes fastest.
Arguments:
- cand_embed: bfloat16 [32768, 256], P(('grp', 'row')), parts along dimension 0, may hold values from -8 to 8
- cand_labels: int32 [32768], P(('grp', 'row')), parts along dimension 0, may hold values from 0 to 31
- tgt_embed: bfloat16 [4096, 256], P(('grp', 'row')), parts along dimension 0, may hold values from -8 to 8
- tgt_labels: int32 [4096], P(('grp', 'row')), parts along dimension 0, may hold values from 0 to 31
Outputs:
- cand_potential: float32 [32, 32768], P(None, ('grp', 'row')), parts along dimension 1
- tgt_scaling: float32 [32, 4096], P(None, ('grp', 'row')), parts along dimension 1
- coupling_mass: float32 [32, 32768], P(None, ('grp', 'row')), parts along dimension 1
The draws below stay inside these ranges and needn't reach their ends.
There are 2 independent parts, one for each index of `grp`. The reference program is written for one: setup_inputs(seed, part) draws one part's arguments, and reference() takes and returns one part's arrays. A program takes and returns all parts, laid end to end along the dimension named above; each array names one. Nothing has to cross between parts.
All inputs are finite; a program needn't handle non-finite values.
Results may differ from the reference program's by a relative error of at most 0.0027.
Values may be sent and summed in bfloat16 or wider, within the bound.
No kernel may reach another device: no remote copies, remote signals or barrier semaphores. Data moves between devices by JAX's collectives and lax.ppermute only.
A program may use at most 64 MiB of HBM per device.

```python
import math
import jax
import jax.numpy as jnp
from jax import lax

E = 256
CLASSES = 32
ITERS = 3
NC = 16384
NT = 2048


def cand_classes(key):
    inner = jax.random.fold_in(key, 101)
    first = jax.random.randint(jax.random.fold_in(inner, 1), (NC,), 0, CLASSES)
    second = jax.random.randint(jax.random.fold_in(inner, 2), (NC,), 0, 2 * CLASSES)
    return jnp.minimum(first, second).astype(jnp.int32)


def tgt_classes(key):
    inner = jax.random.fold_in(key, 202)
    first = jax.random.randint(jax.random.fold_in(inner, 1), (NT,), 0, CLASSES)
    second = jax.random.randint(jax.random.fold_in(inner, 2), (NT,), -CLASSES, CLASSES)
    return jnp.maximum(first, second).astype(jnp.int32)


def class_centroids(key):
    return jax.random.normal(jax.random.fold_in(key, 505), (CLASSES, E), jnp.float32)


def mix_rows(labels, centers, noise, center_weight):
    rows = center_weight * jnp.take(centers, labels, axis=0) + noise
    return jnp.clip(rows, -8.0, 8.0).astype(jnp.bfloat16)


def draw_cand_labels(key, part):
    return cand_classes(key)


def draw_tgt_labels(key, part):
    return tgt_classes(key)


def draw_cand_embed(key, part):
    labels = cand_classes(key)
    centers = class_centroids(key)
    key = jax.random.fold_in(key, 11)
    count = labels.shape[0]
    noise = jax.random.normal(jax.random.fold_in(key, 1), (count, E), jnp.float32)
    return mix_rows(labels, centers, noise, 0.6)


def draw_tgt_embed(key, part):
    labels = tgt_classes(key)
    centers = class_centroids(key)
    key = jax.random.fold_in(key, 13)
    count = labels.shape[0]
    noise = jax.random.normal(jax.random.fold_in(key, 1), (count, E), jnp.float32)
    return mix_rows(labels, centers, noise, 0.6)


def setup_inputs(seed: int = 0, part: int = 0) -> dict:
    key_of = jax.random.split(jax.random.key(seed), 5)
    own_keys = jax.random.split(jax.random.fold_in(key_of[4], part), 5)
    return {
        "cand_embed": draw_cand_embed(jax.random.fold_in(jax.random.fold_in(key_of[4], part), 71), part),
        "cand_labels": draw_cand_labels(jax.random.fold_in(jax.random.fold_in(key_of[4], part), 71), part),
        "tgt_embed": draw_tgt_embed(jax.random.fold_in(jax.random.fold_in(key_of[4], part), 71), part),
        "tgt_labels": draw_tgt_labels(jax.random.fold_in(jax.random.fold_in(key_of[4], part), 71), part),
    }


INVERSE_TEMP = 20.0
ENTROPY_TEMP = 0.05

def unit_rows(values):
    widened = values.astype(jnp.float32)
    meansq = lax.optimization_barrier(jnp.mean(widened * widened, axis=1, keepdims=True))
    return (widened * lax.rsqrt(meansq + 1e-06) / math.sqrt(values.shape[1])).astype(jnp.bfloat16)

def kernel_tile(left_unit, right_unit):
    affinity_scores = jnp.dot(left_unit, right_unit.T, preferred_element_type=jnp.float32)
    return jnp.exp(INVERSE_TEMP * affinity_scores).astype(jnp.bfloat16)

def marginals(labels):
    classes = jnp.arange(CLASSES, dtype=jnp.int32)
    weights = 1.0 + 3.0 * (labels[None, :] == classes[:, None]).astype(jnp.float32)
    return weights / lax.optimization_barrier(jnp.sum(weights, axis=1, keepdims=True))

def reference(cand_embed, cand_labels, tgt_embed, tgt_labels):
    cand_unit = unit_rows(cand_embed)
    tgt_unit = unit_rows(tgt_embed)
    cand_marg = marginals(cand_labels)
    tgt_marg = marginals(tgt_labels)
    block = math.gcd(NC, 2048)
    nblocks = NC // block
    cand_blocks = cand_unit.reshape(nblocks, block, E)
    marg_blocks = cand_marg.reshape(CLASSES, nblocks, block).transpose(1, 0, 2)

    def sweep(scale_vb):

        def visit(column_vector, pieces):
            rows_unit, rows_marg = pieces
            tile = kernel_tile(rows_unit, tgt_unit)
            image = jnp.dot(scale_vb, tile.T, preferred_element_type=jnp.float32)
            candidate_scaling = rows_marg / image
            column_vector = column_vector + jnp.dot(candidate_scaling.astype(jnp.bfloat16), tile, preferred_element_type=jnp.float32)
            return (column_vector, candidate_scaling)
        return lax.scan(visit, jnp.zeros((CLASSES, NT), jnp.float32), (cand_blocks, marg_blocks))
    target_scaling = jnp.ones((CLASSES, NT), jnp.float32)
    u_blocks = marg_blocks
    for step in range(ITERS):
        column_vector, u_blocks = sweep(target_scaling.astype(jnp.bfloat16))
        target_scaling = tgt_marg / column_vector
    final_vb = target_scaling.astype(jnp.bfloat16)

    def finish(carry, pieces):
        rows_unit, rows_u = pieces
        tile = kernel_tile(rows_unit, tgt_unit)
        image = jnp.dot(final_vb, tile.T, preferred_element_type=jnp.float32)
        return (carry, NC * rows_u * image)
    unused, mass_blocks = lax.scan(finish, jnp.zeros((), jnp.float32), (cand_blocks, u_blocks))
    candidate_scaling = u_blocks.transpose(1, 0, 2).reshape(CLASSES, NC)
    coupling_mass = mass_blocks.transpose(1, 0, 2).reshape(CLASSES, NC)
    return (ENTROPY_TEMP * jnp.log(candidate_scaling), target_scaling, coupling_mass)
```

```python
import math

import jax
import jax.numpy as jnp
from jax import lax
from jax.sharding import PartitionSpec as P

CLASSES = 32
ITERS = 3
INVERSE_TEMP = 20.0
ENTROPY_TEMP = 0.05
EXTRA = 16


def unit_rows(values):
    widened = values.astype(jnp.float32)
    meansq = jnp.mean(widened * widened, axis=1, keepdims=True)
    return (widened * lax.rsqrt(meansq + 1e-06) / math.sqrt(values.shape[1])).astype(jnp.bfloat16)


def one_hot(labels):
    classes = jnp.arange(CLASSES, dtype=jnp.int32)
    return (labels[None, :] == classes[:, None]).astype(jnp.float32)


def gather_blocks(block):
    devices = lax.axis_size("row")
    return lax.all_to_all(
        jnp.broadcast_to(block[None], (devices,) + block.shape), "row", 0, 0, tiled=False
    )


def scatter_sum(parts):
    got = lax.all_to_all(parts, "row", 0, 0, tiled=False)
    return jnp.sum(got.astype(jnp.float32), axis=0)


def packed_counts(counts, width):
    high = counts.astype(jnp.bfloat16)
    low = (counts - high.astype(jnp.float32)).astype(jnp.bfloat16)
    row = jnp.concatenate([high, low], axis=0)
    return jnp.pad(row, ((0, EXTRA - 4), (0, width - CLASSES)))


def shards(cand_embed, cand_labels, tgt_embed, tgt_labels):
    devices = lax.axis_size("row")
    cand_rows, width = cand_embed.shape
    tgt_rows = tgt_embed.shape[0]
    cand_hot = one_hot(cand_labels)
    tgt_hot = one_hot(tgt_labels)
    counts = jnp.stack([jnp.sum(cand_hot, axis=1), jnp.sum(tgt_hot, axis=1)])
    message = jnp.concatenate([tgt_embed, packed_counts(counts, width)], axis=0)
    gathered = gather_blocks(message)
    tgt_unit = unit_rows(gathered[:, :tgt_rows].reshape(devices * tgt_rows, width))
    parts = gathered[:, tgt_rows : tgt_rows + 4, :CLASSES].astype(jnp.float32)
    sums = jnp.sum(parts, axis=0)
    cand_total = cand_rows * devices + 3.0 * (sums[0] + sums[2])
    tgt_total = tgt_rows * devices + 3.0 * (sums[1] + sums[3])
    cand_marg = (1.0 + 3.0 * cand_hot) / cand_total[:, None]
    tgt_marg = (1.0 + 3.0 * tgt_hot) / tgt_total[:, None]

    scores = jnp.dot(unit_rows(cand_embed), tgt_unit.T, preferred_element_type=jnp.float32)
    kernel = jnp.exp(INVERSE_TEMP * scores).astype(jnp.bfloat16)

    def row_image(scale_vb):
        return jnp.dot(kernel, scale_vb.T, preferred_element_type=jnp.float32).T

    scale_vb = jnp.ones((CLASSES, tgt_rows * devices), jnp.bfloat16)
    for step in range(ITERS):
        scale_u = cand_marg / row_image(scale_vb)
        column_part = jnp.dot(
            scale_u.astype(jnp.bfloat16), kernel, preferred_element_type=jnp.float32
        )
        blocks = column_part.reshape(CLASSES, devices, tgt_rows).transpose(1, 0, 2)
        column = scatter_sum(blocks.astype(jnp.bfloat16))
        scale_v = tgt_marg / column
        got = gather_blocks(scale_v.astype(jnp.bfloat16))
        scale_vb = got.transpose(1, 0, 2).reshape(CLASSES, devices * tgt_rows)
    coupling_mass = cand_rows * devices * scale_u * row_image(scale_vb)
    return (ENTROPY_TEMP * jnp.log(scale_u), scale_v, coupling_mass)


def solution(mesh):
    return jax.shard_map(
        shards,
        mesh=mesh,
        in_specs=(
            P(("grp", "row"), None),
            P(("grp", "row")),
            P(("grp", "row"), None),
            P(("grp", "row")),
        ),
        out_specs=(P(None, ("grp", "row")), P(None, ("grp", "row")), P(None, ("grp", "row"))),
        check_vma=False,
    )
```

```python
import math

import jax
import jax.numpy as jnp
from jax import lax
from jax.sharding import PartitionSpec as P

CLASSES = 32
ITERS = 3
INVERSE_TEMP = 20.0
ENTROPY_TEMP = 0.05
EXTRA = 16


def unit_rows(values):
    widened = values.astype(jnp.float32)
    meansq = jnp.mean(widened * widened, axis=1, keepdims=True)
    return (widened * lax.rsqrt(meansq + 1e-06) / math.sqrt(values.shape[1])).astype(jnp.bfloat16)


def one_hot(labels):
    classes = jnp.arange(CLASSES, dtype=jnp.int32)
    return (labels[None, :] == classes[:, None]).astype(jnp.float32)


def exchange(block, flip):
    devices = lax.axis_size("row")
    return lax.ppermute(block, "row", [(d, d ^ flip) for d in range(devices)])


def masks(bits):
    found = [0]
    for bit in bits:
        found += [m | (1 << bit) for m in found]
    return found


def gather_blocks(block, stages):
    held = {0: block}
    for bits in stages:
        keys = sorted(held)
        stack = jnp.concatenate([held[k] for k in keys]) if len(keys) > 1 else held[keys[0]]
        rows = block.shape[0]
        got = {flip: exchange(stack, flip) for flip in masks(bits)[1:]}
        for flip, found in got.items():
            for place, k in enumerate(keys):
                held[k | flip] = found[place * rows : (place + 1) * rows]
    return [held[s] for s in range(len(held))]


def scatter_sum(parts):
    got = [exchange(parts[s].astype(jnp.bfloat16), s) for s in range(1, len(parts))]
    total = parts[0]
    for block in got:
        total = total + block.astype(jnp.float32)
    return total


def packed_counts(counts, width):
    high = counts.astype(jnp.bfloat16)
    low = (counts - high.astype(jnp.float32)).astype(jnp.bfloat16)
    row = jnp.concatenate([high, low], axis=0)
    return jnp.pad(row, ((0, EXTRA - 4), (0, width - CLASSES)))


def shards(cand_embed, cand_labels, tgt_embed, tgt_labels):
    devices = lax.axis_size("row")
    top = devices.bit_length() - 1
    pairs = [list(range(low, min(low + 2, top))) for low in range(0, top, 2)]
    cand_rows, width = cand_embed.shape
    tgt_rows = tgt_embed.shape[0]
    cand_hot = one_hot(cand_labels)
    tgt_hot = one_hot(tgt_labels)
    counts = jnp.stack([jnp.sum(cand_hot, axis=1), jnp.sum(tgt_hot, axis=1)])
    message = jnp.concatenate([tgt_embed, packed_counts(counts, width)], axis=0)
    gathered = jnp.stack(gather_blocks(message, pairs[1:] + [[1], [0]]))
    tgt_unit = unit_rows(gathered[:, :tgt_rows].reshape(devices * tgt_rows, width))
    parts = gathered[:, tgt_rows : tgt_rows + 4, :CLASSES].astype(jnp.float32)
    sums = jnp.sum(parts, axis=0)
    cand_total = cand_rows * devices + 3.0 * (sums[0] + sums[2])
    tgt_total = tgt_rows * devices + 3.0 * (sums[1] + sums[3])
    cand_marg = (1.0 + 3.0 * cand_hot) / cand_total[:, None]
    tgt_marg = (1.0 + 3.0 * tgt_hot) / tgt_total[:, None]

    scores = jnp.dot(unit_rows(cand_embed), tgt_unit.T, preferred_element_type=jnp.float32)
    kernel = jnp.exp(INVERSE_TEMP * scores).astype(jnp.bfloat16)

    def row_image(scale_vb):
        return jnp.dot(kernel, scale_vb.T, preferred_element_type=jnp.float32).T

    scale_vb = jnp.ones((CLASSES, tgt_rows * devices), jnp.bfloat16)
    for step in range(ITERS):
        scale_u = cand_marg / row_image(scale_vb)
        column_part = jnp.dot(
            scale_u.astype(jnp.bfloat16), kernel, preferred_element_type=jnp.float32
        )
        blocks = [column_part[:, s * tgt_rows : (s + 1) * tgt_rows] for s in range(devices)]
        scale_v = tgt_marg / scatter_sum(blocks)
        scale_vb = jnp.concatenate(gather_blocks(scale_v.astype(jnp.bfloat16), pairs), axis=1)
    coupling_mass = cand_rows * devices * scale_u * row_image(scale_vb)
    return (ENTROPY_TEMP * jnp.log(scale_u), scale_v, coupling_mass)


def solution(mesh):
    return jax.shard_map(
        shards,
        mesh=mesh,
        in_specs=(
            P(("grp", "row"), None),
            P(("grp", "row")),
            P(("grp", "row"), None),
            P(("grp", "row")),
        ),
        out_specs=(P(None, ("grp", "row")), P(None, ("grp", "row")), P(None, ("grp", "row"))),
        check_vma=False,
    )
```

```python
import functools
import math

import jax
import jax.numpy as jnp
from jax import lax
from jax.experimental import pallas as pl
from jax.experimental.pallas import tpu as pltpu
from jax.sharding import PartitionSpec as P

CLASSES = 32
ITERS = 3
INVERSE_TEMP = 20.0
ENTROPY_TEMP = 0.05
LANES = 128
EXTRA = 16
TILE = 256
F32 = jnp.float32
BF16 = jnp.bfloat16


def exchange(block, bit):
    devices = lax.axis_size("row")
    return lax.ppermute(block, "row", [(d, d ^ (1 << bit)) for d in range(devices)])


def call(body, outs, *args, flops=0):
    space = pl.BlockSpec(memory_space=pltpu.VMEM)
    moved = sum(a.size * a.dtype.itemsize for a in args)
    return pl.pallas_call(
        body,
        out_shape=[pltpu.VMEM(shape, dtype) for shape, dtype in outs],
        in_specs=[space] * len(args),
        out_specs=[space] * len(outs),
        compiler_params=pltpu.CompilerParams(vmem_limit_bytes=24 * 1024 * 1024),
        cost_estimate=pl.CostEstimate(flops=flops, bytes_accessed=moved, transcendentals=0),
    )(*[pltpu.with_memory_space_constraint(a, pltpu.VMEM) for a in args])


def unit_rows(values):
    widened = values.astype(F32)
    meansq = jnp.mean(widened * widened, axis=1, keepdims=True)
    return (widened * lax.rsqrt(meansq + 1e-06) / math.sqrt(values.shape[1])).astype(BF16)


def hot(labels, classes=CLASSES):
    rows = lax.broadcasted_iota(jnp.int32, (classes, labels.shape[1]), 0)
    return (labels == rows).astype(F32)


def pack_body(embed_ref, tgt_ref, cand_ref, out_ref):
    rows = embed_ref.shape[0]
    out_ref[:rows, :] = embed_ref[...]
    out_ref[rows:, :LANES] = jnp.broadcast_to(
        tgt_ref[...].astype(F32), (EXTRA, LANES)
    ).astype(BF16)
    counts = lax.dot_general(
        jnp.ones((EXTRA, cand_ref.shape[1]), BF16),
        hot(cand_ref[...], LANES).astype(BF16),
        (((1,), (1,)), ((), ())),
        preferred_element_type=F32,
    )
    high = counts.astype(BF16).astype(F32)
    even = lax.broadcasted_iota(jnp.int32, (EXTRA, LANES), 0) % 2 == 0
    out_ref[rows:, LANES:] = jnp.where(even, high, counts - high).astype(BF16)


def fill_kernel(unit_ref, held_ref, kernel_ref, tgt_rows):
    rows = tgt_rows + EXTRA
    cand_rows = unit_ref.shape[0]
    per = TILE // tgt_rows
    for col in range(0, kernel_ref.shape[1], TILE):
        first = col // tgt_rows
        block = jnp.concatenate(
            [held_ref[pl.ds((first + s) * rows, tgt_rows), :] for s in range(per)]
        )
        tgt_unit = unit_rows(block)
        for row in range(0, cand_rows, TILE):
            scores = lax.dot_general(
                unit_ref[row : row + TILE, :],
                tgt_unit,
                (((1,), (1,)), ((), ())),
                preferred_element_type=F32,
            )
            kernel_ref[row : row + TILE, col : col + TILE] = jnp.exp(
                INVERSE_TEMP * scores
            ).astype(BF16)


def image_of(kernel_ref, scale_v):
    image = lax.dot_general(
        kernel_ref[...], scale_v, (((1,), (1,)), ((), ())), preferred_element_type=F32
    )
    return image.T


def side_by_side(ref):
    return jnp.concatenate([ref[s] for s in range(ref.shape[0])], axis=1)


def put_column(scale_ub, kernel_ref, out_ref):
    part = jnp.dot(scale_ub, kernel_ref[...], preferred_element_type=F32)
    width = out_ref.shape[2]
    for s in range(out_ref.shape[0]):
        out_ref[s] = part[:, s * width : (s + 1) * width].astype(out_ref.dtype)


def near_body(unit_ref, held_ref, kernel_ref, image_ref, *, tgt_rows):
    fill_kernel(unit_ref, held_ref, kernel_ref, tgt_rows)
    image_ref[...] = image_of(kernel_ref, jnp.ones((CLASSES, kernel_ref.shape[1]), BF16))


def far_body(
    unit_ref, near_ref, far_ref, image_ref, label_ref,
    kernel_ref, marg_ref, tgt_marg_ref, scale_ref, column_ref, *, tgt_rows,
):
    rows = tgt_rows + EXTRA
    slots = tgt_marg_ref.shape[0]
    fill_kernel(unit_ref, far_ref, kernel_ref, tgt_rows)
    counts = jnp.zeros((EXTRA, LANES), F32)
    tgt_total = jnp.zeros((CLASSES, 1), F32)
    for ref in (near_ref, far_ref):
        for s in range(slots):
            extra = ref[pl.ds(s * rows + tgt_rows, EXTRA), :].astype(F32)
            counts += extra[:, LANES:]
            weight = 1.0 + 3.0 * hot(extra[:1, :LANES].astype(jnp.int32))
            tgt_total += jnp.sum(weight, axis=1, keepdims=True)
            if ref is near_ref:
                tgt_marg_ref[s] = weight
    for s in range(slots):
        tgt_marg_ref[s] = tgt_marg_ref[s] / tgt_total
    count = jnp.broadcast_to(counts[:1] + counts[1:2], (LANES, LANES)).T[:CLASSES, :1]
    devices = 2 * slots
    cand_total = unit_ref.shape[0] * devices + 3.0 * count
    marg = (1.0 + 3.0 * hot(label_ref[...])) / cand_total
    marg_ref[...] = marg
    ones = jnp.ones((CLASSES, kernel_ref.shape[1]), BF16)
    scale_ub = (marg / (image_ref[...] + image_of(kernel_ref, ones))).astype(BF16)
    scale_ref[...] = scale_ub
    put_column(scale_ub, kernel_ref, column_ref)


def column_body(scale_ref, kernel_ref, column_ref):
    put_column(scale_ref[...], kernel_ref, column_ref)


def image_body(kernel_ref, scale_ref, image_ref):
    image_ref[...] = image_of(kernel_ref, side_by_side(scale_ref))


def step_body(kernel_ref, scale_ref, image_ref, marg_ref, out_ref, rounded_ref, column_ref):
    image = image_ref[...] + image_of(kernel_ref, side_by_side(scale_ref))
    scale_u = marg_ref[...] / image
    out_ref[...] = scale_u
    rounded_ref[...] = scale_u.astype(BF16)
    put_column(scale_u.astype(BF16), kernel_ref, column_ref)


def last_body(kernel_ref, scale_ref, image_ref, u_ref, mass_ref, potential_ref, *, candidates):
    image = image_ref[...] + image_of(kernel_ref, side_by_side(scale_ref))
    scale_u = u_ref[...]
    mass_ref[...] = candidates * scale_u * image
    potential_ref[...] = ENTROPY_TEMP * jnp.log(scale_u)


def shards(cand_embed, cand_labels, tgt_embed, tgt_labels):
    devices = lax.axis_size("row")
    top = devices.bit_length() - 1
    slots = devices // 2
    cand_rows, width = cand_embed.shape
    tgt_rows = tgt_embed.shape[0]
    half = slots * tgt_rows
    cand_labels = cand_labels.reshape(1, cand_rows)
    block = (slots, CLASSES, tgt_rows)
    image_type = ((CLASSES, cand_rows), F32)
    pass_flops = 2 * cand_rows * half * 128

    (held,) = call(
        pack_body,
        [((tgt_rows + EXTRA, width), BF16)],
        tgt_embed, tgt_labels.reshape(1, tgt_rows), cand_labels,
    )
    cand_unit = unit_rows(cand_embed)
    for bit in range(top - 1, 0, -1):
        held = jnp.concatenate([held, exchange(held, bit)])
    far = exchange(held, 0)
    near_kernel, image = call(
        functools.partial(near_body, tgt_rows=tgt_rows),
        [((cand_rows, half), BF16), image_type],
        cand_unit, held, flops=4 * pass_flops,
    )
    far_kernel, cand_marg, tgt_marg, scale_ub, far_column = call(
        functools.partial(far_body, tgt_rows=tgt_rows),
        [
            ((cand_rows, half), BF16), image_type, (block, F32),
            ((CLASSES, cand_rows), BF16), (block, BF16),
        ],
        cand_unit, held, far, image, cand_labels, flops=5 * pass_flops,
    )
    scale_u = None
    for step in range(ITERS):
        if step:
            scale_u, scale_ub, far_column = call(
                step_body,
                [image_type, ((CLASSES, cand_rows), BF16), (block, BF16)],
                far_kernel, far_vb, image, cand_marg, flops=2 * pass_flops,
            )
        got = exchange(far_column, 0)
        (column,) = call(column_body, [(block, F32)], scale_ub, near_kernel, flops=pass_flops)
        column = column + got.astype(F32)
        for bit in range(1, top):
            got = exchange(column.astype(BF16), bit).astype(F32)
            pair = got.reshape((-1, 2, 1 << (top - 1 - bit)) + block[1:])
            column = column + pair[:, ::-1].reshape(block)
        scale_v = tgt_marg / column
        scale_vb = scale_v.astype(BF16)
        far_vb = exchange(scale_vb, 0)
        (image,) = call(image_body, [image_type], near_kernel, scale_vb, flops=pass_flops)
    mass, potential = call(
        functools.partial(last_body, candidates=float(cand_rows * devices)),
        [image_type, image_type],
        far_kernel, far_vb, image, scale_u, flops=pass_flops,
    )
    return (potential, scale_v[0], mass)


def solution(mesh):
    return jax.shard_map(
        shards,
        mesh=mesh,
        in_specs=(
            P(("grp", "row"), None),
            P(("grp", "row")),
            P(("grp", "row"), None),
            P(("grp", "row")),
        ),
        out_specs=(P(None, ("grp", "row")), P(None, ("grp", "row")), P(None, ("grp", "row"))),
        check_vma=False,
    )
```

```python
import functools
import math

import jax
import jax.numpy as jnp
from jax import lax
from jax.experimental import pallas as pl
from jax.experimental.pallas import tpu as pltpu
from jax.sharding import PartitionSpec as P

CLASSES = 32
ITERS = 3
INVERSE_TEMP = 20.0
ENTROPY_TEMP = 0.05
LANES = 128
EXTRA = 16
TILE = 256
F32 = jnp.float32
BF16 = jnp.bfloat16


def exchange(block, flip):
    devices = lax.axis_size("row")
    return lax.ppermute(block, "row", [(d, d ^ flip) for d in range(devices)])


def call(body, outs, *args, flops=0):
    space = pl.BlockSpec(memory_space=pltpu.VMEM)
    moved = sum(a.size * a.dtype.itemsize for a in args)
    return pl.pallas_call(
        body,
        out_shape=[pltpu.VMEM(shape, dtype) for shape, dtype in outs],
        in_specs=[space] * len(args),
        out_specs=[space] * len(outs),
        compiler_params=pltpu.CompilerParams(vmem_limit_bytes=12 * 1024 * 1024),
        cost_estimate=pl.CostEstimate(flops=flops, bytes_accessed=moved, transcendentals=0),
    )(*[pltpu.with_memory_space_constraint(a, pltpu.VMEM) for a in args])


def unit_rows(values):
    widened = values.astype(F32)
    meansq = jnp.mean(widened * widened, axis=1, keepdims=True)
    return (widened * lax.rsqrt(meansq + 1e-06) / math.sqrt(values.shape[1])).astype(BF16)


def hot(labels, classes=CLASSES):
    rows = lax.broadcasted_iota(jnp.int32, (classes, labels.shape[1]), 0)
    return (labels == rows).astype(F32)


def pack_body(embed_hbm, tgt_hbm, cand_hbm, out_ref, tgt_ref, cand_ref, sems):
    rows = embed_hbm.shape[0]
    copies = [
        pltpu.make_async_copy(cand_hbm, cand_ref, sems.at[0]),
        pltpu.make_async_copy(tgt_hbm, tgt_ref, sems.at[1]),
        pltpu.make_async_copy(embed_hbm, out_ref.at[pl.ds(0, rows)], sems.at[2]),
    ]
    for copy in copies:
        copy.start()
    copies[0].wait()
    counts = lax.dot_general(
        jnp.ones((EXTRA, cand_ref.shape[1]), BF16),
        hot(cand_ref[...], LANES).astype(BF16),
        (((1,), (1,)), ((), ())),
        preferred_element_type=F32,
    )
    high = counts.astype(BF16).astype(F32)
    even = lax.broadcasted_iota(jnp.int32, (EXTRA, LANES), 0) % 2 == 0
    out_ref[rows:, LANES:] = jnp.where(even, high, counts - high).astype(BF16)
    copies[1].wait()
    out_ref[rows:, :LANES] = jnp.broadcast_to(
        tgt_ref[...].astype(F32), (EXTRA, LANES)
    ).astype(BF16)
    copies[2].wait()


def pack(tgt_embed, tgt_labels, cand_labels):
    rows, width = tgt_embed.shape
    anywhere = pl.BlockSpec(memory_space=pl.ANY)
    return pl.pallas_call(
        pack_body,
        out_shape=pltpu.VMEM((rows + EXTRA, width), BF16),
        in_specs=[anywhere] * 3,
        out_specs=pl.BlockSpec(memory_space=pltpu.VMEM),
        scratch_shapes=[
            pltpu.VMEM(tgt_labels.shape, jnp.int32),
            pltpu.VMEM(cand_labels.shape, jnp.int32),
            pltpu.SemaphoreType.DMA((3,)),
        ],
        compiler_params=pltpu.CompilerParams(vmem_limit_bytes=12 * 1024 * 1024),
    )(*[
        pltpu.with_memory_space_constraint(a, pltpu.HBM)
        for a in (tgt_embed, tgt_labels, cand_labels)
    ])


def fill_body(unit_ref, held_ref, kernel_ref, sums_ref, *, tgt_rows):
    rows = tgt_rows + EXTRA
    cand_rows = unit_ref.shape[0]
    per = TILE // tgt_rows
    for col in range(0, kernel_ref.shape[1], TILE):
        first = col // tgt_rows
        block = jnp.concatenate(
            [held_ref[pl.ds((first + s) * rows, tgt_rows), :] for s in range(per)]
        )
        tgt_unit = unit_rows(block)
        for row in range(0, cand_rows, TILE):
            scores = lax.dot_general(
                unit_ref[row : row + TILE, :],
                tgt_unit,
                (((1,), (1,)), ((), ())),
                preferred_element_type=F32,
            )
            tile = jnp.exp(INVERSE_TEMP * scores)
            kernel_ref[row : row + TILE, col : col + TILE] = tile.astype(BF16)
            sums = tile[:, :LANES]
            for lane in range(LANES, TILE, LANES):
                sums += tile[:, lane : lane + LANES]
            if col:
                sums += sums_ref[row : row + TILE, :]
            sums_ref[row : row + TILE, :] = sums


def image_of(kernels, scale_ref):
    image = 0.0
    first = 0
    for kernel_ref in kernels:
        slots = kernel_ref.shape[1] // scale_ref.shape[2]
        scale_v = jnp.concatenate([scale_ref[s] for s in range(first, first + slots)], axis=1)
        image += lax.dot_general(
            kernel_ref[...], scale_v, (((1,), (1,)), ((), ())), preferred_element_type=F32
        )
        first += slots
    return image.T


def put_column(scale_ub, kernels, out_ref):
    width = out_ref.shape[2]
    first = 0
    for kernel_ref in kernels:
        part = jnp.dot(scale_ub, kernel_ref[...], preferred_element_type=F32)
        slots = kernel_ref.shape[1] // width
        for s in range(slots):
            out_ref[first + s] = part[:, s * width : (s + 1) * width].astype(out_ref.dtype)
        first += slots


def extras(refs, tgt_rows):
    rows = tgt_rows + EXTRA
    for ref in refs:
        for s in range(ref.shape[0] // rows):
            yield ref[pl.ds(s * rows + tgt_rows, EXTRA), :].astype(F32)


def target_body(near0, near1, far0, far1, marg_ref):
    slots, _, tgt_rows = marg_ref.shape
    total = jnp.zeros((CLASSES, tgt_rows), F32)
    for s, extra in enumerate(extras((near0, near1, far0, far1), tgt_rows)):
        weight = 1.0 + 3.0 * hot(extra[:1, :LANES].astype(jnp.int32))
        total += weight
        if s < slots:
            marg_ref[s] = weight
    total = jnp.sum(total, axis=1, keepdims=True)
    for s in range(slots):
        marg_ref[s] = marg_ref[s] / total


def first_body(
    far0_ref, far1_ref, sums0, sums1, sums2, sums3, near0, near1, held0, held1, weight_ref,
    marg_ref, scale_ref, column_ref,
):
    tgt_rows = column_ref.shape[2]
    counts = jnp.zeros((EXTRA, LANES), F32)
    for extra in extras((near0, near1, held0, held1), tgt_rows):
        counts += extra[:, LANES:]
    count = jnp.broadcast_to(counts[:1] + counts[1:2], (LANES, LANES)).T[:CLASSES, :1]
    candidates = weight_ref.shape[1] * 2 * column_ref.shape[0]
    marg = weight_ref[...] / (candidates + 3.0 * count)
    marg_ref[...] = marg
    sums = sums0[...] + sums1[...] + sums2[...] + sums3[...]
    image = jnp.sum(sums.T, axis=0, keepdims=True)
    scale_ub = (marg / image).astype(BF16)
    scale_ref[...] = scale_ub
    put_column(scale_ub, (far0_ref, far1_ref), column_ref)


def column_body(scale_ref, kernel0, kernel1, column_ref):
    put_column(scale_ref[...], (kernel0, kernel1), column_ref)


def image_body(kernel0, kernel1, scale_ref, image_ref):
    image_ref[...] = image_of((kernel0, kernel1), scale_ref)


def step_body(
    kernel0, kernel1, scale_ref, image_ref, marg_ref, out_ref, rounded_ref, column_ref
):
    image = image_ref[...] + image_of((kernel0, kernel1), scale_ref)
    scale_u = marg_ref[...] / image
    out_ref[...] = scale_u
    rounded_ref[...] = scale_u.astype(BF16)
    put_column(scale_u.astype(BF16), (kernel0, kernel1), column_ref)


def last_body(kernel0, kernel1, scale_ref, image_ref, u_ref, mass_ref, *, candidates):
    image = image_ref[...] + image_of((kernel0, kernel1), scale_ref)
    mass_ref[...] = candidates * u_ref[...] * image


def other_order(blocks, flip):
    slots = blocks.shape[0]
    bits = slots.bit_length() - 1
    cube = blocks.reshape((2,) * bits + blocks.shape[1:])
    turned = [bit - 1 for bit in range(1, bits + 1) if flip >> bit & 1]
    return jnp.flip(cube, turned).reshape(blocks.shape)


def shards(cand_embed, cand_labels, tgt_embed, tgt_labels):
    devices = lax.axis_size("row")
    top = devices.bit_length() - 1
    slots = devices // 2
    cand_rows, width = cand_embed.shape
    tgt_rows = tgt_embed.shape[0]
    quarter = slots // 2 * tgt_rows
    cand_labels = cand_labels.reshape(1, cand_rows)
    block = (slots, CLASSES, tgt_rows)
    image_type = ((CLASSES, cand_rows), F32)
    rounded_type = ((CLASSES, cand_rows), BF16)
    pass_flops = 2 * cand_rows * quarter * 128

    def fill(held):
        return call(
            functools.partial(fill_body, tgt_rows=tgt_rows),
            [((cand_rows, quarter), BF16), ((cand_rows, LANES), F32)],
            cand_unit, held, flops=4 * pass_flops,
        )

    near = [pack(tgt_embed, tgt_labels.reshape(1, tgt_rows), cand_labels)]
    cand_unit = unit_rows(cand_embed)
    weight = 1.0 + 3.0 * hot(cand_labels)
    for bit in range(top - 1, 1, -1):
        near[0] = jnp.concatenate([near[0], exchange(near[0], 1 << bit)])
        near[0], cand_unit, weight = lax.optimization_barrier((near[0], cand_unit, weight))
    near.append(exchange(near[0], 2))
    far = [exchange(near[0], 1)]
    filled = [fill(near[0]), fill(far[0])]
    near[1], filled = lax.optimization_barrier((near[1], filled))
    far.append(exchange(near[1], 1))
    filled += [fill(near[1]), fill(far[1])]
    kernels, sums = zip(*filled)
    near_kernels, far_kernels = kernels[::2], kernels[1::2]

    cand_marg, scale_ub, far_column = call(
        first_body,
        [image_type, rounded_type, (block, BF16)],
        *far_kernels, *sums, *near, *far, weight, flops=2 * pass_flops,
    )
    (tgt_marg,) = call(target_body, [(block, F32)], *near, *far, flops=pass_flops)
    scale_u = None
    for step in range(ITERS):
        if step:
            scale_u, scale_ub, far_column = call(
                step_body,
                [image_type, rounded_type, (block, BF16)],
                *far_kernels, far_vb, image, cand_marg, flops=4 * pass_flops,
            )
        got = exchange(far_column, 1)
        (column,) = call(
            column_body, [(block, F32)], scale_ub, *near_kernels, flops=2 * pass_flops
        )
        column = column + got.astype(F32)
        for low in range(1, top, 2):
            bits = [1 << bit for bit in range(low, min(low + 2, top))]
            flips = bits + [sum(bits)] if len(bits) > 1 else bits
            sent = column.astype(BF16)
            found = [(flip, exchange(sent, flip)) for flip in flips]
            for flip, got in found:
                column = column + other_order(got, flip).astype(F32)
        scale_v = tgt_marg / column
        scale_vb = scale_v.astype(BF16)
        far_vb = exchange(scale_vb, 1)
        (image,) = call(image_body, [image_type], *near_kernels, scale_vb, flops=2 * pass_flops)
    space = pl.BlockSpec(memory_space=pltpu.VMEM)
    last = [*far_kernels, far_vb, image, scale_u]
    mass = pl.pallas_call(
        functools.partial(last_body, candidates=float(cand_rows * devices)),
        out_shape=jax.ShapeDtypeStruct(*image_type),
        in_specs=[space] * len(last),
        out_specs=space,
        compiler_params=pltpu.CompilerParams(vmem_limit_bytes=12 * 1024 * 1024),
    )(*[pltpu.with_memory_space_constraint(a, pltpu.VMEM) for a in last])
    return (ENTROPY_TEMP * jnp.log(scale_u), scale_v[0], mass)


def solution(mesh):
    return jax.shard_map(
        shards,
        mesh=mesh,
        in_specs=(
            P(("grp", "row"), None),
            P(("grp", "row")),
            P(("grp", "row"), None),
            P(("grp", "row")),
        ),
        out_specs=(P(None, ("grp", "row")), P(None, ("grp", "row")), P(None, ("grp", "row"))),
        check_vma=False,
    )
```

```python
import functools
import math

import jax
import jax.numpy as jnp
from jax import lax
from jax.experimental import pallas as pl
from jax.experimental.pallas import tpu as pltpu
from jax.sharding import PartitionSpec as P

CLASSES = 32
ITERS = 3
INVERSE_TEMP = 20.0
ENTROPY_TEMP = 0.05
LANES = 128
EXTRA = 16
TILE = 256
F32 = jnp.float32
BF16 = jnp.bfloat16


def exchange(block, flip):
    devices = lax.axis_size("row")
    return lax.ppermute(block, "row", [(d, d ^ flip) for d in range(devices)])


def call(body, outs, *args, flops=0):
    space = pl.BlockSpec(memory_space=pltpu.VMEM)
    moved = sum(a.size * a.dtype.itemsize for a in args)
    return pl.pallas_call(
        body,
        out_shape=[pltpu.VMEM(shape, dtype) for shape, dtype in outs],
        in_specs=[space] * len(args),
        out_specs=[space] * len(outs),
        compiler_params=pltpu.CompilerParams(vmem_limit_bytes=12 * 1024 * 1024),
        cost_estimate=pl.CostEstimate(flops=flops, bytes_accessed=moved, transcendentals=0),
    )(*[pltpu.with_memory_space_constraint(a, pltpu.VMEM) for a in args])


def unit_rows(values):
    widened = values.astype(F32)
    meansq = jnp.mean(widened * widened, axis=1, keepdims=True)
    return (widened * lax.rsqrt(meansq + 1e-06) / math.sqrt(values.shape[1])).astype(BF16)


def hot(labels, classes=CLASSES):
    rows = lax.broadcasted_iota(jnp.int32, (classes, labels.shape[1]), 0)
    return (labels == rows).astype(F32)


def pack_body(embed_hbm, tgt_hbm, cand_hbm, out_ref, tgt_ref, cand_ref, sems):
    rows = embed_hbm.shape[0]
    copies = [
        pltpu.make_async_copy(cand_hbm, cand_ref, sems.at[0]),
        pltpu.make_async_copy(tgt_hbm, tgt_ref, sems.at[1]),
        pltpu.make_async_copy(embed_hbm, out_ref.at[pl.ds(0, rows)], sems.at[2]),
    ]
    for copy in copies:
        copy.start()
    copies[0].wait()
    counts = lax.dot_general(
        jnp.ones((EXTRA, cand_ref.shape[1]), BF16),
        hot(cand_ref[...], LANES).astype(BF16),
        (((1,), (1,)), ((), ())),
        preferred_element_type=F32,
    )
    high = counts.astype(BF16).astype(F32)
    even = lax.broadcasted_iota(jnp.int32, (EXTRA, LANES), 0) % 2 == 0
    out_ref[rows:, LANES:] = jnp.where(even, high, counts - high).astype(BF16)
    copies[1].wait()
    out_ref[rows:, :LANES] = jnp.broadcast_to(
        tgt_ref[...].astype(F32), (EXTRA, LANES)
    ).astype(BF16)
    copies[2].wait()


def pack(tgt_embed, tgt_labels, cand_labels):
    rows, width = tgt_embed.shape
    anywhere = pl.BlockSpec(memory_space=pl.ANY)
    return pl.pallas_call(
        pack_body,
        out_shape=pltpu.VMEM((rows + EXTRA, width), BF16),
        in_specs=[anywhere] * 3,
        out_specs=pl.BlockSpec(memory_space=pltpu.VMEM),
        scratch_shapes=[
            pltpu.VMEM(tgt_labels.shape, jnp.int32),
            pltpu.VMEM(cand_labels.shape, jnp.int32),
            pltpu.SemaphoreType.DMA((3,)),
        ],
        compiler_params=pltpu.CompilerParams(vmem_limit_bytes=12 * 1024 * 1024),
    )(*[
        pltpu.with_memory_space_constraint(a, pltpu.HBM)
        for a in (tgt_embed, tgt_labels, cand_labels)
    ])


def fill_body(unit_ref, held_ref, kernel_ref, sums_ref, *, tgt_rows):
    rows = tgt_rows + EXTRA
    cand_rows = unit_ref.shape[0]
    per = TILE // tgt_rows
    for col in range(0, kernel_ref.shape[1], TILE):
        first = col // tgt_rows
        block = jnp.concatenate(
            [held_ref[pl.ds((first + s) * rows, tgt_rows), :] for s in range(per)]
        )
        tgt_unit = unit_rows(block)
        for row in range(0, cand_rows, TILE):
            scores = lax.dot_general(
                unit_ref[row : row + TILE, :],
                tgt_unit,
                (((1,), (1,)), ((), ())),
                preferred_element_type=F32,
            )
            tile = jnp.exp(INVERSE_TEMP * scores)
            kernel_ref[row : row + TILE, col : col + TILE] = tile.astype(BF16)
            sums = tile[:, :LANES]
            for lane in range(LANES, TILE, LANES):
                sums += tile[:, lane : lane + LANES]
            if col:
                sums += sums_ref[row : row + TILE, :]
            sums_ref[row : row + TILE, :] = sums


def image_of(kernels, scale_ref):
    image = 0.0
    first = 0
    for kernel_ref in kernels:
        slots = kernel_ref.shape[1] // scale_ref.shape[2]
        scale_v = jnp.concatenate([scale_ref[s] for s in range(first, first + slots)], axis=1)
        image += lax.dot_general(
            kernel_ref[...], scale_v, (((1,), (1,)), ((), ())), preferred_element_type=F32
        )
        first += slots
    return image.T


def put_column(scale_ub, kernels, out_ref):
    width = out_ref.shape[2]
    first = 0
    for kernel_ref in kernels:
        part = jnp.dot(scale_ub, kernel_ref[...], preferred_element_type=F32)
        slots = kernel_ref.shape[1] // width
        for s in range(slots):
            out_ref[first + s] = part[:, s * width : (s + 1) * width].astype(out_ref.dtype)
        first += slots


def extras(refs, tgt_rows):
    rows = tgt_rows + EXTRA
    for ref in refs:
        for s in range(ref.shape[0] // rows):
            yield ref[pl.ds(s * rows + tgt_rows, EXTRA), :].astype(F32)


def target_body(near0, near1, far0, far1, marg_ref):
    slots, _, tgt_rows = marg_ref.shape
    total = jnp.zeros((CLASSES, tgt_rows), F32)
    for s, extra in enumerate(extras((near0, near1, far0, far1), tgt_rows)):
        weight = 1.0 + 3.0 * hot(extra[:1, :LANES].astype(jnp.int32))
        total += weight
        if s < slots:
            marg_ref[s] = weight
    total = jnp.sum(total, axis=1, keepdims=True)
    for s in range(slots):
        marg_ref[s] = marg_ref[s] / total


def first_body(
    far0_ref, far1_ref, sums0, sums1, sums2, sums3, near0, near1, held0, held1, weight_ref,
    marg_ref, scale_ref, column_ref,
):
    tgt_rows = column_ref.shape[2]
    counts = jnp.zeros((EXTRA, LANES), F32)
    for extra in extras((near0, near1, held0, held1), tgt_rows):
        counts += extra[:, LANES:]
    count = jnp.broadcast_to(counts[:1] + counts[1:2], (LANES, LANES)).T[:CLASSES, :1]
    candidates = weight_ref.shape[1] * 2 * column_ref.shape[0]
    marg = weight_ref[...] / (candidates + 3.0 * count)
    marg_ref[...] = marg
    sums = sums0[...] + sums1[...] + sums2[...] + sums3[...]
    image = jnp.sum(sums.T, axis=0, keepdims=True)
    scale_ub = (marg / image).astype(BF16)
    scale_ref[...] = scale_ub
    put_column(scale_ub, (far0_ref, far1_ref), column_ref)


def column_body(scale_ref, kernel0, kernel1, column_ref):
    put_column(scale_ref[...], (kernel0, kernel1), column_ref)


def image_body(kernel0, kernel1, scale_ref, image_ref):
    image_ref[...] = image_of((kernel0, kernel1), scale_ref)


def step_body(
    kernel0, kernel1, scale_ref, image_ref, marg_ref, out_ref, rounded_ref, column_ref
):
    image = image_ref[...] + image_of((kernel0, kernel1), scale_ref)
    scale_u = marg_ref[...] / image
    out_ref[...] = scale_u
    rounded_ref[...] = scale_u.astype(BF16)
    put_column(scale_u.astype(BF16), (kernel0, kernel1), column_ref)


def last_body(kernel0, kernel1, scale_ref, image_ref, u_ref, mass_ref, *, candidates):
    image = image_ref[...] + image_of((kernel0, kernel1), scale_ref)
    mass_ref[...] = candidates * u_ref[...] * image


def slot_of(slot, flip, slots):
    top = slots.bit_length()
    return slot ^ sum(1 << (top - 1 - bit) for bit in range(1, top) if flip >> bit & 1)


def total_of(slot, own_ref, got_refs, flips):
    total = own_ref[slot]
    for flip, got_ref in zip(flips, got_refs):
        total += got_ref[slot_of(slot, flip, own_ref.shape[0])].astype(F32)
    return total


def sum_body(own_ref, *refs, flips):
    *got_refs, total_ref, sent_ref = refs
    for slot in range(own_ref.shape[0]):
        total = total_of(slot, own_ref, got_refs, flips)
        total_ref[slot] = total
        sent_ref[slot] = total.astype(BF16)


def scale_body(own_ref, marg_ref, *refs, flips):
    *got_refs, scale_ref, rounded_ref = refs
    for slot in range(own_ref.shape[0]):
        scale_v = marg_ref[slot] / total_of(slot, own_ref, got_refs, flips)
        scale_ref[slot] = scale_v
        rounded_ref[slot] = scale_v.astype(BF16)


def shards(cand_embed, cand_labels, tgt_embed, tgt_labels):
    devices = lax.axis_size("row")
    top = devices.bit_length() - 1
    slots = devices // 2
    cand_rows, width = cand_embed.shape
    tgt_rows = tgt_embed.shape[0]
    quarter = slots // 2 * tgt_rows
    cand_labels = cand_labels.reshape(1, cand_rows)
    block = (slots, CLASSES, tgt_rows)
    image_type = ((CLASSES, cand_rows), F32)
    rounded_type = ((CLASSES, cand_rows), BF16)
    pass_flops = 2 * cand_rows * quarter * 128

    def fill(held):
        return call(
            functools.partial(fill_body, tgt_rows=tgt_rows),
            [((cand_rows, quarter), BF16), ((cand_rows, LANES), F32)],
            cand_unit, held, flops=4 * pass_flops,
        )

    near = [pack(tgt_embed, tgt_labels.reshape(1, tgt_rows), cand_labels)]
    cand_unit = unit_rows(cand_embed)
    weight = 1.0 + 3.0 * hot(cand_labels)
    for bit in range(top - 1, 1, -1):
        near[0] = jnp.concatenate([near[0], exchange(near[0], 1 << bit)])
        near[0], cand_unit, weight = lax.optimization_barrier((near[0], cand_unit, weight))
    near.append(exchange(near[0], 2))
    far = [exchange(near[0], 1)]
    filled = [fill(near[0]), fill(far[0])]
    near[1], filled = lax.optimization_barrier((near[1], filled))
    far.append(exchange(near[1], 1))
    filled += [fill(near[1]), fill(far[1])]
    kernels, sums = zip(*filled)
    near_kernels, far_kernels = kernels[::2], kernels[1::2]

    cand_marg, scale_ub, far_column = call(
        first_body,
        [image_type, rounded_type, (block, BF16)],
        *far_kernels, *sums, *near, *far, weight, flops=2 * pass_flops,
    )
    (tgt_marg,) = call(target_body, [(block, F32)], *near, *far, flops=pass_flops)
    scale_u = None
    for step in range(ITERS):
        if step:
            scale_u, scale_ub, far_column = call(
                step_body,
                [image_type, rounded_type, (block, BF16)],
                *far_kernels, far_vb, image, cand_marg, flops=4 * pass_flops,
            )
        got = exchange(far_column, 1)
        (column,) = call(
            column_body, [(block, F32)], scale_ub, *near_kernels, flops=2 * pass_flops
        )
        column = column + got.astype(F32)
        sent = column.astype(BF16)
        both = [(block, F32), (block, BF16)]
        for low in range(1, top, 2):
            bits = [1 << bit for bit in range(low, min(low + 2, top))]
            flips = bits + [sum(bits)] if len(bits) > 1 else bits
            found = [exchange(sent, flip) for flip in flips]
            if low + 2 < top:
                column, sent = call(functools.partial(sum_body, flips=flips), both, column, *found)
        scale_v, scale_vb = call(
            functools.partial(scale_body, flips=flips), both, column, tgt_marg, *found
        )
        far_vb = exchange(scale_vb, 1)
        (image,) = call(image_body, [image_type], *near_kernels, scale_vb, flops=2 * pass_flops)
    space = pl.BlockSpec(memory_space=pltpu.VMEM)
    last = [*far_kernels, far_vb, image, scale_u]
    mass = pl.pallas_call(
        functools.partial(last_body, candidates=float(cand_rows * devices)),
        out_shape=jax.ShapeDtypeStruct(*image_type),
        in_specs=[space] * len(last),
        out_specs=space,
        compiler_params=pltpu.CompilerParams(vmem_limit_bytes=12 * 1024 * 1024),
    )(*[pltpu.with_memory_space_constraint(a, pltpu.VMEM) for a in last])
    return (ENTROPY_TEMP * jnp.log(scale_u), scale_v[0], mass)


def solution(mesh):
    return jax.shard_map(
        shards,
        mesh=mesh,
        in_specs=(
            P(("grp", "row"), None),
            P(("grp", "row")),
            P(("grp", "row"), None),
            P(("grp", "row")),
        ),
        out_specs=(P(None, ("grp", "row")), P(None, ("grp", "row")), P(None, ("grp", "row"))),
        check_vma=False,
    )
```

```python
import functools
import math

import jax
import jax.numpy as jnp
from jax import lax
from jax.experimental import pallas as pl
from jax.experimental.pallas import tpu as pltpu
from jax.sharding import PartitionSpec as P

CLASSES = 32
ITERS = 3
INVERSE_TEMP = 20.0
ENTROPY_TEMP = 0.05
LANES = 128
EXTRA = 16
TILE = 256
F32 = jnp.float32
BF16 = jnp.bfloat16


def exchange(block, flip):
    devices = lax.axis_size("row")
    return lax.ppermute(block, "row", [(d, d ^ flip) for d in range(devices)])


def call(body, outs, *args, flops=0):
    space = pl.BlockSpec(memory_space=pltpu.VMEM)
    moved = sum(a.size * a.dtype.itemsize for a in args)
    return pl.pallas_call(
        body,
        out_shape=[pltpu.VMEM(shape, dtype) for shape, dtype in outs],
        in_specs=[space] * len(args),
        out_specs=[space] * len(outs),
        compiler_params=pltpu.CompilerParams(vmem_limit_bytes=12 * 1024 * 1024),
        cost_estimate=pl.CostEstimate(flops=flops, bytes_accessed=moved, transcendentals=0),
    )(*[pltpu.with_memory_space_constraint(a, pltpu.VMEM) for a in args])


def unit_rows(values):
    widened = values.astype(F32)
    meansq = jnp.mean(widened * widened, axis=1, keepdims=True)
    return (widened * lax.rsqrt(meansq + 1e-06) / math.sqrt(values.shape[1])).astype(BF16)


def hot(labels, classes=CLASSES):
    rows = lax.broadcasted_iota(jnp.int32, (classes, labels.shape[1]), 0)
    return (labels == rows).astype(F32)


def pack_body(embed_hbm, tgt_hbm, cand_hbm, out_ref, tgt_ref, cand_ref, sems):
    rows = embed_hbm.shape[0]
    copies = [
        pltpu.make_async_copy(cand_hbm, cand_ref, sems.at[0]),
        pltpu.make_async_copy(tgt_hbm, tgt_ref, sems.at[1]),
        pltpu.make_async_copy(embed_hbm, out_ref.at[pl.ds(0, rows)], sems.at[2]),
    ]
    for copy in copies:
        copy.start()
    copies[0].wait()
    counts = lax.dot_general(
        jnp.ones((EXTRA, cand_ref.shape[1]), BF16),
        hot(cand_ref[...], LANES).astype(BF16),
        (((1,), (1,)), ((), ())),
        preferred_element_type=F32,
    )
    high = counts.astype(BF16).astype(F32)
    even = lax.broadcasted_iota(jnp.int32, (EXTRA, LANES), 0) % 2 == 0
    out_ref[rows:, LANES:] = jnp.where(even, high, counts - high).astype(BF16)
    copies[1].wait()
    out_ref[rows:, :LANES] = jnp.broadcast_to(
        tgt_ref[...].astype(F32), (EXTRA, LANES)
    ).astype(BF16)
    copies[2].wait()


def pack(tgt_embed, tgt_labels, cand_labels):
    rows, width = tgt_embed.shape
    anywhere = pl.BlockSpec(memory_space=pl.ANY)
    return pl.pallas_call(
        pack_body,
        out_shape=pltpu.VMEM((rows + EXTRA, width), BF16),
        in_specs=[anywhere] * 3,
        out_specs=pl.BlockSpec(memory_space=pltpu.VMEM),
        scratch_shapes=[
            pltpu.VMEM(tgt_labels.shape, jnp.int32),
            pltpu.VMEM(cand_labels.shape, jnp.int32),
            pltpu.SemaphoreType.DMA((3,)),
        ],
        compiler_params=pltpu.CompilerParams(vmem_limit_bytes=12 * 1024 * 1024),
    )(*[
        pltpu.with_memory_space_constraint(a, pltpu.HBM)
        for a in (tgt_embed, tgt_labels, cand_labels)
    ])


def fill_body(unit_ref, held_ref, kernel_ref, sums_ref, *, tgt_rows):
    rows = tgt_rows + EXTRA
    cand_rows = unit_ref.shape[0]
    per = TILE // tgt_rows
    for col in range(0, kernel_ref.shape[1], TILE):
        first = col // tgt_rows
        block = jnp.concatenate(
            [held_ref[pl.ds((first + s) * rows, tgt_rows), :] for s in range(per)]
        )
        tgt_unit = unit_rows(block)
        for row in range(0, cand_rows, TILE):
            scores = lax.dot_general(
                unit_ref[row : row + TILE, :],
                tgt_unit,
                (((1,), (1,)), ((), ())),
                preferred_element_type=F32,
            )
            tile = jnp.exp(INVERSE_TEMP * scores)
            kernel_ref[row : row + TILE, col : col + TILE] = tile.astype(BF16)
            sums = tile[:, :LANES]
            for lane in range(LANES, TILE, LANES):
                sums += tile[:, lane : lane + LANES]
            if col:
                sums += sums_ref[row : row + TILE, :]
            sums_ref[row : row + TILE, :] = sums


def image_of(kernels, scale_ref):
    image = 0.0
    first = 0
    for kernel_ref in kernels:
        slots = kernel_ref.shape[1] // scale_ref.shape[2]
        scale_v = jnp.concatenate([scale_ref[s] for s in range(first, first + slots)], axis=1)
        image += lax.dot_general(
            kernel_ref[...], scale_v, (((1,), (1,)), ((), ())), preferred_element_type=F32
        )
        first += slots
    return image.T


def put_column(scale_ub, kernels, out_ref):
    width = out_ref.shape[2]
    first = 0
    for kernel_ref in kernels:
        part = jnp.dot(scale_ub, kernel_ref[...], preferred_element_type=F32)
        slots = kernel_ref.shape[1] // width
        for s in range(slots):
            out_ref[first + s] = part[:, s * width : (s + 1) * width].astype(out_ref.dtype)
        first += slots


def extras(refs, tgt_rows):
    rows = tgt_rows + EXTRA
    for ref in refs:
        for s in range(ref.shape[0] // rows):
            yield ref[pl.ds(s * rows + tgt_rows, EXTRA), :].astype(F32)


def target_body(*refs):
    *held_refs, marg_ref = refs
    slots, _, tgt_rows = marg_ref.shape
    total = jnp.zeros((CLASSES, tgt_rows), F32)
    for s, extra in enumerate(extras(held_refs, tgt_rows)):
        weight = 1.0 + 3.0 * hot(extra[:1, :LANES].astype(jnp.int32))
        total += weight
        if s < slots:
            marg_ref[s] = weight
    total = jnp.sum(total, axis=1, keepdims=True)
    for s in range(slots):
        marg_ref[s] = marg_ref[s] / total


def first_body(weight_ref, *refs, parts):
    refs, (marg_ref, scale_ref, column_ref) = refs[:-3], refs[-3:]
    kernels, sums_refs, held_refs = refs[:parts], refs[parts : 3 * parts], refs[3 * parts :]
    counts = jnp.zeros((EXTRA, LANES), F32)
    for extra in extras(held_refs, column_ref.shape[2]):
        counts += extra[:, LANES:]
    count = jnp.broadcast_to(counts[:1] + counts[1:2], (LANES, LANES)).T[:CLASSES, :1]
    candidates = weight_ref.shape[1] * 2 * column_ref.shape[0]
    marg = weight_ref[...] / (candidates + 3.0 * count)
    marg_ref[...] = marg
    sums = sum(ref[...] for ref in sums_refs)
    image = jnp.sum(sums.T, axis=0, keepdims=True)
    scale_ub = (marg / image).astype(BF16)
    scale_ref[...] = scale_ub
    put_column(scale_ub, kernels, column_ref)


def column_body(scale_ref, *refs):
    put_column(scale_ref[...], refs[:-1], refs[-1])


def image_body(scale_ref, *refs):
    refs[-1][...] = image_of(refs[:-1], scale_ref)


def step_body(scale_ref, image_ref, marg_ref, *refs):
    kernels, (out_ref, rounded_ref, column_ref) = refs[:-3], refs[-3:]
    image = image_ref[...] + image_of(kernels, scale_ref)
    scale_u = marg_ref[...] / image
    out_ref[...] = scale_u
    rounded_ref[...] = scale_u.astype(BF16)
    put_column(scale_u.astype(BF16), kernels, column_ref)


def last_body(scale_ref, image_ref, u_ref, scale_v_ref, *refs, candidates):
    kernels, (mass_ref, own_ref) = refs[:-2], refs[-2:]
    own_ref[...] = scale_v_ref[0]
    image = image_ref[...] + image_of(kernels, scale_ref)
    mass_ref[...] = candidates * u_ref[...] * image


def slot_of(slot, flip, slots):
    top = slots.bit_length()
    return slot ^ sum(1 << (top - 1 - bit) for bit in range(1, top) if flip >> bit & 1)


def group_body(got_ref, total_ref, sent_ref, *, members):
    me = lax.axis_index("row") // 2 % members
    slots = total_ref.shape[0]
    for slot in range(slots):
        total = 0.0
        for place in range(members):
            turned = sum(
                ((me // (1 << bit) + place // (1 << bit)) % 2) * (slots >> (bit + 1))
                * (1 - 2 * (slot // (slots >> (bit + 1)) % 2))
                for bit in range(members.bit_length() - 1)
            )
            total += got_ref[place, slot + turned].astype(F32)
        total_ref[slot] = total
        sent_ref[slot] = total.astype(BF16)


def total_of(slot, own_ref, got_refs, flips):
    total = own_ref[slot]
    for flip, got_ref in zip(flips, got_refs):
        total += got_ref[slot_of(slot, flip, own_ref.shape[0])].astype(F32)
    return total


def sum_body(own_ref, *refs, flips):
    *got_refs, total_ref, sent_ref = refs
    for slot in range(own_ref.shape[0]):
        total = total_of(slot, own_ref, got_refs, flips)
        total_ref[slot] = total
        sent_ref[slot] = total.astype(BF16)


def scale_body(own_ref, marg_ref, *refs, flips):
    got_refs, outs = refs[: len(flips)], refs[len(flips) :]
    for slot in range(own_ref.shape[0]):
        scale_v = marg_ref[slot] / total_of(slot, own_ref, got_refs, flips)
        for out_ref in outs:
            out_ref[slot] = scale_v.astype(out_ref.dtype)


def shards(cand_embed, cand_labels, tgt_embed, tgt_labels):
    devices = lax.axis_size("row")
    top = devices.bit_length() - 1
    slots = devices // 2
    cand_rows, width = cand_embed.shape
    tgt_rows = tgt_embed.shape[0]
    cand_labels = cand_labels.reshape(1, cand_rows)
    block = (slots, CLASSES, tgt_rows)
    image_type = ((CLASSES, cand_rows), F32)
    rounded_type = ((CLASSES, cand_rows), BF16)
    half_flops = 2 * cand_rows * slots * tgt_rows * 128

    def fill(held):
        columns = held.shape[0] // (tgt_rows + EXTRA) * tgt_rows
        return call(
            functools.partial(fill_body, tgt_rows=tgt_rows),
            [((cand_rows, columns), BF16), ((cand_rows, LANES), F32)],
            cand_unit, held, flops=4 * 2 * cand_rows * columns * 128,
        )

    held = piece = pack(tgt_embed, tgt_labels.reshape(1, tgt_rows), cand_labels)
    cand_unit = unit_rows(cand_embed)
    weight = 1.0 + 3.0 * hot(cand_labels)
    across = []
    for bit in range(top - 1, 1, -1):
        turned = exchange(held, 1 << bit)
        across.append(exchange(piece, 2))
        piece, across, cand_unit, weight = lax.optimization_barrier(
            (turned, across, cand_unit, weight)
        )
        held = jnp.concatenate([held, piece])
    later = exchange(piece, 2)
    near = [held, jnp.concatenate(across)]
    far = [exchange(part, 1) for part in near]
    filled = [[fill(part) for part in side] for side in (near, far)]
    later, filled = lax.optimization_barrier((later, filled))
    near.append(later)
    far.append(exchange(later, 1))
    for side, parts in zip((near, far), filled):
        parts.append(fill(side[-1]))
    near_kernels, near_sums = zip(*filled[0])
    far_kernels, far_sums = zip(*filled[1])

    cand_marg, scale_ub, far_column = call(
        functools.partial(first_body, parts=len(near)),
        [image_type, rounded_type, (block, BF16)],
        weight, *far_kernels, *near_sums, *far_sums, *near, *far, flops=half_flops,
    )
    (tgt_marg,) = call(target_body, [(block, F32)], *near, *far, flops=half_flops)
    for step in range(ITERS):
        if step:
            scale_u, scale_ub, far_column = call(
                step_body,
                [image_type, rounded_type, (block, BF16)],
                far_vb, image, cand_marg, *far_kernels, flops=2 * half_flops,
            )
        got = exchange(far_column, 1)
        (column,) = call(
            column_body, [(block, F32)], scale_ub, *near_kernels, flops=half_flops
        )
        sent = (column + got.astype(F32)).astype(BF16)
        groups = [
            [base + core + 2 * place for place in range(4)]
            for base in range(0, devices, 8) for core in range(2)
        ]
        got = lax.all_to_all(
            jnp.broadcast_to(sent[None], (4,) + sent.shape), "row", 0, 0,
            axis_index_groups=groups,
        )
        both = [(block, F32), (block, BF16)]
        column, sent = call(functools.partial(group_body, members=4), both, got)
        for low in range(3, top, 2):
            bits = [1 << bit for bit in range(low, min(low + 2, top))]
            flips = bits + [sum(bits)] if len(bits) > 1 else bits
            found = [exchange(sent, flip) for flip in flips]
            if low + 2 < top:
                column, sent = call(functools.partial(sum_body, flips=flips), both, column, *found)
        last = step == ITERS - 1
        scale_vb, *scale_v = call(
            functools.partial(scale_body, flips=flips),
            [(block, BF16)] + [(block, F32)] * last,
            column, tgt_marg, *found,
        )
        far_vb = exchange(scale_vb, 1)
        (image,) = call(image_body, [image_type], scale_vb, *near_kernels, flops=half_flops)
    space = pl.BlockSpec(memory_space=pltpu.VMEM)
    args = [far_vb, image, scale_u, *scale_v, *far_kernels]
    mass, tgt_scaling = pl.pallas_call(
        functools.partial(last_body, candidates=float(cand_rows * devices)),
        out_shape=[
            jax.ShapeDtypeStruct(*image_type), jax.ShapeDtypeStruct((CLASSES, tgt_rows), F32)
        ],
        in_specs=[space] * len(args),
        out_specs=[space] * 2,
        compiler_params=pltpu.CompilerParams(vmem_limit_bytes=12 * 1024 * 1024),
    )(*[pltpu.with_memory_space_constraint(a, pltpu.VMEM) for a in args])
    return (ENTROPY_TEMP * jnp.log(scale_u), tgt_scaling, mass)


def solution(mesh):
    return jax.shard_map(
        shards,
        mesh=mesh,
        in_specs=(
            P(("grp", "row"), None),
            P(("grp", "row")),
            P(("grp", "row"), None),
            P(("grp", "row")),
        ),
        out_specs=(P(None, ("grp", "row")), P(None, ("grp", "row")), P(None, ("grp", "row"))),
        check_vma=False,
    )
```

```python
import functools
import itertools
import math

import jax
import jax.numpy as jnp
from jax import lax
from jax.experimental import pallas as pl
from jax.experimental.pallas import tpu as pltpu
from jax.sharding import PartitionSpec as P

CLASSES = 32
ITERS = 3
INVERSE_TEMP = 20.0
ENTROPY_TEMP = 0.05
LANES = 128
EXTRA = 16
TILE = 256
F32 = jnp.float32
BF16 = jnp.bfloat16


def slot_bits(core, top):
    layer = list(range(2, top))
    return (layer if core else layer[::-1]) + [1]


def rounds(core, top):
    groups = [list(range(low, min(low + 2, top))) for low in range(1, top, 2)]
    return groups[::-1] if core else groups


def flips_of(bits):
    flips = [0]
    for bit in bits:
        flips += [flip | 1 << bit for flip in flips]
    return flips[1:]


def exchange(block, *flips):
    devices = lax.axis_size("row")
    pairs = [(d, d ^ flips[d % len(flips)]) for d in range(devices) if flips[d % len(flips)]]
    return lax.ppermute(block, "row", pairs)


def call(body, outs, *args, flops=0):
    space = pl.BlockSpec(memory_space=pltpu.VMEM)
    moved = sum(a.size * a.dtype.itemsize for a in args)
    return pl.pallas_call(
        body,
        out_shape=[pltpu.VMEM(shape, dtype) for shape, dtype in outs],
        in_specs=[space] * len(args),
        out_specs=[space] * len(outs),
        compiler_params=pltpu.CompilerParams(vmem_limit_bytes=12 * 1024 * 1024),
        cost_estimate=pl.CostEstimate(flops=flops, bytes_accessed=moved, transcendentals=0),
    )(*[pltpu.with_memory_space_constraint(a, pltpu.VMEM) for a in args])


def unit_rows(values):
    widened = values.astype(F32)
    meansq = jnp.mean(widened * widened, axis=1, keepdims=True)
    return (widened * lax.rsqrt(meansq + 1e-06) / math.sqrt(values.shape[1])).astype(BF16)


def hot(labels, classes=CLASSES):
    rows = lax.broadcasted_iota(jnp.int32, (classes, labels.shape[1]), 0)
    return (labels == rows).astype(F32)


def pack_body(embed_hbm, tgt_hbm, cand_hbm, out_ref, tgt_ref, cand_ref, sems):
    rows = embed_hbm.shape[0]
    copies = [
        pltpu.make_async_copy(cand_hbm, cand_ref, sems.at[0]),
        pltpu.make_async_copy(tgt_hbm, tgt_ref, sems.at[1]),
        pltpu.make_async_copy(embed_hbm, out_ref.at[pl.ds(0, rows)], sems.at[2]),
    ]
    for copy in copies:
        copy.start()
    copies[0].wait()
    counts = lax.dot_general(
        jnp.ones((EXTRA, cand_ref.shape[1]), BF16),
        hot(cand_ref[...], LANES).astype(BF16),
        (((1,), (1,)), ((), ())),
        preferred_element_type=F32,
    )
    high = counts.astype(BF16).astype(F32)
    even = lax.broadcasted_iota(jnp.int32, (EXTRA, LANES), 0) % 2 == 0
    out_ref[rows:, LANES:] = jnp.where(even, high, counts - high).astype(BF16)
    copies[1].wait()
    out_ref[rows:, :LANES] = jnp.broadcast_to(
        tgt_ref[...].astype(F32), (EXTRA, LANES)
    ).astype(BF16)
    copies[2].wait()


def pack(tgt_embed, tgt_labels, cand_labels):
    rows, width = tgt_embed.shape
    anywhere = pl.BlockSpec(memory_space=pl.ANY)
    return pl.pallas_call(
        pack_body,
        out_shape=pltpu.VMEM((rows + EXTRA, width), BF16),
        in_specs=[anywhere] * 3,
        out_specs=pl.BlockSpec(memory_space=pltpu.VMEM),
        scratch_shapes=[
            pltpu.VMEM(tgt_labels.shape, jnp.int32),
            pltpu.VMEM(cand_labels.shape, jnp.int32),
            pltpu.SemaphoreType.DMA((3,)),
        ],
        compiler_params=pltpu.CompilerParams(vmem_limit_bytes=12 * 1024 * 1024),
    )(*[
        pltpu.with_memory_space_constraint(a, pltpu.HBM)
        for a in (tgt_embed, tgt_labels, cand_labels)
    ])


def fill_body(unit_ref, held_ref, kernel_ref, sums_ref, *, tgt_rows):
    rows = tgt_rows + EXTRA
    cand_rows = unit_ref.shape[0]
    per = TILE // tgt_rows
    for col in range(0, kernel_ref.shape[1], TILE):
        first = col // tgt_rows
        block = jnp.concatenate(
            [held_ref[pl.ds((first + s) * rows, tgt_rows), :] for s in range(per)]
        )
        tgt_unit = unit_rows(block)
        for row in range(0, cand_rows, TILE):
            scores = lax.dot_general(
                unit_ref[row : row + TILE, :],
                tgt_unit,
                (((1,), (1,)), ((), ())),
                preferred_element_type=F32,
            )
            tile = jnp.exp(INVERSE_TEMP * scores)
            kernel_ref[row : row + TILE, col : col + TILE] = tile.astype(BF16)
            sums = tile[:, :LANES]
            for lane in range(LANES, TILE, LANES):
                sums += tile[:, lane : lane + LANES]
            if col:
                sums += sums_ref[row : row + TILE, :]
            sums_ref[row : row + TILE, :] = sums


def image_of(kernels, scale_ref):
    image = 0.0
    first = 0
    for kernel_ref in kernels:
        slots = kernel_ref.shape[1] // scale_ref.shape[2]
        scale_v = jnp.concatenate([scale_ref[s] for s in range(first, first + slots)], axis=1)
        image += lax.dot_general(
            kernel_ref[...], scale_v, (((1,), (1,)), ((), ())), preferred_element_type=F32
        )
        first += slots
    return image.T


def put_column(scale_ub, kernels, out_ref):
    width = out_ref.shape[2]
    first = 0
    for kernel_ref in kernels:
        part = jnp.dot(scale_ub, kernel_ref[...], preferred_element_type=F32)
        slots = kernel_ref.shape[1] // width
        for s in range(slots):
            out_ref[first + s] = part[:, s * width : (s + 1) * width].astype(out_ref.dtype)
        first += slots


def extras(refs, tgt_rows):
    rows = tgt_rows + EXTRA
    for ref in refs:
        for s in range(ref.shape[0] // rows):
            yield ref[pl.ds(s * rows + tgt_rows, EXTRA), :].astype(F32)


def target_body(*refs):
    *held_refs, marg_ref = refs
    slots, _, tgt_rows = marg_ref.shape
    total = jnp.zeros((CLASSES, tgt_rows), F32)
    for s, extra in enumerate(extras(held_refs, tgt_rows)):
        weight = 1.0 + 3.0 * hot(extra[:1, :LANES].astype(jnp.int32))
        total += weight
        if s < slots:
            marg_ref[s] = weight
    total = jnp.sum(total, axis=1, keepdims=True)
    for s in range(slots):
        marg_ref[s] = marg_ref[s] / total


def first_body(weight_ref, *refs, parts):
    refs, (marg_ref, scale_ref, column_ref) = refs[:-3], refs[-3:]
    kernels, sums_refs, held_refs = refs[:parts], refs[parts : 3 * parts], refs[3 * parts :]
    counts = jnp.zeros((EXTRA, LANES), F32)
    for extra in extras(held_refs, column_ref.shape[2]):
        counts += extra[:, LANES:]
    count = jnp.broadcast_to(counts[:1] + counts[1:2], (LANES, LANES)).T[:CLASSES, :1]
    candidates = weight_ref.shape[1] * 2 * column_ref.shape[0]
    marg = weight_ref[...] / (candidates + 3.0 * count)
    marg_ref[...] = marg
    sums = sum(ref[...] for ref in sums_refs)
    image = jnp.sum(sums.T, axis=0, keepdims=True)
    scale_ub = (marg / image).astype(BF16)
    scale_ref[...] = scale_ub
    put_column(scale_ub, kernels, column_ref)


def column_body(scale_ref, *refs):
    put_column(scale_ref[...], refs[:-1], refs[-1])


def image_body(scale_ref, *refs):
    refs[-1][...] = image_of(refs[:-1], scale_ref)


def step_body(scale_ref, image_ref, marg_ref, *refs):
    kernels, (out_ref, rounded_ref, column_ref) = refs[:-3], refs[-3:]
    image = image_ref[...] + image_of(kernels, scale_ref)
    scale_u = marg_ref[...] / image
    out_ref[...] = scale_u
    rounded_ref[...] = scale_u.astype(BF16)
    put_column(scale_u.astype(BF16), kernels, column_ref)


def last_body(scale_ref, image_ref, u_ref, scale_v_ref, *refs, candidates):
    kernels, (mass_ref, own_ref) = refs[:-2], refs[-2:]
    own_ref[...] = scale_v_ref[0]
    image = image_ref[...] + image_of(kernels, scale_ref)
    mass_ref[...] = candidates * u_ref[...] * image


def slot_of(slot, flips, slots):
    top = slots.bit_length()
    found = []
    for core, flip in enumerate(flips):
        turned = sum(1 << i for i, bit in enumerate(slot_bits(core, top)) if flip >> bit & 1)
        found.append(slot ^ turned)
    if found[0] == found[1]:
        return found[0]
    return found[0] + lax.axis_index("row") % 2 * (found[1] - found[0])


def total_of(slot, own_ref, got_refs, flips):
    total = own_ref[slot]
    for pair, got_ref in zip(flips, got_refs):
        total += got_ref[slot_of(slot, pair, own_ref.shape[0])].astype(F32)
    return total


def sum_body(own_ref, *refs, flips):
    *got_refs, total_ref, sent_ref = refs
    for slot in range(own_ref.shape[0]):
        total = total_of(slot, own_ref, got_refs, flips)
        total_ref[slot] = total
        sent_ref[slot] = total.astype(BF16)


def scale_body(own_ref, marg_ref, *refs, flips):
    got_refs, outs = refs[: len(flips)], refs[len(flips) :]
    for slot in range(own_ref.shape[0]):
        scale_v = marg_ref[slot] / total_of(slot, own_ref, got_refs, flips)
        for out_ref in outs:
            out_ref[slot] = scale_v.astype(out_ref.dtype)


def shards(cand_embed, cand_labels, tgt_embed, tgt_labels):
    devices = lax.axis_size("row")
    top = devices.bit_length() - 1
    slots = devices // 2
    cand_rows, width = cand_embed.shape
    tgt_rows = tgt_embed.shape[0]
    cand_labels = cand_labels.reshape(1, cand_rows)
    block = (slots, CLASSES, tgt_rows)
    image_type = ((CLASSES, cand_rows), F32)
    rounded_type = ((CLASSES, cand_rows), BF16)
    half_flops = 2 * cand_rows * slots * tgt_rows * 128

    def fill(held):
        columns = held.shape[0] // (tgt_rows + EXTRA) * tgt_rows
        return call(
            functools.partial(fill_body, tgt_rows=tgt_rows),
            [((cand_rows, columns), BF16), ((cand_rows, LANES), F32)],
            cand_unit, held, flops=4 * 2 * cand_rows * columns * 128,
        )

    held = piece = pack(tgt_embed, tgt_labels.reshape(1, tgt_rows), cand_labels)
    cand_unit = unit_rows(cand_embed)
    weight = 1.0 + 3.0 * hot(cand_labels)
    across = []
    for bits in list(zip(slot_bits(0, top), slot_bits(1, top)))[:-1]:
        turned = exchange(held, *[1 << bit for bit in bits])
        across.append(exchange(piece, 2))
        piece, across, cand_unit, weight = lax.optimization_barrier(
            (turned, across, cand_unit, weight)
        )
        held = jnp.concatenate([held, piece])
    later = exchange(piece, 2)
    near = [held, jnp.concatenate(across)]
    far = [exchange(part, 1) for part in near]
    filled = [[fill(part) for part in side] for side in (near, far)]
    later, filled = lax.optimization_barrier((later, filled))
    near.append(later)
    far.append(exchange(later, 1))
    for side, parts in zip((near, far), filled):
        parts.append(fill(side[-1]))
    near_kernels, near_sums = zip(*filled[0])
    far_kernels, far_sums = zip(*filled[1])

    cand_marg, scale_ub, far_column = call(
        functools.partial(first_body, parts=len(near)),
        [image_type, rounded_type, (block, BF16)],
        weight, *far_kernels, *near_sums, *far_sums, *near, *far, flops=half_flops,
    )
    (tgt_marg,) = call(target_body, [(block, F32)], *near, *far, flops=half_flops)
    for step in range(ITERS):
        if step:
            scale_u, scale_ub, far_column = call(
                step_body,
                [image_type, rounded_type, (block, BF16)],
                far_vb, image, cand_marg, *far_kernels, flops=2 * half_flops,
            )
        got = exchange(far_column, 1)
        (column,) = call(
            column_body, [(block, F32)], scale_ub, *near_kernels, flops=half_flops
        )
        column = column + got.astype(F32)
        sent = column.astype(BF16)
        order = list(zip(rounds(0, top), rounds(1, top)))
        for place, pair in enumerate(order):
            flips = list(itertools.zip_longest(*[flips_of(bits) for bits in pair], fillvalue=0))
            found = [exchange(sent, *turn) for turn in flips]
            if place < len(order) - 1:
                column, sent = call(
                    functools.partial(sum_body, flips=flips),
                    [(block, F32), (block, BF16)], column, *found,
                )
        last = step == ITERS - 1
        if last:
            potential = ENTROPY_TEMP * jnp.log(scale_u)
            found, potential = lax.optimization_barrier((found, potential))
        scale_vb, *scale_v = call(
            functools.partial(scale_body, flips=flips),
            [(block, BF16)] + [(block, F32)] * last,
            column, tgt_marg, *found,
        )
        far_vb = exchange(scale_vb, 1)
        (image,) = call(image_body, [image_type], scale_vb, *near_kernels, flops=half_flops)
    space = pl.BlockSpec(memory_space=pltpu.VMEM)
    args = [far_vb, image, scale_u, *scale_v, *far_kernels]
    mass, tgt_scaling = pl.pallas_call(
        functools.partial(last_body, candidates=float(cand_rows * devices)),
        out_shape=[
            jax.ShapeDtypeStruct(*image_type), jax.ShapeDtypeStruct((CLASSES, tgt_rows), F32)
        ],
        in_specs=[space] * len(args),
        out_specs=[space] * 2,
        compiler_params=pltpu.CompilerParams(vmem_limit_bytes=12 * 1024 * 1024),
    )(*[pltpu.with_memory_space_constraint(a, pltpu.VMEM) for a in args])
    return (potential, tgt_scaling, mass)


def solution(mesh):
    return jax.shard_map(
        shards,
        mesh=mesh,
        in_specs=(
            P(("grp", "row"), None),
            P(("grp", "row")),
            P(("grp", "row"), None),
            P(("grp", "row")),
        ),
        out_specs=(P(None, ("grp", "row")), P(None, ("grp", "row")), P(None, ("grp", "row"))),
        check_vma=False,
    )
```

```python
import functools
import math

import jax
import jax.numpy as jnp
from jax import lax
from jax.experimental import pallas as pl
from jax.experimental.pallas import tpu as pltpu
from jax.sharding import PartitionSpec as P

CLASSES = 32
ITERS = 3
INVERSE_TEMP = 20.0
ENTROPY_TEMP = 0.05
LANES = 128
EXTRA = 16
TILE = 256
F32 = jnp.float32
BF16 = jnp.bfloat16


def slot_bits(core, top):
    layer = list(range(2, top))
    return (layer if core else layer[::-1]) + [1]


def rounds(core, top):
    bits = list(range(1, top))
    bits = bits[core:] + bits[:core]
    return [bits[low : low + 2] for low in range(0, len(bits), 2)]


def flips_of(bits):
    flips = [0]
    for bit in bits:
        flips += [flip | 1 << bit for flip in flips]
    return flips[1:]


def exchange(block, *flips):
    devices = lax.axis_size("row")
    return lax.ppermute(block, "row", [(d, d ^ flips[d % len(flips)]) for d in range(devices)])


def call(body, outs, *args, flops=0):
    space = pl.BlockSpec(memory_space=pltpu.VMEM)
    moved = sum(a.size * a.dtype.itemsize for a in args)
    return pl.pallas_call(
        body,
        out_shape=[pltpu.VMEM(shape, dtype) for shape, dtype in outs],
        in_specs=[space] * len(args),
        out_specs=[space] * len(outs),
        compiler_params=pltpu.CompilerParams(vmem_limit_bytes=12 * 1024 * 1024),
        cost_estimate=pl.CostEstimate(flops=flops, bytes_accessed=moved, transcendentals=0),
    )(*[pltpu.with_memory_space_constraint(a, pltpu.VMEM) for a in args])


def unit_rows(values):
    widened = values.astype(F32)
    meansq = jnp.mean(widened * widened, axis=1, keepdims=True)
    return (widened * lax.rsqrt(meansq + 1e-06) / math.sqrt(values.shape[1])).astype(BF16)


def hot(labels, classes=CLASSES):
    rows = lax.broadcasted_iota(jnp.int32, (classes, labels.shape[1]), 0)
    return (labels == rows).astype(F32)


def pack_body(embed_hbm, tgt_hbm, cand_hbm, out_ref, tgt_ref, cand_ref, sems):
    rows = embed_hbm.shape[0]
    copies = [
        pltpu.make_async_copy(cand_hbm, cand_ref, sems.at[0]),
        pltpu.make_async_copy(tgt_hbm, tgt_ref, sems.at[1]),
        pltpu.make_async_copy(embed_hbm, out_ref.at[pl.ds(0, rows)], sems.at[2]),
    ]
    for copy in copies:
        copy.start()
    copies[0].wait()
    counts = lax.dot_general(
        jnp.ones((EXTRA, cand_ref.shape[1]), BF16),
        hot(cand_ref[...]).astype(BF16),
        (((1,), (1,)), ((), ())),
        preferred_element_type=F32,
    )
    high = counts.astype(BF16).astype(F32)
    even = lax.broadcasted_iota(jnp.int32, counts.shape, 0) % 2 == 0
    out_ref[rows:, LANES:] = jnp.zeros((EXTRA, LANES), BF16)
    out_ref[rows:, LANES : LANES + CLASSES] = jnp.where(even, high, counts - high).astype(BF16)
    copies[1].wait()
    out_ref[rows:, :LANES] = jnp.broadcast_to(
        tgt_ref[...].astype(F32), (EXTRA, LANES)
    ).astype(BF16)
    copies[2].wait()


def pack(tgt_embed, tgt_labels, cand_labels):
    rows, width = tgt_embed.shape
    anywhere = pl.BlockSpec(memory_space=pl.ANY)
    return pl.pallas_call(
        pack_body,
        out_shape=pltpu.VMEM((rows + EXTRA, width), BF16),
        in_specs=[anywhere] * 3,
        out_specs=pl.BlockSpec(memory_space=pltpu.VMEM),
        scratch_shapes=[
            pltpu.VMEM(tgt_labels.shape, jnp.int32),
            pltpu.VMEM(cand_labels.shape, jnp.int32),
            pltpu.SemaphoreType.DMA((3,)),
        ],
        compiler_params=pltpu.CompilerParams(vmem_limit_bytes=12 * 1024 * 1024),
    )(*[
        pltpu.with_memory_space_constraint(a, pltpu.HBM)
        for a in (tgt_embed, tgt_labels, cand_labels)
    ])


def fill_body(unit_ref, held_ref, kernel_ref, sums_ref, *, tgt_rows):
    rows = tgt_rows + EXTRA
    cand_rows = unit_ref.shape[0]
    per = TILE // tgt_rows
    for col in range(0, kernel_ref.shape[1], TILE):
        first = col // tgt_rows
        block = jnp.concatenate(
            [held_ref[pl.ds((first + s) * rows, tgt_rows), :] for s in range(per)]
        )
        tgt_unit = unit_rows(block)
        for row in range(0, cand_rows, TILE):
            scores = lax.dot_general(
                unit_ref[row : row + TILE, :],
                tgt_unit,
                (((1,), (1,)), ((), ())),
                preferred_element_type=F32,
            )
            tile = jnp.exp(INVERSE_TEMP * scores)
            kernel_ref[row : row + TILE, col : col + TILE] = tile.astype(BF16)
            sums = tile[:, :LANES]
            for lane in range(LANES, TILE, LANES):
                sums += tile[:, lane : lane + LANES]
            if col:
                sums += sums_ref[row : row + TILE, :]
            sums_ref[row : row + TILE, :] = sums


def image_of(kernels, scale_ref):
    image = 0.0
    first = 0
    for kernel_ref in kernels:
        slots = kernel_ref.shape[1] // scale_ref.shape[2]
        scale_v = jnp.concatenate([scale_ref[s] for s in range(first, first + slots)], axis=1)
        image += lax.dot_general(
            kernel_ref[...], scale_v, (((1,), (1,)), ((), ())), preferred_element_type=F32
        )
        first += slots
    return image.T


def put_column(scale_ub, kernels, out_ref):
    width = out_ref.shape[2]
    first = 0
    for kernel_ref in kernels:
        part = jnp.dot(scale_ub, kernel_ref[...], preferred_element_type=F32)
        slots = kernel_ref.shape[1] // width
        for s in range(slots):
            out_ref[first + s] = part[:, s * width : (s + 1) * width].astype(out_ref.dtype)
        first += slots


def extras(refs, tgt_rows):
    rows = tgt_rows + EXTRA
    for ref in refs:
        for s in range(ref.shape[0] // rows):
            yield ref[pl.ds(s * rows + tgt_rows, EXTRA), :].astype(F32)


def target_body(*refs):
    *held_refs, marg_ref = refs
    slots, _, tgt_rows = marg_ref.shape
    total = jnp.zeros((CLASSES, tgt_rows), F32)
    for s, extra in enumerate(extras(held_refs, tgt_rows)):
        weight = 1.0 + 3.0 * hot(extra[:1, :LANES].astype(jnp.int32))
        total += weight
        if s < slots:
            marg_ref[s] = weight
    total = jnp.sum(total, axis=1, keepdims=True)
    for s in range(slots):
        marg_ref[s] = marg_ref[s] / total


def first_body(weight_ref, *refs, parts):
    refs, (marg_ref, scale_ref, column_ref) = refs[:-3], refs[-3:]
    kernels, sums_refs, held_refs = refs[:parts], refs[parts : 3 * parts], refs[3 * parts :]
    counts = jnp.zeros((EXTRA, LANES), F32)
    for extra in extras(held_refs, column_ref.shape[2]):
        counts += extra[:, LANES:]
    count = jnp.broadcast_to(counts[:1] + counts[1:2], (LANES, LANES)).T[:CLASSES, :1]
    candidates = weight_ref.shape[1] * 2 * column_ref.shape[0]
    marg = weight_ref[...] / (candidates + 3.0 * count)
    marg_ref[...] = marg
    sums = sum(ref[...] for ref in sums_refs)
    image = jnp.sum(sums.T, axis=0, keepdims=True)
    scale_ub = (marg / image).astype(BF16)
    scale_ref[...] = scale_ub
    put_column(scale_ub, kernels, column_ref)


def column_body(scale_ref, *refs):
    put_column(scale_ref[...], refs[:-1], refs[-1])


def image_body(scale_ref, *refs):
    refs[-1][...] = image_of(refs[:-1], scale_ref)


def step_body(scale_ref, image_ref, marg_ref, *refs):
    kernels, (out_ref, rounded_ref, column_ref) = refs[:-3], refs[-3:]
    image = image_ref[...] + image_of(kernels, scale_ref)
    scale_u = marg_ref[...] / image
    out_ref[...] = scale_u
    rounded_ref[...] = scale_u.astype(BF16)
    put_column(scale_u.astype(BF16), kernels, column_ref)


def last_body(scale_ref, image_ref, u_ref, scale_v_ref, *refs, candidates):
    kernels, (mass_ref, own_ref) = refs[:-2], refs[-2:]
    own_ref[...] = scale_v_ref[0]
    image = image_ref[...] + image_of(kernels, scale_ref)
    mass_ref[...] = candidates * u_ref[...] * image


def slot_of(slot, flips, slots):
    top = slots.bit_length()
    found = []
    for core, flip in enumerate(flips):
        turned = sum(1 << i for i, bit in enumerate(slot_bits(core, top)) if flip >> bit & 1)
        found.append(slot ^ turned)
    if found[0] == found[1]:
        return found[0]
    return found[0] + lax.axis_index("row") % 2 * (found[1] - found[0])


def total_of(slot, own_ref, got_refs, flips):
    total = own_ref[slot]
    for pair, got_ref in zip(flips, got_refs):
        total += got_ref[slot_of(slot, pair, own_ref.shape[0])].astype(F32)
    return total


def sum_body(own_ref, *refs, flips):
    *got_refs, total_ref, sent_ref = refs
    for slot in range(own_ref.shape[0]):
        total = total_of(slot, own_ref, got_refs, flips)
        total_ref[slot] = total
        sent_ref[slot] = total.astype(BF16)


def scale_body(own_ref, marg_ref, *refs, flips):
    got_refs, outs = refs[: len(flips)], refs[len(flips) :]
    for slot in range(own_ref.shape[0]):
        scale_v = marg_ref[slot] / total_of(slot, own_ref, got_refs, flips)
        for out_ref in outs:
            out_ref[slot] = scale_v.astype(out_ref.dtype)


def shards(cand_embed, cand_labels, tgt_embed, tgt_labels):
    devices = lax.axis_size("row")
    top = devices.bit_length() - 1
    slots = devices // 2
    cand_rows, width = cand_embed.shape
    tgt_rows = tgt_embed.shape[0]
    cand_labels = cand_labels.reshape(1, cand_rows)
    block = (slots, CLASSES, tgt_rows)
    image_type = ((CLASSES, cand_rows), F32)
    rounded_type = ((CLASSES, cand_rows), BF16)
    half_flops = 2 * cand_rows * slots * tgt_rows * 128

    def fill(held):
        columns = held.shape[0] // (tgt_rows + EXTRA) * tgt_rows
        return call(
            functools.partial(fill_body, tgt_rows=tgt_rows),
            [((cand_rows, columns), BF16), ((cand_rows, LANES), F32)],
            cand_unit, held, flops=4 * 2 * cand_rows * columns * 128,
        )

    held = piece = pack(tgt_embed, tgt_labels.reshape(1, tgt_rows), cand_labels)
    cand_unit = unit_rows(cand_embed)
    weight = 1.0 + 3.0 * hot(cand_labels)
    across = []
    for bits in list(zip(slot_bits(0, top), slot_bits(1, top)))[:-1]:
        turned = exchange(held, *[1 << bit for bit in bits])
        across.append(exchange(piece, 2))
        piece, across, cand_unit, weight = lax.optimization_barrier(
            (turned, across, cand_unit, weight)
        )
        held = jnp.concatenate([held, piece])
    later = exchange(piece, 2)
    near = [held, jnp.concatenate(across)]
    far = [exchange(part, 1) for part in near]
    filled = [[fill(part) for part in side] for side in (near, far)]
    later, filled = lax.optimization_barrier((later, filled))
    near.append(later)
    far.append(exchange(later, 1))
    for side, parts in zip((near, far), filled):
        parts.append(fill(side[-1]))
    near_kernels, near_sums = zip(*filled[0])
    far_kernels, far_sums = zip(*filled[1])

    cand_marg, scale_ub, far_column = call(
        functools.partial(first_body, parts=len(near)),
        [image_type, rounded_type, (block, BF16)],
        weight, *far_kernels, *near_sums, *far_sums, *near, *far, flops=half_flops,
    )
    (tgt_marg,) = call(target_body, [(block, F32)], *near, *far, flops=half_flops)
    for step in range(ITERS):
        if step:
            scale_u, scale_ub, far_column = call(
                step_body,
                [image_type, rounded_type, (block, BF16)],
                far_vb, image, cand_marg, *far_kernels, flops=2 * half_flops,
            )
        got = exchange(far_column, 1)
        (column,) = call(
            column_body, [(block, F32)], scale_ub, *near_kernels, flops=half_flops
        )
        column = column + got.astype(F32)
        sent = column.astype(BF16)
        order = list(zip(rounds(0, top), rounds(1, top)))
        for place, pair in enumerate(order):
            flips = list(zip(*[flips_of(bits) for bits in pair]))
            found = [exchange(sent, *turn) for turn in flips]
            if place < len(order) - 1:
                column, sent = call(
                    functools.partial(sum_body, flips=flips),
                    [(block, F32), (block, BF16)], column, *found,
                )
        last = step == ITERS - 1
        if last:
            potential = ENTROPY_TEMP * jnp.log(scale_u)
            found, potential = lax.optimization_barrier((found, potential))
        scale_vb, *scale_v = call(
            functools.partial(scale_body, flips=flips),
            [(block, BF16)] + [(block, F32)] * last,
            column, tgt_marg, *found,
        )
        far_vb = exchange(scale_vb, 1)
        (image,) = call(image_body, [image_type], scale_vb, *near_kernels, flops=half_flops)
    space = pl.BlockSpec(memory_space=pltpu.VMEM)
    args = [far_vb, image, scale_u, *scale_v, *far_kernels]
    mass, tgt_scaling = pl.pallas_call(
        functools.partial(last_body, candidates=float(cand_rows * devices)),
        out_shape=[
            jax.ShapeDtypeStruct(*image_type), jax.ShapeDtypeStruct((CLASSES, tgt_rows), F32)
        ],
        in_specs=[space] * len(args),
        out_specs=[space] * 2,
        compiler_params=pltpu.CompilerParams(vmem_limit_bytes=12 * 1024 * 1024),
    )(*[pltpu.with_memory_space_constraint(a, pltpu.VMEM) for a in args])
    return (potential, tgt_scaling, mass)


def solution(mesh):
    return jax.shard_map(
        shards,
        mesh=mesh,
        in_specs=(
            P(("grp", "row"), None),
            P(("grp", "row")),
            P(("grp", "row"), None),
            P(("grp", "row")),
        ),
        out_specs=(P(None, ("grp", "row")), P(None, ("grp", "row")), P(None, ("grp", "row"))),
        check_vma=False,
    )
```

```python
import functools
import math

import jax
import jax.numpy as jnp
from jax import lax
from jax.experimental import pallas as pl
from jax.experimental.pallas import tpu as pltpu
from jax.sharding import PartitionSpec as P

CLASSES = 32
ITERS = 3
INVERSE_TEMP = 20.0
ENTROPY_TEMP = 0.05
LANES = 128
EXTRA = 16
TILE = 256
F32 = jnp.float32
BF16 = jnp.bfloat16


def slot_bits(core, top):
    layer = list(range(2, top))
    return (layer if core else layer[::-1]) + [1]


def flips_of(bits):
    flips = [0]
    for bit in bits:
        flips += [flip | 1 << bit for flip in flips]
    return flips[1:]


def rounds(top):
    layers = [list(range(low, min(low + 2, top))) for low in range(2, top, 2)]
    order = [flips_of(bits) for bits in [[1]] + layers]
    found = []
    for pair in zip(order, order[1:] + order[:1]):
        longest = max(len(flips) for flips in pair)
        found.append(list(zip(*[flips + [0] * (longest - len(flips)) for flips in pair])))
    return found


def exchange(block, *flips):
    devices = lax.axis_size("row")
    return lax.ppermute(block, "row", [(d, d ^ flips[d % len(flips)]) for d in range(devices)])


def call(body, outs, *args, flops=0):
    space = pl.BlockSpec(memory_space=pltpu.VMEM)
    moved = sum(a.size * a.dtype.itemsize for a in args)
    return pl.pallas_call(
        body,
        out_shape=[pltpu.VMEM(shape, dtype) for shape, dtype in outs],
        in_specs=[space] * len(args),
        out_specs=[space] * len(outs),
        compiler_params=pltpu.CompilerParams(vmem_limit_bytes=12 * 1024 * 1024),
        cost_estimate=pl.CostEstimate(flops=flops, bytes_accessed=moved, transcendentals=0),
    )(*[pltpu.with_memory_space_constraint(a, pltpu.VMEM) for a in args])


def unit_rows(values):
    widened = values.astype(F32)
    meansq = jnp.mean(widened * widened, axis=1, keepdims=True)
    return (widened * lax.rsqrt(meansq + 1e-06) / math.sqrt(values.shape[1])).astype(BF16)


def hot(labels, classes=CLASSES):
    rows = lax.broadcasted_iota(jnp.int32, (classes, labels.shape[1]), 0)
    return (labels == rows).astype(F32)


def pack_body(embed_hbm, tgt_hbm, cand_hbm, out_ref, tgt_ref, cand_ref, sems):
    rows = embed_hbm.shape[0]
    copies = [
        pltpu.make_async_copy(cand_hbm, cand_ref, sems.at[0]),
        pltpu.make_async_copy(tgt_hbm, tgt_ref, sems.at[1]),
        pltpu.make_async_copy(embed_hbm, out_ref.at[pl.ds(0, rows)], sems.at[2]),
    ]
    for copy in copies:
        copy.start()
    copies[0].wait()
    counts = lax.dot_general(
        jnp.ones((EXTRA, cand_ref.shape[1]), BF16),
        hot(cand_ref[...]).astype(BF16),
        (((1,), (1,)), ((), ())),
        preferred_element_type=F32,
    )
    high = counts.astype(BF16).astype(F32)
    even = lax.broadcasted_iota(jnp.int32, counts.shape, 0) % 2 == 0
    out_ref[rows:, LANES:] = jnp.zeros((EXTRA, LANES), BF16)
    out_ref[rows:, LANES : LANES + CLASSES] = jnp.where(even, high, counts - high).astype(BF16)
    copies[1].wait()
    out_ref[rows:, :LANES] = jnp.broadcast_to(
        tgt_ref[...].astype(F32), (EXTRA, LANES)
    ).astype(BF16)
    copies[2].wait()


def pack(tgt_embed, tgt_labels, cand_labels):
    rows, width = tgt_embed.shape
    anywhere = pl.BlockSpec(memory_space=pl.ANY)
    return pl.pallas_call(
        pack_body,
        out_shape=pltpu.VMEM((rows + EXTRA, width), BF16),
        in_specs=[anywhere] * 3,
        out_specs=pl.BlockSpec(memory_space=pltpu.VMEM),
        scratch_shapes=[
            pltpu.VMEM(tgt_labels.shape, jnp.int32),
            pltpu.VMEM(cand_labels.shape, jnp.int32),
            pltpu.SemaphoreType.DMA((3,)),
        ],
        compiler_params=pltpu.CompilerParams(vmem_limit_bytes=12 * 1024 * 1024),
    )(*[
        pltpu.with_memory_space_constraint(a, pltpu.HBM)
        for a in (tgt_embed, tgt_labels, cand_labels)
    ])


def fill_body(unit_ref, held_ref, kernel_ref, sums_ref, *, tgt_rows):
    rows = tgt_rows + EXTRA
    cand_rows = unit_ref.shape[0]
    per = TILE // tgt_rows
    for col in range(0, kernel_ref.shape[1], TILE):
        first = col // tgt_rows
        block = jnp.concatenate(
            [held_ref[pl.ds((first + s) * rows, tgt_rows), :] for s in range(per)]
        )
        tgt_unit = unit_rows(block)
        for row in range(0, cand_rows, TILE):
            scores = lax.dot_general(
                unit_ref[row : row + TILE, :],
                tgt_unit,
                (((1,), (1,)), ((), ())),
                preferred_element_type=F32,
            )
            tile = jnp.exp(INVERSE_TEMP * scores)
            kernel_ref[row : row + TILE, col : col + TILE] = tile.astype(BF16)
            sums = tile[:, :LANES]
            for lane in range(LANES, TILE, LANES):
                sums += tile[:, lane : lane + LANES]
            if col:
                sums += sums_ref[row : row + TILE, :]
            sums_ref[row : row + TILE, :] = sums


def image_of(kernels, scale_ref):
    image = 0.0
    first = 0
    for kernel_ref in kernels:
        slots = kernel_ref.shape[1] // scale_ref.shape[2]
        scale_v = jnp.concatenate([scale_ref[s] for s in range(first, first + slots)], axis=1)
        image += lax.dot_general(
            kernel_ref[...], scale_v, (((1,), (1,)), ((), ())), preferred_element_type=F32
        )
        first += slots
    return image.T


def put_column(scale_ub, kernels, out_ref):
    width = out_ref.shape[2]
    first = 0
    for kernel_ref in kernels:
        part = jnp.dot(scale_ub, kernel_ref[...], preferred_element_type=F32)
        slots = kernel_ref.shape[1] // width
        for s in range(slots):
            out_ref[first + s] = part[:, s * width : (s + 1) * width].astype(out_ref.dtype)
        first += slots


def extras(refs, tgt_rows):
    rows = tgt_rows + EXTRA
    for ref in refs:
        for s in range(ref.shape[0] // rows):
            yield ref[pl.ds(s * rows + tgt_rows, EXTRA), :].astype(F32)


def target_body(*refs):
    *held_refs, marg_ref = refs
    slots, _, tgt_rows = marg_ref.shape
    total = jnp.zeros((CLASSES, tgt_rows), F32)
    for s, extra in enumerate(extras(held_refs, tgt_rows)):
        weight = 1.0 + 3.0 * hot(extra[:1, :LANES].astype(jnp.int32))
        total += weight
        if s < slots:
            marg_ref[s] = weight
    total = jnp.sum(total, axis=1, keepdims=True)
    for s in range(slots):
        marg_ref[s] = marg_ref[s] / total


def first_body(weight_ref, *refs, parts):
    refs, (marg_ref, scale_ref, column_ref) = refs[:-3], refs[-3:]
    kernels, sums_refs, held_refs = refs[:parts], refs[parts : 3 * parts], refs[3 * parts :]
    counts = jnp.zeros((EXTRA, LANES), F32)
    for extra in extras(held_refs, column_ref.shape[2]):
        counts += extra[:, LANES:]
    count = jnp.broadcast_to(counts[:1] + counts[1:2], (LANES, LANES)).T[:CLASSES, :1]
    candidates = weight_ref.shape[1] * 2 * column_ref.shape[0]
    marg = weight_ref[...] / (candidates + 3.0 * count)
    marg_ref[...] = marg
    sums = sum(ref[...] for ref in sums_refs)
    image = jnp.sum(sums.T, axis=0, keepdims=True)
    scale_ub = (marg / image).astype(BF16)
    scale_ref[...] = scale_ub
    put_column(scale_ub, kernels, column_ref)


def column_body(scale_ref, *refs):
    put_column(scale_ref[...], refs[:-1], refs[-1])


def image_body(scale_ref, *refs):
    refs[-1][...] = image_of(refs[:-1], scale_ref)


def step_body(scale_ref, image_ref, marg_ref, *refs):
    kernels, (out_ref, rounded_ref, column_ref) = refs[:-3], refs[-3:]
    image = image_ref[...] + image_of(kernels, scale_ref)
    scale_u = marg_ref[...] / image
    out_ref[...] = scale_u
    rounded_ref[...] = scale_u.astype(BF16)
    put_column(scale_u.astype(BF16), kernels, column_ref)


def last_body(scale_ref, image_ref, u_ref, scale_v_ref, *refs, candidates):
    kernels, (mass_ref, own_ref) = refs[:-2], refs[-2:]
    own_ref[...] = scale_v_ref[0]
    image = image_ref[...] + image_of(kernels, scale_ref)
    mass_ref[...] = candidates * u_ref[...] * image


def slot_of(slot, flips, slots):
    top = slots.bit_length()
    found = []
    for core, flip in enumerate(flips):
        turned = sum(1 << i for i, bit in enumerate(slot_bits(core, top)) if flip >> bit & 1)
        found.append(slot ^ turned)
    if found[0] == found[1]:
        return found[0]
    return found[0] + lax.axis_index("row") % 2 * (found[1] - found[0])


def total_of(slot, own_ref, got_refs, flips):
    total = own_ref[slot]
    for pair, got_ref in zip(flips, got_refs):
        got = got_ref[slot_of(slot, pair, own_ref.shape[0])].astype(F32)
        if not all(pair):
            got = jnp.where(lax.axis_index("row") % 2 == (pair[0] == 0), got, 0.0)
        total += got
    return total


def sum_body(own_ref, *refs, flips):
    *got_refs, total_ref, sent_ref = refs
    for slot in range(own_ref.shape[0]):
        total = total_of(slot, own_ref, got_refs, flips)
        total_ref[slot] = total
        sent_ref[slot] = total.astype(BF16)


def scale_body(own_ref, marg_ref, *refs, flips):
    got_refs, outs = refs[: len(flips)], refs[len(flips) :]
    for slot in range(own_ref.shape[0]):
        scale_v = marg_ref[slot] / total_of(slot, own_ref, got_refs, flips)
        for out_ref in outs:
            out_ref[slot] = scale_v.astype(out_ref.dtype)


def shards(cand_embed, cand_labels, tgt_embed, tgt_labels):
    devices = lax.axis_size("row")
    top = devices.bit_length() - 1
    slots = devices // 2
    cand_rows, width = cand_embed.shape
    tgt_rows = tgt_embed.shape[0]
    cand_labels = cand_labels.reshape(1, cand_rows)
    block = (slots, CLASSES, tgt_rows)
    image_type = ((CLASSES, cand_rows), F32)
    rounded_type = ((CLASSES, cand_rows), BF16)
    half_flops = 2 * cand_rows * slots * tgt_rows * 128

    def fill(held):
        columns = held.shape[0] // (tgt_rows + EXTRA) * tgt_rows
        return call(
            functools.partial(fill_body, tgt_rows=tgt_rows),
            [((cand_rows, columns), BF16), ((cand_rows, LANES), F32)],
            cand_unit, held, flops=4 * 2 * cand_rows * columns * 128,
        )

    held = piece = pack(tgt_embed, tgt_labels.reshape(1, tgt_rows), cand_labels)
    cand_unit = unit_rows(cand_embed)
    weight = 1.0 + 3.0 * hot(cand_labels)
    across = []
    for bits in list(zip(slot_bits(0, top), slot_bits(1, top)))[:-1]:
        turned = exchange(held, *[1 << bit for bit in bits])
        across.append(exchange(piece, 2))
        piece, across, cand_unit, weight = lax.optimization_barrier(
            (turned, across, cand_unit, weight)
        )
        held = jnp.concatenate([held, piece])
    later = exchange(piece, 2)
    near = [held, jnp.concatenate(across)]
    far = [exchange(part, 1) for part in near]
    filled = [[fill(part) for part in side] for side in (near, far)]
    later, filled = lax.optimization_barrier((later, filled))
    near.append(later)
    far.append(exchange(later, 1))
    for side, parts in zip((near, far), filled):
        parts.append(fill(side[-1]))
    near_kernels, near_sums = zip(*filled[0])
    far_kernels, far_sums = zip(*filled[1])

    cand_marg, scale_ub, far_column = call(
        functools.partial(first_body, parts=len(near)),
        [image_type, rounded_type, (block, BF16)],
        weight, *far_kernels, *near_sums, *far_sums, *near, *far, flops=half_flops,
    )
    (tgt_marg,) = call(target_body, [(block, F32)], *near, *far, flops=half_flops)
    for step in range(ITERS):
        if step:
            scale_u, scale_ub, far_column = call(
                step_body,
                [image_type, rounded_type, (block, BF16)],
                far_vb, image, cand_marg, *far_kernels, flops=2 * half_flops,
            )
        got = exchange(far_column, 1)
        (column,) = call(
            column_body, [(block, F32)], scale_ub, *near_kernels, flops=half_flops
        )
        column = column + got.astype(F32)
        sent = column.astype(BF16)
        order = rounds(top)
        for place, flips in enumerate(order):
            found = [exchange(sent, *turn) for turn in flips]
            if place < len(order) - 1:
                column, sent = call(
                    functools.partial(sum_body, flips=flips),
                    [(block, F32), (block, BF16)], column, *found,
                )
        last = step == ITERS - 1
        if last:
            potential = ENTROPY_TEMP * jnp.log(scale_u)
            found, potential = lax.optimization_barrier((found, potential))
        scale_vb, *scale_v = call(
            functools.partial(scale_body, flips=flips),
            [(block, BF16)] + [(block, F32)] * last,
            column, tgt_marg, *found,
        )
        far_vb = exchange(scale_vb, 1)
        (image,) = call(image_body, [image_type], scale_vb, *near_kernels, flops=half_flops)
    space = pl.BlockSpec(memory_space=pltpu.VMEM)
    args = [far_vb, image, scale_u, *scale_v, *far_kernels]
    mass, tgt_scaling = pl.pallas_call(
        functools.partial(last_body, candidates=float(cand_rows * devices)),
        out_shape=[
            jax.ShapeDtypeStruct(*image_type), jax.ShapeDtypeStruct((CLASSES, tgt_rows), F32)
        ],
        in_specs=[space] * len(args),
        out_specs=[space] * 2,
        compiler_params=pltpu.CompilerParams(vmem_limit_bytes=12 * 1024 * 1024),
    )(*[pltpu.with_memory_space_constraint(a, pltpu.VMEM) for a in args])
    return (potential, tgt_scaling, mass)


def solution(mesh):
    return jax.shard_map(
        shards,
        mesh=mesh,
        in_specs=(
            P(("grp", "row"), None),
            P(("grp", "row")),
            P(("grp", "row"), None),
            P(("grp", "row")),
        ),
        out_specs=(P(None, ("grp", "row")), P(None, ("grp", "row")), P(None, ("grp", "row"))),
        check_vma=False,
    )
```

```python
import functools
import math

import jax
import jax.numpy as jnp
from jax import lax
from jax.experimental import pallas as pl
from jax.experimental.pallas import tpu as pltpu
from jax.sharding import PartitionSpec as P

CLASSES = 32
ITERS = 3
INVERSE_TEMP = 20.0
ENTROPY_TEMP = 0.05
LANES = 128
EXTRA = 16
TILE = 256
F32 = jnp.float32
BF16 = jnp.bfloat16


def slot_bits(core, top):
    layer = list(range(2, top))
    return (layer if core else layer[::-1]) + [1]


def rounds(core, top):
    bits = list(range(1, top))
    bits = bits[core:] + bits[:core]
    return [[bit] for bit in bits]


def flips_of(bits):
    flips = [0]
    for bit in bits:
        flips += [flip | 1 << bit for flip in flips]
    return flips[1:]


def exchange(block, *flips):
    devices = lax.axis_size("row")
    return lax.ppermute(block, "row", [(d, d ^ flips[d % len(flips)]) for d in range(devices)])


def call(body, outs, *args, flops=0):
    space = pl.BlockSpec(memory_space=pltpu.VMEM)
    moved = sum(a.size * a.dtype.itemsize for a in args)
    return pl.pallas_call(
        body,
        out_shape=[pltpu.VMEM(shape, dtype) for shape, dtype in outs],
        in_specs=[space] * len(args),
        out_specs=[space] * len(outs),
        compiler_params=pltpu.CompilerParams(vmem_limit_bytes=12 * 1024 * 1024),
        cost_estimate=pl.CostEstimate(flops=flops, bytes_accessed=moved, transcendentals=0),
    )(*[pltpu.with_memory_space_constraint(a, pltpu.VMEM) for a in args])


def unit_rows(values):
    widened = values.astype(F32)
    meansq = jnp.mean(widened * widened, axis=1, keepdims=True)
    return (widened * lax.rsqrt(meansq + 1e-06) / math.sqrt(values.shape[1])).astype(BF16)


def hot(labels, classes=CLASSES):
    rows = lax.broadcasted_iota(jnp.int32, (classes, labels.shape[1]), 0)
    return (labels == rows).astype(F32)


def pack_body(embed_hbm, tgt_hbm, cand_hbm, out_ref, tgt_ref, cand_ref, sems):
    rows = embed_hbm.shape[0]
    copies = [
        pltpu.make_async_copy(cand_hbm, cand_ref, sems.at[0]),
        pltpu.make_async_copy(tgt_hbm, tgt_ref, sems.at[1]),
        pltpu.make_async_copy(embed_hbm, out_ref.at[pl.ds(0, rows)], sems.at[2]),
    ]
    for copy in copies:
        copy.start()
    copies[0].wait()
    counts = lax.dot_general(
        jnp.ones((EXTRA, cand_ref.shape[1]), BF16),
        hot(cand_ref[...]).astype(BF16),
        (((1,), (1,)), ((), ())),
        preferred_element_type=F32,
    )
    high = counts.astype(BF16).astype(F32)
    even = lax.broadcasted_iota(jnp.int32, counts.shape, 0) % 2 == 0
    out_ref[rows:, LANES:] = jnp.zeros((EXTRA, LANES), BF16)
    out_ref[rows:, LANES : LANES + CLASSES] = jnp.where(even, high, counts - high).astype(BF16)
    copies[1].wait()
    out_ref[rows:, :LANES] = jnp.broadcast_to(
        tgt_ref[...].astype(F32), (EXTRA, LANES)
    ).astype(BF16)
    copies[2].wait()


def pack(tgt_embed, tgt_labels, cand_labels):
    rows, width = tgt_embed.shape
    anywhere = pl.BlockSpec(memory_space=pl.ANY)
    return pl.pallas_call(
        pack_body,
        out_shape=pltpu.VMEM((rows + EXTRA, width), BF16),
        in_specs=[anywhere] * 3,
        out_specs=pl.BlockSpec(memory_space=pltpu.VMEM),
        scratch_shapes=[
            pltpu.VMEM(tgt_labels.shape, jnp.int32),
            pltpu.VMEM(cand_labels.shape, jnp.int32),
            pltpu.SemaphoreType.DMA((3,)),
        ],
        compiler_params=pltpu.CompilerParams(vmem_limit_bytes=12 * 1024 * 1024),
    )(*[
        pltpu.with_memory_space_constraint(a, pltpu.HBM)
        for a in (tgt_embed, tgt_labels, cand_labels)
    ])


def fill_body(unit_ref, held_ref, kernel_ref, sums_ref, *, tgt_rows):
    rows = tgt_rows + EXTRA
    cand_rows = unit_ref.shape[0]
    per = TILE // tgt_rows
    for col in range(0, kernel_ref.shape[1], TILE):
        first = col // tgt_rows
        block = jnp.concatenate(
            [held_ref[pl.ds((first + s) * rows, tgt_rows), :] for s in range(per)]
        )
        tgt_unit = unit_rows(block)
        for row in range(0, cand_rows, TILE):
            scores = lax.dot_general(
                unit_ref[row : row + TILE, :],
                tgt_unit,
                (((1,), (1,)), ((), ())),
                preferred_element_type=F32,
            )
            tile = jnp.exp(INVERSE_TEMP * scores)
            kernel_ref[row : row + TILE, col : col + TILE] = tile.astype(BF16)
            sums = tile[:, :LANES]
            for lane in range(LANES, TILE, LANES):
                sums += tile[:, lane : lane + LANES]
            if col:
                sums += sums_ref[row : row + TILE, :]
            sums_ref[row : row + TILE, :] = sums


def image_of(kernels, scale_ref):
    image = 0.0
    first = 0
    for kernel_ref in kernels:
        slots = kernel_ref.shape[1] // scale_ref.shape[2]
        scale_v = jnp.concatenate([scale_ref[s] for s in range(first, first + slots)], axis=1)
        image += lax.dot_general(
            kernel_ref[...], scale_v, (((1,), (1,)), ((), ())), preferred_element_type=F32
        )
        first += slots
    return image.T


def put_column(scale_ub, kernels, out_ref):
    width = out_ref.shape[2]
    first = 0
    for kernel_ref in kernels:
        part = jnp.dot(scale_ub, kernel_ref[...], preferred_element_type=F32)
        slots = kernel_ref.shape[1] // width
        for s in range(slots):
            out_ref[first + s] = part[:, s * width : (s + 1) * width].astype(out_ref.dtype)
        first += slots


def extras(refs, tgt_rows):
    rows = tgt_rows + EXTRA
    for ref in refs:
        for s in range(ref.shape[0] // rows):
            yield ref[pl.ds(s * rows + tgt_rows, EXTRA), :].astype(F32)


def target_body(*refs):
    *held_refs, marg_ref = refs
    slots, _, tgt_rows = marg_ref.shape
    total = jnp.zeros((CLASSES, tgt_rows), F32)
    for s, extra in enumerate(extras(held_refs, tgt_rows)):
        weight = 1.0 + 3.0 * hot(extra[:1, :LANES].astype(jnp.int32))
        total += weight
        if s < slots:
            marg_ref[s] = weight
    total = jnp.sum(total, axis=1, keepdims=True)
    for s in range(slots):
        marg_ref[s] = marg_ref[s] / total


def first_body(weight_ref, *refs, parts):
    refs, (marg_ref, scale_ref, column_ref) = refs[:-3], refs[-3:]
    kernels, sums_refs, held_refs = refs[:parts], refs[parts : 3 * parts], refs[3 * parts :]
    counts = jnp.zeros((EXTRA, LANES), F32)
    for extra in extras(held_refs, column_ref.shape[2]):
        counts += extra[:, LANES:]
    count = jnp.broadcast_to(counts[:1] + counts[1:2], (LANES, LANES)).T[:CLASSES, :1]
    candidates = weight_ref.shape[1] * 2 * column_ref.shape[0]
    marg = weight_ref[...] / (candidates + 3.0 * count)
    marg_ref[...] = marg
    sums = sum(ref[...] for ref in sums_refs)
    image = jnp.sum(sums.T, axis=0, keepdims=True)
    scale_ub = (marg / image).astype(BF16)
    scale_ref[...] = scale_ub
    put_column(scale_ub, kernels, column_ref)


def column_body(scale_ref, *refs):
    put_column(scale_ref[...], refs[:-1], refs[-1])


def image_body(scale_ref, *refs):
    refs[-1][...] = image_of(refs[:-1], scale_ref)


def step_body(scale_ref, image_ref, marg_ref, *refs):
    kernels, (out_ref, rounded_ref, column_ref) = refs[:-3], refs[-3:]
    image = image_ref[...] + image_of(kernels, scale_ref)
    scale_u = marg_ref[...] / image
    out_ref[...] = scale_u
    rounded_ref[...] = scale_u.astype(BF16)
    put_column(scale_u.astype(BF16), kernels, column_ref)


def last_body(scale_ref, image_ref, u_ref, scale_v_ref, *refs, candidates):
    kernels, (mass_ref, own_ref) = refs[:-2], refs[-2:]
    own_ref[...] = scale_v_ref[0]
    image = image_ref[...] + image_of(kernels, scale_ref)
    mass_ref[...] = candidates * u_ref[...] * image


def slot_of(slot, flips, slots):
    top = slots.bit_length()
    found = []
    for core, flip in enumerate(flips):
        turned = sum(1 << i for i, bit in enumerate(slot_bits(core, top)) if flip >> bit & 1)
        found.append(slot ^ turned)
    if found[0] == found[1]:
        return found[0]
    return found[0] + lax.axis_index("row") % 2 * (found[1] - found[0])


def total_of(slot, own_ref, got_refs, flips):
    total = own_ref[slot]
    for pair, got_ref in zip(flips, got_refs):
        total += got_ref[slot_of(slot, pair, own_ref.shape[0])].astype(F32)
    return total


def sum_body(own_ref, *refs, flips):
    *got_refs, total_ref, sent_ref = refs
    for slot in range(own_ref.shape[0]):
        total = total_of(slot, own_ref, got_refs, flips)
        total_ref[slot] = total
        sent_ref[slot] = total.astype(BF16)


def scale_body(own_ref, marg_ref, *refs, flips):
    got_refs, outs = refs[: len(flips)], refs[len(flips) :]
    for slot in range(own_ref.shape[0]):
        scale_v = marg_ref[slot] / total_of(slot, own_ref, got_refs, flips)
        for out_ref in outs:
            out_ref[slot] = scale_v.astype(out_ref.dtype)


def shards(cand_embed, cand_labels, tgt_embed, tgt_labels):
    devices = lax.axis_size("row")
    top = devices.bit_length() - 1
    slots = devices // 2
    cand_rows, width = cand_embed.shape
    tgt_rows = tgt_embed.shape[0]
    cand_labels = cand_labels.reshape(1, cand_rows)
    block = (slots, CLASSES, tgt_rows)
    image_type = ((CLASSES, cand_rows), F32)
    rounded_type = ((CLASSES, cand_rows), BF16)
    half_flops = 2 * cand_rows * slots * tgt_rows * 128

    def fill(held):
        columns = held.shape[0] // (tgt_rows + EXTRA) * tgt_rows
        return call(
            functools.partial(fill_body, tgt_rows=tgt_rows),
            [((cand_rows, columns), BF16), ((cand_rows, LANES), F32)],
            cand_unit, held, flops=4 * 2 * cand_rows * columns * 128,
        )

    held = piece = pack(tgt_embed, tgt_labels.reshape(1, tgt_rows), cand_labels)
    cand_unit = unit_rows(cand_embed)
    weight = 1.0 + 3.0 * hot(cand_labels)
    across = []
    for bits in list(zip(slot_bits(0, top), slot_bits(1, top)))[:-1]:
        turned = exchange(held, *[1 << bit for bit in bits])
        across.append(exchange(piece, 2))
        piece, across, cand_unit, weight = lax.optimization_barrier(
            (turned, across, cand_unit, weight)
        )
        held = jnp.concatenate([held, piece])
    later = exchange(piece, 2)
    near = [held, jnp.concatenate(across)]
    far = [exchange(part, 1) for part in near]
    filled = [[fill(part) for part in side] for side in (near, far)]
    later, filled = lax.optimization_barrier((later, filled))
    near.append(later)
    far.append(exchange(later, 1))
    for side, parts in zip((near, far), filled):
        parts.append(fill(side[-1]))
    near_kernels, near_sums = zip(*filled[0])
    far_kernels, far_sums = zip(*filled[1])

    cand_marg, scale_ub, far_column = call(
        functools.partial(first_body, parts=len(near)),
        [image_type, rounded_type, (block, BF16)],
        weight, *far_kernels, *near_sums, *far_sums, *near, *far, flops=half_flops,
    )
    (tgt_marg,) = call(target_body, [(block, F32)], *near, *far, flops=half_flops)
    for step in range(ITERS):
        if step:
            scale_u, scale_ub, far_column = call(
                step_body,
                [image_type, rounded_type, (block, BF16)],
                far_vb, image, cand_marg, *far_kernels, flops=2 * half_flops,
            )
        got = exchange(far_column, 1)
        (column,) = call(
            column_body, [(block, F32)], scale_ub, *near_kernels, flops=half_flops
        )
        column = column + got.astype(F32)
        sent = column.astype(BF16)
        order = list(zip(rounds(0, top), rounds(1, top)))
        for place, pair in enumerate(order):
            flips = list(zip(*[flips_of(bits) for bits in pair]))
            found = [exchange(sent, *turn) for turn in flips]
            if place < len(order) - 1:
                column, sent = call(
                    functools.partial(sum_body, flips=flips),
                    [(block, F32), (block, BF16)], column, *found,
                )
        last = step == ITERS - 1
        if last:
            potential = ENTROPY_TEMP * jnp.log(scale_u)
            found, potential = lax.optimization_barrier((found, potential))
        scale_vb, *scale_v = call(
            functools.partial(scale_body, flips=flips),
            [(block, BF16)] + [(block, F32)] * last,
            column, tgt_marg, *found,
        )
        far_vb = exchange(scale_vb, 1)
        (image,) = call(image_body, [image_type], scale_vb, *near_kernels, flops=half_flops)
    space = pl.BlockSpec(memory_space=pltpu.VMEM)
    args = [far_vb, image, scale_u, *scale_v, *far_kernels]
    mass, tgt_scaling = pl.pallas_call(
        functools.partial(last_body, candidates=float(cand_rows * devices)),
        out_shape=[
            jax.ShapeDtypeStruct(*image_type), jax.ShapeDtypeStruct((CLASSES, tgt_rows), F32)
        ],
        in_specs=[space] * len(args),
        out_specs=[space] * 2,
        compiler_params=pltpu.CompilerParams(vmem_limit_bytes=12 * 1024 * 1024),
    )(*[pltpu.with_memory_space_constraint(a, pltpu.VMEM) for a in args])
    return (potential, tgt_scaling, mass)


def solution(mesh):
    return jax.shard_map(
        shards,
        mesh=mesh,
        in_specs=(
            P(("grp", "row"), None),
            P(("grp", "row")),
            P(("grp", "row"), None),
            P(("grp", "row")),
        ),
        out_specs=(P(None, ("grp", "row")), P(None, ("grp", "row")), P(None, ("grp", "row"))),
        check_vma=False,
    )
```

```python
import functools
import math

import jax
import jax.numpy as jnp
from jax import lax
from jax.experimental import pallas as pl
from jax.experimental.pallas import tpu as pltpu
from jax.sharding import PartitionSpec as P

CLASSES = 32
ITERS = 3
INVERSE_TEMP = 20.0
ENTROPY_TEMP = 0.05
LANES = 128
EXTRA = 16
TILE = 256
F32 = jnp.float32
BF16 = jnp.bfloat16


def slot_bits(core, top):
    layer = list(range(2, top))
    return (layer if core else layer[::-1]) + [1]


def rounds(core, top):
    bits = list(range(1, top))
    bits = bits[1 - core :] + bits[: 1 - core]
    return [bits[low : low + 2] for low in range(0, len(bits), 2)]


def flips_of(bits):
    flips = [0]
    for bit in bits:
        flips += [flip | 1 << bit for flip in flips]
    return flips[1:]


def exchange(block, *flips):
    devices = lax.axis_size("row")
    return lax.ppermute(block, "row", [(d, d ^ flips[d % len(flips)]) for d in range(devices)])


def call(body, outs, *args, flops=0):
    space = pl.BlockSpec(memory_space=pltpu.VMEM)
    moved = sum(a.size * a.dtype.itemsize for a in args)
    return pl.pallas_call(
        body,
        out_shape=[pltpu.VMEM(shape, dtype) for shape, dtype in outs],
        in_specs=[space] * len(args),
        out_specs=[space] * len(outs),
        compiler_params=pltpu.CompilerParams(vmem_limit_bytes=12 * 1024 * 1024),
        cost_estimate=pl.CostEstimate(flops=flops, bytes_accessed=moved, transcendentals=0),
    )(*[pltpu.with_memory_space_constraint(a, pltpu.VMEM) for a in args])


def unit_rows(values):
    widened = values.astype(F32)
    meansq = jnp.mean(widened * widened, axis=1, keepdims=True)
    return (widened * lax.rsqrt(meansq + 1e-06) / math.sqrt(values.shape[1])).astype(BF16)


def hot(labels, classes=CLASSES):
    rows = lax.broadcasted_iota(jnp.int32, (classes, labels.shape[1]), 0)
    return (labels == rows).astype(F32)


def pack_body(embed_hbm, tgt_hbm, cand_hbm, out_ref, tgt_ref, cand_ref, sems):
    rows = embed_hbm.shape[0]
    copies = [
        pltpu.make_async_copy(cand_hbm, cand_ref, sems.at[0]),
        pltpu.make_async_copy(tgt_hbm, tgt_ref, sems.at[1]),
        pltpu.make_async_copy(embed_hbm, out_ref.at[pl.ds(0, rows)], sems.at[2]),
    ]
    for copy in copies:
        copy.start()
    copies[0].wait()
    counts = lax.dot_general(
        jnp.ones((EXTRA, cand_ref.shape[1]), BF16),
        hot(cand_ref[...]).astype(BF16),
        (((1,), (1,)), ((), ())),
        preferred_element_type=F32,
    )
    high = counts.astype(BF16).astype(F32)
    even = lax.broadcasted_iota(jnp.int32, counts.shape, 0) % 2 == 0
    out_ref[rows:, LANES:] = jnp.zeros((EXTRA, LANES), BF16)
    out_ref[rows:, LANES : LANES + CLASSES] = jnp.where(even, high, counts - high).astype(BF16)
    copies[1].wait()
    out_ref[rows:, :LANES] = jnp.broadcast_to(
        tgt_ref[...].astype(F32), (EXTRA, LANES)
    ).astype(BF16)
    copies[2].wait()


def pack(tgt_embed, tgt_labels, cand_labels):
    rows, width = tgt_embed.shape
    anywhere = pl.BlockSpec(memory_space=pl.ANY)
    return pl.pallas_call(
        pack_body,
        out_shape=pltpu.VMEM((rows + EXTRA, width), BF16),
        in_specs=[anywhere] * 3,
        out_specs=pl.BlockSpec(memory_space=pltpu.VMEM),
        scratch_shapes=[
            pltpu.VMEM(tgt_labels.shape, jnp.int32),
            pltpu.VMEM(cand_labels.shape, jnp.int32),
            pltpu.SemaphoreType.DMA((3,)),
        ],
        compiler_params=pltpu.CompilerParams(vmem_limit_bytes=12 * 1024 * 1024),
    )(*[
        pltpu.with_memory_space_constraint(a, pltpu.HBM)
        for a in (tgt_embed, tgt_labels, cand_labels)
    ])


def fill_body(unit_ref, held_ref, kernel_ref, sums_ref, *, tgt_rows):
    rows = tgt_rows + EXTRA
    cand_rows = unit_ref.shape[0]
    per = TILE // tgt_rows
    for col in range(0, kernel_ref.shape[1], TILE):
        first = col // tgt_rows
        block = jnp.concatenate(
            [held_ref[pl.ds((first + s) * rows, tgt_rows), :] for s in range(per)]
        )
        tgt_unit = unit_rows(block)
        for row in range(0, cand_rows, TILE):
            scores = lax.dot_general(
                unit_ref[row : row + TILE, :],
                tgt_unit,
                (((1,), (1,)), ((), ())),
                preferred_element_type=F32,
            )
            tile = jnp.exp(INVERSE_TEMP * scores)
            kernel_ref[row : row + TILE, col : col + TILE] = tile.astype(BF16)
            sums = tile[:, :LANES]
            for lane in range(LANES, TILE, LANES):
                sums += tile[:, lane : lane + LANES]
            if col:
                sums += sums_ref[row : row + TILE, :]
            sums_ref[row : row + TILE, :] = sums


def image_of(kernels, scale_ref):
    image = 0.0
    first = 0
    for kernel_ref in kernels:
        slots = kernel_ref.shape[1] // scale_ref.shape[2]
        scale_v = jnp.concatenate([scale_ref[s] for s in range(first, first + slots)], axis=1)
        image += lax.dot_general(
            kernel_ref[...], scale_v, (((1,), (1,)), ((), ())), preferred_element_type=F32
        )
        first += slots
    return image.T


def put_column(scale_ub, kernels, out_ref):
    width = out_ref.shape[2]
    first = 0
    for kernel_ref in kernels:
        part = jnp.dot(scale_ub, kernel_ref[...], preferred_element_type=F32)
        slots = kernel_ref.shape[1] // width
        for s in range(slots):
            out_ref[first + s] = part[:, s * width : (s + 1) * width].astype(out_ref.dtype)
        first += slots


def extras(refs, tgt_rows):
    rows = tgt_rows + EXTRA
    for ref in refs:
        for s in range(ref.shape[0] // rows):
            yield ref[pl.ds(s * rows + tgt_rows, EXTRA), :].astype(F32)


def target_body(*refs):
    *held_refs, marg_ref = refs
    slots, _, tgt_rows = marg_ref.shape
    total = jnp.zeros((CLASSES, tgt_rows), F32)
    for s, extra in enumerate(extras(held_refs, tgt_rows)):
        weight = 1.0 + 3.0 * hot(extra[:1, :LANES].astype(jnp.int32))
        total += weight
        if s < slots:
            marg_ref[s] = weight
    total = jnp.sum(total, axis=1, keepdims=True)
    for s in range(slots):
        marg_ref[s] = marg_ref[s] / total


def first_body(weight_ref, *refs, parts):
    refs, (marg_ref, scale_ref, column_ref) = refs[:-3], refs[-3:]
    kernels, sums_refs, held_refs = refs[:parts], refs[parts : 3 * parts], refs[3 * parts :]
    counts = jnp.zeros((EXTRA, LANES), F32)
    for extra in extras(held_refs, column_ref.shape[2]):
        counts += extra[:, LANES:]
    count = jnp.broadcast_to(counts[:1] + counts[1:2], (LANES, LANES)).T[:CLASSES, :1]
    candidates = weight_ref.shape[1] * 2 * column_ref.shape[0]
    marg = weight_ref[...] / (candidates + 3.0 * count)
    marg_ref[...] = marg
    sums = sum(ref[...] for ref in sums_refs)
    image = jnp.sum(sums.T, axis=0, keepdims=True)
    scale_ub = (marg / image).astype(BF16)
    scale_ref[...] = scale_ub
    put_column(scale_ub, kernels, column_ref)


def column_body(scale_ref, *refs):
    put_column(scale_ref[...], refs[:-1], refs[-1])


def image_body(scale_ref, *refs):
    refs[-1][...] = image_of(refs[:-1], scale_ref)


def step_body(scale_ref, image_ref, marg_ref, *refs):
    kernels, (out_ref, rounded_ref, column_ref) = refs[:-3], refs[-3:]
    image = image_ref[...] + image_of(kernels, scale_ref)
    scale_u = marg_ref[...] / image
    out_ref[...] = scale_u
    rounded_ref[...] = scale_u.astype(BF16)
    put_column(scale_u.astype(BF16), kernels, column_ref)


def last_body(scale_ref, image_ref, u_ref, scale_v_ref, *refs, candidates):
    kernels, (mass_ref, own_ref) = refs[:-2], refs[-2:]
    own_ref[...] = scale_v_ref[0]
    image = image_ref[...] + image_of(kernels, scale_ref)
    mass_ref[...] = candidates * u_ref[...] * image


def slot_of(slot, flips, slots):
    top = slots.bit_length()
    found = []
    for core, flip in enumerate(flips):
        turned = sum(1 << i for i, bit in enumerate(slot_bits(core, top)) if flip >> bit & 1)
        found.append(slot ^ turned)
    if found[0] == found[1]:
        return found[0]
    return found[0] + lax.axis_index("row") % 2 * (found[1] - found[0])


def total_of(slot, own_ref, got_refs, flips):
    total = own_ref[slot]
    for pair, got_ref in zip(flips, got_refs):
        total += got_ref[slot_of(slot, pair, own_ref.shape[0])].astype(F32)
    return total


def sum_body(own_ref, *refs, flips):
    *got_refs, total_ref, sent_ref = refs
    for slot in range(own_ref.shape[0]):
        total = total_of(slot, own_ref, got_refs, flips)
        total_ref[slot] = total
        sent_ref[slot] = total.astype(BF16)


def scale_body(own_ref, marg_ref, *refs, flips):
    got_refs, outs = refs[: len(flips)], refs[len(flips) :]
    for slot in range(own_ref.shape[0]):
        scale_v = marg_ref[slot] / total_of(slot, own_ref, got_refs, flips)
        for out_ref in outs:
            out_ref[slot] = scale_v.astype(out_ref.dtype)


def shards(cand_embed, cand_labels, tgt_embed, tgt_labels):
    devices = lax.axis_size("row")
    top = devices.bit_length() - 1
    slots = devices // 2
    cand_rows, width = cand_embed.shape
    tgt_rows = tgt_embed.shape[0]
    cand_labels = cand_labels.reshape(1, cand_rows)
    block = (slots, CLASSES, tgt_rows)
    image_type = ((CLASSES, cand_rows), F32)
    rounded_type = ((CLASSES, cand_rows), BF16)
    half_flops = 2 * cand_rows * slots * tgt_rows * 128

    def fill(held):
        columns = held.shape[0] // (tgt_rows + EXTRA) * tgt_rows
        return call(
            functools.partial(fill_body, tgt_rows=tgt_rows),
            [((cand_rows, columns), BF16), ((cand_rows, LANES), F32)],
            cand_unit, held, flops=4 * 2 * cand_rows * columns * 128,
        )

    held = piece = pack(tgt_embed, tgt_labels.reshape(1, tgt_rows), cand_labels)
    cand_unit = unit_rows(cand_embed)
    weight = 1.0 + 3.0 * hot(cand_labels)
    across = []
    for bits in list(zip(slot_bits(0, top), slot_bits(1, top)))[:-1]:
        turned = exchange(held, *[1 << bit for bit in bits])
        across.append(exchange(piece, 2))
        piece, across, cand_unit, weight = lax.optimization_barrier(
            (turned, across, cand_unit, weight)
        )
        held = jnp.concatenate([held, piece])
    later = exchange(piece, 2)
    near = [held, jnp.concatenate(across)]
    far = [exchange(part, 1) for part in near]
    filled = [[fill(part) for part in side] for side in (near, far)]
    later, filled = lax.optimization_barrier((later, filled))
    near.append(later)
    far.append(exchange(later, 1))
    for side, parts in zip((near, far), filled):
        parts.append(fill(side[-1]))
    near_kernels, near_sums = zip(*filled[0])
    far_kernels, far_sums = zip(*filled[1])

    cand_marg, scale_ub, far_column = call(
        functools.partial(first_body, parts=len(near)),
        [image_type, rounded_type, (block, BF16)],
        weight, *far_kernels, *near_sums, *far_sums, *near, *far, flops=half_flops,
    )
    (tgt_marg,) = call(target_body, [(block, F32)], *near, *far, flops=half_flops)
    for step in range(ITERS):
        if step:
            scale_u, scale_ub, far_column = call(
                step_body,
                [image_type, rounded_type, (block, BF16)],
                far_vb, image, cand_marg, *far_kernels, flops=2 * half_flops,
            )
        got = exchange(far_column, 1)
        (column,) = call(
            column_body, [(block, F32)], scale_ub, *near_kernels, flops=half_flops
        )
        column = column + got.astype(F32)
        sent = column.astype(BF16)
        order = list(zip(rounds(0, top), rounds(1, top)))
        for place, pair in enumerate(order):
            flips = list(zip(*[flips_of(bits) for bits in pair]))
            found = [exchange(sent, *turn) for turn in flips]
            if place < len(order) - 1:
                column, sent = call(
                    functools.partial(sum_body, flips=flips),
                    [(block, F32), (block, BF16)], column, *found,
                )
        last = step == ITERS - 1
        if last:
            potential = ENTROPY_TEMP * jnp.log(scale_u)
            found, potential = lax.optimization_barrier((found, potential))
        scale_vb, *scale_v = call(
            functools.partial(scale_body, flips=flips),
            [(block, BF16)] + [(block, F32)] * last,
            column, tgt_marg, *found,
        )
        far_vb = exchange(scale_vb, 1)
        (image,) = call(image_body, [image_type], scale_vb, *near_kernels, flops=half_flops)
    space = pl.BlockSpec(memory_space=pltpu.VMEM)
    args = [far_vb, image, scale_u, *scale_v, *far_kernels]
    mass, tgt_scaling = pl.pallas_call(
        functools.partial(last_body, candidates=float(cand_rows * devices)),
        out_shape=[
            jax.ShapeDtypeStruct(*image_type), jax.ShapeDtypeStruct((CLASSES, tgt_rows), F32)
        ],
        in_specs=[space] * len(args),
        out_specs=[space] * 2,
        compiler_params=pltpu.CompilerParams(vmem_limit_bytes=12 * 1024 * 1024),
    )(*[pltpu.with_memory_space_constraint(a, pltpu.VMEM) for a in args])
    return (potential, tgt_scaling, mass)


def solution(mesh):
    return jax.shard_map(
        shards,
        mesh=mesh,
        in_specs=(
            P(("grp", "row"), None),
            P(("grp", "row")),
            P(("grp", "row"), None),
            P(("grp", "row")),
        ),
        out_specs=(P(None, ("grp", "row")), P(None, ("grp", "row")), P(None, ("grp", "row"))),
        check_vma=False,
    )
```

```python
import functools
import math

import jax
import jax.numpy as jnp
from jax import lax
from jax.experimental import pallas as pl
from jax.experimental.pallas import tpu as pltpu
from jax.sharding import PartitionSpec as P

CLASSES = 32
ITERS = 3
INVERSE_TEMP = 20.0
ENTROPY_TEMP = 0.05
LANES = 128
EXTRA = 16
TILE = 256
F32 = jnp.float32
BF16 = jnp.bfloat16


def parity(index, top):
    return sum(index // (1 << bit) % 2 for bit in range(top)) % 2


def slot_bits(kind, top):
    layer = list(range(2, top))
    return (layer if kind else layer[::-1]) + [1]


def rounds(kind, top):
    bits = list(range(1, top))
    bits = bits[1 - kind :] + bits[: 1 - kind]
    return [bits[low : low + 2] for low in range(0, len(bits), 2)]


def flips_of(bits):
    flips = [0]
    for bit in bits:
        flips += [flip | 1 << bit for flip in flips]
    return flips[1:]


def exchange(block, *flips):
    devices = lax.axis_size("row")
    top = devices.bit_length() - 1
    pairs = []
    for d in range(devices):
        flip = flips[parity(d, top) % len(flips)]
        pairs.append((d, d ^ flip ^ parity(flip, top)))
    return lax.ppermute(block, "row", pairs)


def swap(block):
    devices = lax.axis_size("row")
    return lax.ppermute(block, "row", [(d, d ^ 1) for d in range(devices)])


def call(body, outs, *args, flops=0):
    space = pl.BlockSpec(memory_space=pltpu.VMEM)
    moved = sum(a.size * a.dtype.itemsize for a in args)
    return pl.pallas_call(
        body,
        out_shape=[pltpu.VMEM(shape, dtype) for shape, dtype in outs],
        in_specs=[space] * len(args),
        out_specs=[space] * len(outs),
        compiler_params=pltpu.CompilerParams(vmem_limit_bytes=12 * 1024 * 1024),
        cost_estimate=pl.CostEstimate(flops=flops, bytes_accessed=moved, transcendentals=0),
    )(*[pltpu.with_memory_space_constraint(a, pltpu.VMEM) for a in args])


def unit_rows(values):
    widened = values.astype(F32)
    meansq = jnp.mean(widened * widened, axis=1, keepdims=True)
    return (widened * lax.rsqrt(meansq + 1e-06) / math.sqrt(values.shape[1])).astype(BF16)


def hot(labels, classes=CLASSES):
    rows = lax.broadcasted_iota(jnp.int32, (classes, labels.shape[1]), 0)
    return (labels == rows).astype(F32)


def pack_body(embed_hbm, tgt_hbm, cand_hbm, out_ref, tgt_ref, cand_ref, sems):
    rows = embed_hbm.shape[0]
    copies = [
        pltpu.make_async_copy(cand_hbm, cand_ref, sems.at[0]),
        pltpu.make_async_copy(tgt_hbm, tgt_ref, sems.at[1]),
        pltpu.make_async_copy(embed_hbm, out_ref.at[pl.ds(0, rows)], sems.at[2]),
    ]
    for copy in copies:
        copy.start()
    copies[0].wait()
    counts = lax.dot_general(
        jnp.ones((EXTRA, cand_ref.shape[1]), BF16),
        hot(cand_ref[...]).astype(BF16),
        (((1,), (1,)), ((), ())),
        preferred_element_type=F32,
    )
    high = counts.astype(BF16).astype(F32)
    even = lax.broadcasted_iota(jnp.int32, counts.shape, 0) % 2 == 0
    out_ref[rows:, LANES:] = jnp.zeros((EXTRA, LANES), BF16)
    out_ref[rows:, LANES : LANES + CLASSES] = jnp.where(even, high, counts - high).astype(BF16)
    copies[1].wait()
    out_ref[rows:, :LANES] = jnp.broadcast_to(
        tgt_ref[...].astype(F32), (EXTRA, LANES)
    ).astype(BF16)
    copies[2].wait()


def pack(tgt_embed, tgt_labels, cand_labels):
    rows, width = tgt_embed.shape
    anywhere = pl.BlockSpec(memory_space=pl.ANY)
    return pl.pallas_call(
        pack_body,
        out_shape=pltpu.VMEM((rows + EXTRA, width), BF16),
        in_specs=[anywhere] * 3,
        out_specs=pl.BlockSpec(memory_space=pltpu.VMEM),
        scratch_shapes=[
            pltpu.VMEM(tgt_labels.shape, jnp.int32),
            pltpu.VMEM(cand_labels.shape, jnp.int32),
            pltpu.SemaphoreType.DMA((3,)),
        ],
        compiler_params=pltpu.CompilerParams(vmem_limit_bytes=12 * 1024 * 1024),
    )(*[
        pltpu.with_memory_space_constraint(a, pltpu.HBM)
        for a in (tgt_embed, tgt_labels, cand_labels)
    ])


def fill_body(unit_ref, held_ref, kernel_ref, sums_ref, *, tgt_rows):
    rows = tgt_rows + EXTRA
    cand_rows = unit_ref.shape[0]
    per = TILE // tgt_rows
    for col in range(0, kernel_ref.shape[1], TILE):
        first = col // tgt_rows
        block = jnp.concatenate(
            [held_ref[pl.ds((first + s) * rows, tgt_rows), :] for s in range(per)]
        )
        tgt_unit = unit_rows(block)
        for row in range(0, cand_rows, TILE):
            scores = lax.dot_general(
                unit_ref[row : row + TILE, :],
                tgt_unit,
                (((1,), (1,)), ((), ())),
                preferred_element_type=F32,
            )
            tile = jnp.exp(INVERSE_TEMP * scores)
            kernel_ref[row : row + TILE, col : col + TILE] = tile.astype(BF16)
            sums = tile[:, :LANES]
            for lane in range(LANES, TILE, LANES):
                sums += tile[:, lane : lane + LANES]
            if col:
                sums += sums_ref[row : row + TILE, :]
            sums_ref[row : row + TILE, :] = sums


def image_of(kernels, scale_ref):
    image = 0.0
    first = 0
    for kernel_ref in kernels:
        slots = kernel_ref.shape[1] // scale_ref.shape[2]
        scale_v = jnp.concatenate([scale_ref[s] for s in range(first, first + slots)], axis=1)
        image += lax.dot_general(
            kernel_ref[...], scale_v, (((1,), (1,)), ((), ())), preferred_element_type=F32
        )
        first += slots
    return image.T


def put_column(scale_ub, kernels, out_ref):
    width = out_ref.shape[2]
    first = 0
    for kernel_ref in kernels:
        part = jnp.dot(scale_ub, kernel_ref[...], preferred_element_type=F32)
        slots = kernel_ref.shape[1] // width
        for s in range(slots):
            out_ref[first + s] = part[:, s * width : (s + 1) * width].astype(out_ref.dtype)
        first += slots


def extras(refs, tgt_rows):
    rows = tgt_rows + EXTRA
    for ref in refs:
        for s in range(ref.shape[0] // rows):
            yield ref[pl.ds(s * rows + tgt_rows, EXTRA), :].astype(F32)


def target_body(*refs):
    *held_refs, marg_ref = refs
    slots, _, tgt_rows = marg_ref.shape
    total = jnp.zeros((CLASSES, tgt_rows), F32)
    for s, extra in enumerate(extras(held_refs, tgt_rows)):
        weight = 1.0 + 3.0 * hot(extra[:1, :LANES].astype(jnp.int32))
        total += weight
        if s < slots:
            marg_ref[s] = weight
    total = jnp.sum(total, axis=1, keepdims=True)
    for s in range(slots):
        marg_ref[s] = marg_ref[s] / total


def first_body(weight_ref, *refs, parts):
    refs, (marg_ref, scale_ref, column_ref) = refs[:-3], refs[-3:]
    kernels, sums_refs, held_refs = refs[:parts], refs[parts : 3 * parts], refs[3 * parts :]
    counts = jnp.zeros((EXTRA, LANES), F32)
    for extra in extras(held_refs, column_ref.shape[2]):
        counts += extra[:, LANES:]
    count = jnp.broadcast_to(counts[:1] + counts[1:2], (LANES, LANES)).T[:CLASSES, :1]
    candidates = weight_ref.shape[1] * 2 * column_ref.shape[0]
    marg = weight_ref[...] / (candidates + 3.0 * count)
    marg_ref[...] = marg
    sums = sum(ref[...] for ref in sums_refs)
    image = jnp.sum(sums.T, axis=0, keepdims=True)
    scale_ub = (marg / image).astype(BF16)
    scale_ref[...] = scale_ub
    put_column(scale_ub, kernels, column_ref)


def column_body(scale_ref, *refs):
    put_column(scale_ref[...], refs[:-1], refs[-1])


def image_body(scale_ref, *refs):
    refs[-1][...] = image_of(refs[:-1], scale_ref)


def step_body(scale_ref, image_ref, marg_ref, *refs, parts):
    kernels, (rounded_ref, column_ref, *out_refs) = refs[:parts], refs[parts:]
    image = image_ref[...] + image_of(kernels, scale_ref)
    scale_u = marg_ref[...] / image
    for out_ref in out_refs:
        out_ref[...] = scale_u
    rounded_ref[...] = scale_u.astype(BF16)
    put_column(scale_u.astype(BF16), kernels, column_ref)


def last_body(scale_ref, image_ref, u_ref, scale_v_ref, *refs, candidates):
    kernels, (mass_ref, own_ref) = refs[:-2], refs[-2:]
    own_ref[...] = scale_v_ref[0]
    image = image_ref[...] + image_of(kernels, scale_ref)
    mass_ref[...] = candidates * u_ref[...] * image


def slot_of(slot, flips, slots):
    top = slots.bit_length()
    found = []
    for kind, flip in enumerate(flips):
        turned = sum(1 << i for i, bit in enumerate(slot_bits(kind, top)) if flip >> bit & 1)
        found.append(slot ^ turned)
    if found[0] == found[1]:
        return found[0]
    return found[0] + parity(lax.axis_index("row"), top) * (found[1] - found[0])


def total_of(slot, own_ref, got_refs, flips):
    total = own_ref[slot]
    for pair, got_ref in zip(flips, got_refs):
        total += got_ref[slot_of(slot, pair, own_ref.shape[0])].astype(F32)
    return total


def sum_body(own_ref, *refs, flips):
    *got_refs, total_ref, sent_ref = refs
    for slot in range(own_ref.shape[0]):
        total = total_of(slot, own_ref, got_refs, flips)
        total_ref[slot] = total
        sent_ref[slot] = total.astype(BF16)


def scale_body(own_ref, marg_ref, *refs, flips):
    got_refs, outs = refs[: len(flips)], refs[len(flips) :]
    for slot in range(own_ref.shape[0]):
        scale_v = marg_ref[slot] / total_of(slot, own_ref, got_refs, flips)
        for out_ref in outs:
            out_ref[slot] = scale_v.astype(out_ref.dtype)


def shards(cand_embed, cand_labels, tgt_embed, tgt_labels):
    devices = lax.axis_size("row")
    top = devices.bit_length() - 1
    slots = devices // 2
    cand_rows, width = cand_embed.shape
    tgt_rows = tgt_embed.shape[0]
    cand_labels = cand_labels.reshape(1, cand_rows)
    block = (slots, CLASSES, tgt_rows)
    image_type = ((CLASSES, cand_rows), F32)
    rounded_type = ((CLASSES, cand_rows), BF16)
    half_flops = 2 * cand_rows * slots * tgt_rows * 128

    def fill(held):
        columns = held.shape[0] // (tgt_rows + EXTRA) * tgt_rows
        return call(
            functools.partial(fill_body, tgt_rows=tgt_rows),
            [((cand_rows, columns), BF16), ((cand_rows, LANES), F32)],
            cand_unit, held, flops=4 * 2 * cand_rows * columns * 128,
        )

    held = piece = pack(tgt_embed, tgt_labels.reshape(1, tgt_rows), cand_labels)
    cand_unit = unit_rows(cand_embed)
    weight = 1.0 + 3.0 * hot(cand_labels)
    across = []
    for bits in list(zip(slot_bits(0, top), slot_bits(1, top)))[:-1]:
        turned = exchange(held, *[1 << bit for bit in bits])
        across.append(exchange(piece, 2))
        piece, across, cand_unit, weight = lax.optimization_barrier(
            (turned, across, cand_unit, weight)
        )
        held = jnp.concatenate([held, piece])
    later = exchange(piece, 2)
    near = [held, jnp.concatenate(across)]
    far = [swap(part) for part in near]
    filled = [[fill(part) for part in side] for side in (near, far)]
    later, filled = lax.optimization_barrier((later, filled))
    near.append(later)
    far.append(swap(later))
    for side, parts in zip((near, far), filled):
        parts.append(fill(side[-1]))
    near_kernels, near_sums = zip(*filled[0])
    far_kernels, far_sums = zip(*filled[1])

    cand_marg, scale_ub, far_column = call(
        functools.partial(first_body, parts=len(near)),
        [image_type, rounded_type, (block, BF16)],
        weight, *far_kernels, *near_sums, *far_sums, *near, *far, flops=half_flops,
    )
    (tgt_marg,) = call(target_body, [(block, F32)], *near, *far, flops=half_flops)
    for step in range(ITERS):
        last = step == ITERS - 1
        if step:
            scale_ub, far_column, *scale_u = call(
                functools.partial(step_body, parts=len(far)),
                [rounded_type, (block, BF16)] + [image_type] * last,
                far_vb, image, cand_marg, *far_kernels, flops=2 * half_flops,
            )
        got = swap(far_column)
        (column,) = call(
            column_body, [(block, F32)], scale_ub, *near_kernels, flops=half_flops
        )
        column = column + got.astype(F32)
        sent = column.astype(BF16)
        order = list(zip(rounds(0, top), rounds(1, top)))
        for place, pair in enumerate(order):
            flips = list(zip(*[flips_of(bits) for bits in pair]))
            found = [exchange(sent, *turn) for turn in flips]
            if place < len(order) - 1:
                column, sent = call(
                    functools.partial(sum_body, flips=flips),
                    [(block, F32), (block, BF16)], column, *found,
                )
        if last:
            potential = ENTROPY_TEMP * jnp.log(scale_u[0])
            found, potential = lax.optimization_barrier((found, potential))
        scale_vb, *scale_v = call(
            functools.partial(scale_body, flips=flips),
            [(block, BF16)] + [(block, F32)] * last,
            column, tgt_marg, *found,
        )
        far_vb = swap(scale_vb)
        (image,) = call(image_body, [image_type], scale_vb, *near_kernels, flops=half_flops)
    space = pl.BlockSpec(memory_space=pltpu.VMEM)
    args = [far_vb, image, *scale_u, *scale_v, *far_kernels]
    mass, tgt_scaling = pl.pallas_call(
        functools.partial(last_body, candidates=float(cand_rows * devices)),
        out_shape=[
            jax.ShapeDtypeStruct(*image_type), jax.ShapeDtypeStruct((CLASSES, tgt_rows), F32)
        ],
        in_specs=[space] * len(args),
        out_specs=[space] * 2,
        compiler_params=pltpu.CompilerParams(vmem_limit_bytes=12 * 1024 * 1024),
    )(*[pltpu.with_memory_space_constraint(a, pltpu.VMEM) for a in args])
    return (potential, tgt_scaling, mass)


def solution(mesh):
    return jax.shard_map(
        shards,
        mesh=mesh,
        in_specs=(
            P(("grp", "row"), None),
            P(("grp", "row")),
            P(("grp", "row"), None),
            P(("grp", "row")),
        ),
        out_specs=(P(None, ("grp", "row")), P(None, ("grp", "row")), P(None, ("grp", "row"))),
        check_vma=False,
    )
```

```python
import functools
import math

import jax
import jax.numpy as jnp
from jax import lax
from jax.experimental import pallas as pl
from jax.experimental.pallas import tpu as pltpu
from jax.sharding import PartitionSpec as P

CLASSES = 32
ITERS = 3
INVERSE_TEMP = 20.0
ENTROPY_TEMP = 0.05
LANES = 128
EXTRA = 16
TILE = 256
F32 = jnp.float32
BF16 = jnp.bfloat16


def parity(index, top):
    return sum(index // (1 << bit) % 2 for bit in range(top)) % 2


def slot_bits(kind, top):
    layer = list(range(2, top))
    return (layer if kind else layer[::-1]) + [1]


def rounds(top):
    bits = list(range(1, top))
    return [bits[low : low + 2] for low in range(0, len(bits), 2)]


def flips_of(bits):
    flips = [0]
    for bit in bits:
        flips += [flip | 1 << bit for flip in flips]
    return flips[1:]


def exchange(block, *flips):
    devices = lax.axis_size("row")
    top = devices.bit_length() - 1
    pairs = []
    for d in range(devices):
        flip = flips[parity(d, top) % len(flips)]
        pairs.append((d, d ^ flip ^ parity(flip, top)))
    return lax.ppermute(block, "row", pairs)


def swap(block):
    devices = lax.axis_size("row")
    return lax.ppermute(block, "row", [(d, d ^ 1) for d in range(devices)])


def call(body, outs, *args, flops=0):
    space = pl.BlockSpec(memory_space=pltpu.VMEM)
    moved = sum(a.size * a.dtype.itemsize for a in args)
    return pl.pallas_call(
        body,
        out_shape=[pltpu.VMEM(shape, dtype) for shape, dtype in outs],
        in_specs=[space] * len(args),
        out_specs=[space] * len(outs),
        compiler_params=pltpu.CompilerParams(vmem_limit_bytes=12 * 1024 * 1024),
        cost_estimate=pl.CostEstimate(flops=flops, bytes_accessed=moved, transcendentals=0),
    )(*[pltpu.with_memory_space_constraint(a, pltpu.VMEM) for a in args])


def unit_rows(values):
    widened = values.astype(F32)
    meansq = jnp.mean(widened * widened, axis=1, keepdims=True)
    return (widened * lax.rsqrt(meansq + 1e-06) / math.sqrt(values.shape[1])).astype(BF16)


def hot(labels, classes=CLASSES):
    rows = lax.broadcasted_iota(jnp.int32, (classes, labels.shape[1]), 0)
    return (labels == rows).astype(F32)


def pack_body(embed_hbm, tgt_hbm, cand_hbm, out_ref, tgt_ref, cand_ref, sems):
    rows = embed_hbm.shape[0]
    copies = [
        pltpu.make_async_copy(cand_hbm, cand_ref, sems.at[0]),
        pltpu.make_async_copy(tgt_hbm, tgt_ref, sems.at[1]),
        pltpu.make_async_copy(embed_hbm, out_ref.at[pl.ds(0, rows)], sems.at[2]),
    ]
    for copy in copies:
        copy.start()
    copies[0].wait()
    counts = lax.dot_general(
        jnp.ones((EXTRA, cand_ref.shape[1]), BF16),
        hot(cand_ref[...]).astype(BF16),
        (((1,), (1,)), ((), ())),
        preferred_element_type=F32,
    )
    high = counts.astype(BF16).astype(F32)
    even = lax.broadcasted_iota(jnp.int32, counts.shape, 0) % 2 == 0
    out_ref[rows:, LANES:] = jnp.zeros((EXTRA, LANES), BF16)
    out_ref[rows:, LANES : LANES + CLASSES] = jnp.where(even, high, counts - high).astype(BF16)
    copies[1].wait()
    out_ref[rows:, :LANES] = jnp.broadcast_to(
        tgt_ref[...].astype(F32), (EXTRA, LANES)
    ).astype(BF16)
    copies[2].wait()


def pack(tgt_embed, tgt_labels, cand_labels):
    rows, width = tgt_embed.shape
    anywhere = pl.BlockSpec(memory_space=pl.ANY)
    return pl.pallas_call(
        pack_body,
        out_shape=pltpu.VMEM((rows + EXTRA, width), BF16),
        in_specs=[anywhere] * 3,
        out_specs=pl.BlockSpec(memory_space=pltpu.VMEM),
        scratch_shapes=[
            pltpu.VMEM(tgt_labels.shape, jnp.int32),
            pltpu.VMEM(cand_labels.shape, jnp.int32),
            pltpu.SemaphoreType.DMA((3,)),
        ],
        compiler_params=pltpu.CompilerParams(vmem_limit_bytes=12 * 1024 * 1024),
    )(*[
        pltpu.with_memory_space_constraint(a, pltpu.HBM)
        for a in (tgt_embed, tgt_labels, cand_labels)
    ])


def fill_body(unit_ref, held_ref, kernel_ref, sums_ref, *, tgt_rows):
    rows = tgt_rows + EXTRA
    cand_rows = unit_ref.shape[0]
    per = TILE // tgt_rows
    for col in range(0, kernel_ref.shape[1], TILE):
        first = col // tgt_rows
        block = jnp.concatenate(
            [held_ref[pl.ds((first + s) * rows, tgt_rows), :] for s in range(per)]
        )
        tgt_unit = unit_rows(block)
        for row in range(0, cand_rows, TILE):
            scores = lax.dot_general(
                unit_ref[row : row + TILE, :],
                tgt_unit,
                (((1,), (1,)), ((), ())),
                preferred_element_type=F32,
            )
            tile = jnp.exp(INVERSE_TEMP * scores)
            kernel_ref[row : row + TILE, col : col + TILE] = tile.astype(BF16)
            sums = tile[:, :LANES]
            for lane in range(LANES, TILE, LANES):
                sums += tile[:, lane : lane + LANES]
            if col:
                sums += sums_ref[row : row + TILE, :]
            sums_ref[row : row + TILE, :] = sums


def image_of(kernels, scale_ref):
    image = 0.0
    first = 0
    for kernel_ref in kernels:
        slots = kernel_ref.shape[1] // scale_ref.shape[2]
        scale_v = jnp.concatenate([scale_ref[s] for s in range(first, first + slots)], axis=1)
        image += lax.dot_general(
            kernel_ref[...], scale_v, (((1,), (1,)), ((), ())), preferred_element_type=F32
        )
        first += slots
    return image.T


def put_column(scale_ub, kernels, out_ref):
    width = out_ref.shape[2]
    first = 0
    for kernel_ref in kernels:
        part = jnp.dot(scale_ub, kernel_ref[...], preferred_element_type=F32)
        slots = kernel_ref.shape[1] // width
        for s in range(slots):
            out_ref[first + s] = part[:, s * width : (s + 1) * width].astype(out_ref.dtype)
        first += slots


def extras(refs, tgt_rows):
    rows = tgt_rows + EXTRA
    for ref in refs:
        for s in range(ref.shape[0] // rows):
            yield ref[pl.ds(s * rows + tgt_rows, EXTRA), :].astype(F32)


def target_body(*refs):
    *held_refs, marg_ref = refs
    slots, _, tgt_rows = marg_ref.shape
    total = jnp.zeros((CLASSES, tgt_rows), F32)
    for s, extra in enumerate(extras(held_refs, tgt_rows)):
        weight = 1.0 + 3.0 * hot(extra[:1, :LANES].astype(jnp.int32))
        total += weight
        if s < slots:
            marg_ref[s] = weight
    total = jnp.sum(total, axis=1, keepdims=True)
    for s in range(slots):
        marg_ref[s] = marg_ref[s] / total


def first_body(weight_ref, *refs, parts):
    refs, (marg_ref, scale_ref, column_ref) = refs[:-3], refs[-3:]
    kernels, sums_refs, held_refs = refs[:parts], refs[parts : 3 * parts], refs[3 * parts :]
    counts = jnp.zeros((EXTRA, LANES), F32)
    for extra in extras(held_refs, column_ref.shape[2]):
        counts += extra[:, LANES:]
    count = jnp.broadcast_to(counts[:1] + counts[1:2], (LANES, LANES)).T[:CLASSES, :1]
    candidates = weight_ref.shape[1] * 2 * column_ref.shape[0]
    marg = weight_ref[...] / (candidates + 3.0 * count)
    marg_ref[...] = marg
    sums = sum(ref[...] for ref in sums_refs)
    image = jnp.sum(sums.T, axis=0, keepdims=True)
    scale_ub = (marg / image).astype(BF16)
    scale_ref[...] = scale_ub
    put_column(scale_ub, kernels, column_ref)


def column_body(scale_ref, *refs):
    put_column(scale_ref[...], refs[:-1], refs[-1])


def image_body(scale_ref, *refs):
    refs[-1][...] = image_of(refs[:-1], scale_ref)


def step_body(scale_ref, image_ref, marg_ref, *refs, parts):
    kernels, (rounded_ref, column_ref, *out_refs) = refs[:parts], refs[parts:]
    image = image_ref[...] + image_of(kernels, scale_ref)
    scale_u = marg_ref[...] / image
    for out_ref in out_refs:
        out_ref[...] = scale_u
    rounded_ref[...] = scale_u.astype(BF16)
    put_column(scale_u.astype(BF16), kernels, column_ref)


def last_body(scale_ref, image_ref, u_ref, scale_v_ref, *refs, candidates):
    kernels, (mass_ref, own_ref) = refs[:-2], refs[-2:]
    own_ref[...] = scale_v_ref[0]
    image = image_ref[...] + image_of(kernels, scale_ref)
    mass_ref[...] = candidates * u_ref[...] * image


def slot_of(slot, flips, slots):
    top = slots.bit_length()
    found = []
    for kind, flip in enumerate(flips):
        turned = sum(1 << i for i, bit in enumerate(slot_bits(kind, top)) if flip >> bit & 1)
        found.append(slot ^ turned)
    if found[0] == found[1]:
        return found[0]
    return found[0] + parity(lax.axis_index("row"), top) * (found[1] - found[0])


def total_of(slot, own_ref, got_refs, flips):
    total = own_ref[slot]
    for pair, got_ref in zip(flips, got_refs):
        total += got_ref[slot_of(slot, pair, own_ref.shape[0])].astype(F32)
    return total


def sum_body(own_ref, *refs, flips):
    *got_refs, total_ref, sent_ref = refs
    for slot in range(own_ref.shape[0]):
        total = total_of(slot, own_ref, got_refs, flips)
        total_ref[slot] = total
        sent_ref[slot] = total.astype(BF16)


def scale_body(own_ref, marg_ref, *refs, flips):
    got_refs, outs = refs[: len(flips)], refs[len(flips) :]
    for slot in range(own_ref.shape[0]):
        scale_v = marg_ref[slot] / total_of(slot, own_ref, got_refs, flips)
        for out_ref in outs:
            out_ref[slot] = scale_v.astype(out_ref.dtype)


def shards(cand_embed, cand_labels, tgt_embed, tgt_labels):
    devices = lax.axis_size("row")
    top = devices.bit_length() - 1
    slots = devices // 2
    cand_rows, width = cand_embed.shape
    tgt_rows = tgt_embed.shape[0]
    cand_labels = cand_labels.reshape(1, cand_rows)
    block = (slots, CLASSES, tgt_rows)
    image_type = ((CLASSES, cand_rows), F32)
    rounded_type = ((CLASSES, cand_rows), BF16)
    half_flops = 2 * cand_rows * slots * tgt_rows * 128

    def fill(held):
        columns = held.shape[0] // (tgt_rows + EXTRA) * tgt_rows
        return call(
            functools.partial(fill_body, tgt_rows=tgt_rows),
            [((cand_rows, columns), BF16), ((cand_rows, LANES), F32)],
            cand_unit, held, flops=4 * 2 * cand_rows * columns * 128,
        )

    held = piece = pack(tgt_embed, tgt_labels.reshape(1, tgt_rows), cand_labels)
    cand_unit = unit_rows(cand_embed)
    weight = 1.0 + 3.0 * hot(cand_labels)
    across = []
    for bits in list(zip(slot_bits(0, top), slot_bits(1, top)))[:-1]:
        turned = exchange(held, *[1 << bit for bit in bits])
        across.append(exchange(piece, 2))
        piece, across, cand_unit, weight = lax.optimization_barrier(
            (turned, across, cand_unit, weight)
        )
        held = jnp.concatenate([held, piece])
    later = exchange(piece, 2)
    near = [held, jnp.concatenate(across)]
    far = [swap(part) for part in near]
    filled = [[fill(part) for part in side] for side in (near, far)]
    later, filled = lax.optimization_barrier((later, filled))
    near.append(later)
    far.append(swap(later))
    for side, parts in zip((near, far), filled):
        parts.append(fill(side[-1]))
    near_kernels, near_sums = zip(*filled[0])
    far_kernels, far_sums = zip(*filled[1])

    cand_marg, scale_ub, far_column = call(
        functools.partial(first_body, parts=len(near)),
        [image_type, rounded_type, (block, BF16)],
        weight, *far_kernels, *near_sums, *far_sums, *near, *far, flops=half_flops,
    )
    (tgt_marg,) = call(target_body, [(block, F32)], *near, *far, flops=half_flops)
    for step in range(ITERS):
        last = step == ITERS - 1
        if step:
            scale_ub, far_column, *scale_u = call(
                functools.partial(step_body, parts=len(far)),
                [rounded_type, (block, BF16)] + [image_type] * last,
                far_vb, image, cand_marg, *far_kernels, flops=2 * half_flops,
            )
        got = swap(far_column)
        (column,) = call(
            column_body, [(block, F32)], scale_ub, *near_kernels, flops=half_flops
        )
        column = column + got.astype(F32)
        sent = column.astype(BF16)
        order = rounds(top)
        for place, bits in enumerate(order):
            flips = [(flip, flip) for flip in flips_of(bits)]
            found = [exchange(sent, *turn) for turn in flips]
            if place < len(order) - 1:
                column, sent = call(
                    functools.partial(sum_body, flips=flips),
                    [(block, F32), (block, BF16)], column, *found,
                )
        if last:
            potential = ENTROPY_TEMP * jnp.log(scale_u[0])
            found, potential = lax.optimization_barrier((found, potential))
        scale_vb, *scale_v = call(
            functools.partial(scale_body, flips=flips),
            [(block, BF16)] + [(block, F32)] * last,
            column, tgt_marg, *found,
        )
        far_vb = swap(scale_vb)
        (image,) = call(image_body, [image_type], scale_vb, *near_kernels, flops=half_flops)
    space = pl.BlockSpec(memory_space=pltpu.VMEM)
    args = [far_vb, image, *scale_u, *scale_v, *far_kernels]
    mass, tgt_scaling = pl.pallas_call(
        functools.partial(last_body, candidates=float(cand_rows * devices)),
        out_shape=[
            jax.ShapeDtypeStruct(*image_type), jax.ShapeDtypeStruct((CLASSES, tgt_rows), F32)
        ],
        in_specs=[space] * len(args),
        out_specs=[space] * 2,
        compiler_params=pltpu.CompilerParams(vmem_limit_bytes=12 * 1024 * 1024),
    )(*[pltpu.with_memory_space_constraint(a, pltpu.VMEM) for a in args])
    return (potential, tgt_scaling, mass)


def solution(mesh):
    return jax.shard_map(
        shards,
        mesh=mesh,
        in_specs=(
            P(("grp", "row"), None),
            P(("grp", "row")),
            P(("grp", "row"), None),
            P(("grp", "row")),
        ),
        out_specs=(P(None, ("grp", "row")), P(None, ("grp", "row")), P(None, ("grp", "row"))),
        check_vma=False,
    )
```

```python
import functools
import math

import jax
import jax.numpy as jnp
from jax import lax
from jax.experimental import pallas as pl
from jax.experimental.pallas import tpu as pltpu
from jax.sharding import PartitionSpec as P

CLASSES = 32
ITERS = 3
INVERSE_TEMP = 20.0
ENTROPY_TEMP = 0.05
LANES = 128
EXTRA = 16
TILE = 256
F32 = jnp.float32
BF16 = jnp.bfloat16


def parity(index, top):
    return sum(index // (1 << bit) % 2 for bit in range(top)) % 2


def slot_bits(kind, top):
    layer = list(range(2, top))
    return (layer if kind else layer[::-1]) + [1]


def order(kind, top):
    bits = list(range(1, top))
    return bits[1 - kind :] + bits[: 1 - kind]


def flips_of(bits):
    flips = [0]
    for bit in bits:
        flips += [flip | 1 << bit for flip in flips]
    return flips[1:]


def exchange(block, *flips):
    devices = lax.axis_size("row")
    top = devices.bit_length() - 1
    pairs = []
    for d in range(devices):
        flip = flips[parity(d, top) % len(flips)]
        pairs.append((d, d ^ flip ^ parity(flip, top)))
    return lax.ppermute(block, "row", pairs)


def swap(block):
    devices = lax.axis_size("row")
    return lax.ppermute(block, "row", [(d, d ^ 1) for d in range(devices)])


def call(body, outs, *args, flops=0):
    space = pl.BlockSpec(memory_space=pltpu.VMEM)
    moved = sum(a.size * a.dtype.itemsize for a in args)
    return pl.pallas_call(
        body,
        out_shape=[pltpu.VMEM(shape, dtype) for shape, dtype in outs],
        in_specs=[space] * len(args),
        out_specs=[space] * len(outs),
        compiler_params=pltpu.CompilerParams(vmem_limit_bytes=12 * 1024 * 1024),
        cost_estimate=pl.CostEstimate(flops=flops, bytes_accessed=moved, transcendentals=0),
    )(*[pltpu.with_memory_space_constraint(a, pltpu.VMEM) for a in args])


def unit_rows(values):
    widened = values.astype(F32)
    meansq = jnp.mean(widened * widened, axis=1, keepdims=True)
    return (widened * lax.rsqrt(meansq + 1e-06) / math.sqrt(values.shape[1])).astype(BF16)


def hot(labels, classes=CLASSES):
    rows = lax.broadcasted_iota(jnp.int32, (classes, labels.shape[1]), 0)
    return (labels == rows).astype(F32)


def pack_body(embed_hbm, tgt_hbm, cand_hbm, out_ref, tgt_ref, cand_ref, sems):
    rows = embed_hbm.shape[0]
    copies = [
        pltpu.make_async_copy(cand_hbm, cand_ref, sems.at[0]),
        pltpu.make_async_copy(tgt_hbm, tgt_ref, sems.at[1]),
        pltpu.make_async_copy(embed_hbm, out_ref.at[pl.ds(0, rows)], sems.at[2]),
    ]
    for copy in copies:
        copy.start()
    copies[0].wait()
    counts = lax.dot_general(
        jnp.ones((EXTRA, cand_ref.shape[1]), BF16),
        hot(cand_ref[...]).astype(BF16),
        (((1,), (1,)), ((), ())),
        preferred_element_type=F32,
    )
    high = counts.astype(BF16).astype(F32)
    even = lax.broadcasted_iota(jnp.int32, counts.shape, 0) % 2 == 0
    out_ref[rows:, LANES:] = jnp.zeros((EXTRA, LANES), BF16)
    out_ref[rows:, LANES : LANES + CLASSES] = jnp.where(even, high, counts - high).astype(BF16)
    copies[1].wait()
    out_ref[rows:, :LANES] = jnp.broadcast_to(
        tgt_ref[...].astype(F32), (EXTRA, LANES)
    ).astype(BF16)
    copies[2].wait()


def pack(tgt_embed, tgt_labels, cand_labels):
    rows, width = tgt_embed.shape
    anywhere = pl.BlockSpec(memory_space=pl.ANY)
    return pl.pallas_call(
        pack_body,
        out_shape=pltpu.VMEM((rows + EXTRA, width), BF16),
        in_specs=[anywhere] * 3,
        out_specs=pl.BlockSpec(memory_space=pltpu.VMEM),
        scratch_shapes=[
            pltpu.VMEM(tgt_labels.shape, jnp.int32),
            pltpu.VMEM(cand_labels.shape, jnp.int32),
            pltpu.SemaphoreType.DMA((3,)),
        ],
        compiler_params=pltpu.CompilerParams(vmem_limit_bytes=12 * 1024 * 1024),
    )(*[
        pltpu.with_memory_space_constraint(a, pltpu.HBM)
        for a in (tgt_embed, tgt_labels, cand_labels)
    ])


def fill_body(unit_ref, held_ref, kernel_ref, sums_ref, *, tgt_rows):
    rows = tgt_rows + EXTRA
    cand_rows = unit_ref.shape[0]
    per = TILE // tgt_rows
    for col in range(0, kernel_ref.shape[1], TILE):
        first = col // tgt_rows
        block = jnp.concatenate(
            [held_ref[pl.ds((first + s) * rows, tgt_rows), :] for s in range(per)]
        )
        tgt_unit = unit_rows(block)
        for row in range(0, cand_rows, TILE):
            scores = lax.dot_general(
                unit_ref[row : row + TILE, :],
                tgt_unit,
                (((1,), (1,)), ((), ())),
                preferred_element_type=F32,
            )
            tile = jnp.exp(INVERSE_TEMP * scores)
            kernel_ref[row : row + TILE, col : col + TILE] = tile.astype(BF16)
            sums = tile[:, :LANES]
            for lane in range(LANES, TILE, LANES):
                sums += tile[:, lane : lane + LANES]
            if col:
                sums += sums_ref[row : row + TILE, :]
            sums_ref[row : row + TILE, :] = sums


def image_of(kernels, scale_ref):
    image = 0.0
    first = 0
    for kernel_ref in kernels:
        slots = kernel_ref.shape[1] // scale_ref.shape[2]
        scale_v = jnp.concatenate([scale_ref[s] for s in range(first, first + slots)], axis=1)
        image += lax.dot_general(
            kernel_ref[...], scale_v, (((1,), (1,)), ((), ())), preferred_element_type=F32
        )
        first += slots
    return image.T


def put_column(scale_ub, kernels, out_ref):
    width = out_ref.shape[2]
    first = 0
    for kernel_ref in kernels:
        part = jnp.dot(scale_ub, kernel_ref[...], preferred_element_type=F32)
        slots = kernel_ref.shape[1] // width
        for s in range(slots):
            out_ref[first + s] = part[:, s * width : (s + 1) * width].astype(out_ref.dtype)
        first += slots


def extras(refs, tgt_rows):
    rows = tgt_rows + EXTRA
    for ref in refs:
        for s in range(ref.shape[0] // rows):
            yield ref[pl.ds(s * rows + tgt_rows, EXTRA), :].astype(F32)


def target_body(*refs):
    *held_refs, marg_ref = refs
    slots, _, tgt_rows = marg_ref.shape
    total = jnp.zeros((CLASSES, tgt_rows), F32)
    for s, extra in enumerate(extras(held_refs, tgt_rows)):
        weight = 1.0 + 3.0 * hot(extra[:1, :LANES].astype(jnp.int32))
        total += weight
        if s < slots:
            marg_ref[s] = weight
    total = jnp.sum(total, axis=1, keepdims=True)
    for s in range(slots):
        marg_ref[s] = marg_ref[s] / total


def first_body(weight_ref, *refs, parts):
    refs, (marg_ref, scale_ref, column_ref) = refs[:-3], refs[-3:]
    kernels, sums_refs, held_refs = refs[:parts], refs[parts : 3 * parts], refs[3 * parts :]
    counts = jnp.zeros((EXTRA, LANES), F32)
    for extra in extras(held_refs, column_ref.shape[2]):
        counts += extra[:, LANES:]
    count = jnp.broadcast_to(counts[:1] + counts[1:2], (LANES, LANES)).T[:CLASSES, :1]
    candidates = weight_ref.shape[1] * 2 * column_ref.shape[0]
    marg = weight_ref[...] / (candidates + 3.0 * count)
    marg_ref[...] = marg
    sums = sum(ref[...] for ref in sums_refs)
    image = jnp.sum(sums.T, axis=0, keepdims=True)
    scale_ub = (marg / image).astype(BF16)
    scale_ref[...] = scale_ub
    put_column(scale_ub, kernels, column_ref)


def column_body(scale_ref, *refs):
    put_column(scale_ref[...], refs[:-1], refs[-1])


def image_body(scale_ref, *refs):
    refs[-1][...] = image_of(refs[:-1], scale_ref)


def step_body(scale_ref, image_ref, marg_ref, *refs, parts):
    kernels, (rounded_ref, column_ref, *out_refs) = refs[:parts], refs[parts:]
    image = image_ref[...] + image_of(kernels, scale_ref)
    scale_u = marg_ref[...] / image
    for out_ref in out_refs:
        out_ref[...] = scale_u
    rounded_ref[...] = scale_u.astype(BF16)
    put_column(scale_u.astype(BF16), kernels, column_ref)


def last_body(scale_ref, image_ref, u_ref, scale_v_ref, *refs, candidates):
    kernels, (mass_ref, own_ref) = refs[:-2], refs[-2:]
    own_ref[...] = scale_v_ref[0]
    image = image_ref[...] + image_of(kernels, scale_ref)
    mass_ref[...] = candidates * u_ref[...] * image


def spread(top):
    return list(zip(*[flips_of(order(kind, top)[:2]) for kind in range(2)]))


def slot_of(kept, flips, top):
    found = []
    for kind, flip in enumerate(flips):
        own = sum(1 << bit for i, bit in enumerate(order(kind, top)[2:]) if kept >> i & 1)
        bits = enumerate(slot_bits(kind, top))
        found.append(sum(1 << i for i, bit in bits if (flip ^ own) >> bit & 1))
    if found[0] == found[1]:
        return found[0]
    return found[0] + parity(lax.axis_index("row"), top) * (found[1] - found[0])


def part_body(column_ref, got_ref, *out_refs, top):
    for out_ref, flips in zip(out_refs, [(0, 0)] + spread(top)):
        for kept in range(out_ref.shape[0]):
            slot = slot_of(kept, flips, top)
            total = column_ref[slot] + got_ref[slot].astype(F32)
            out_ref[kept] = total.astype(out_ref.dtype)


def total_of(kept, own_ref, got_refs, masks):
    total = own_ref[kept]
    for mask, got_ref in zip(masks, got_refs):
        total += got_ref[kept ^ mask].astype(F32)
    return total


def sum_body(own_ref, *refs, masks):
    *got_refs, total_ref, sent_ref = refs
    for kept in range(own_ref.shape[0]):
        total = total_of(kept, own_ref, got_refs, masks)
        total_ref[kept] = total
        sent_ref[kept] = total.astype(BF16)


def scale_body(own_ref, marg_ref, *refs, masks, top):
    got_refs, outs = refs[: len(masks)], refs[len(masks) :]
    for kept in range(own_ref.shape[0]):
        marg = marg_ref[slot_of(kept, (0, 0), top)]
        scale_v = marg / total_of(kept, own_ref, got_refs, masks)
        for out_ref in outs:
            out_ref[kept] = scale_v.astype(out_ref.dtype)


def join_body(*refs, top):
    *part_refs, out_ref = refs
    for part_ref, flips in zip(part_refs, [(0, 0)] + spread(top)):
        for kept in range(part_ref.shape[0]):
            out_ref[slot_of(kept, flips, top)] = part_ref[kept]


def shards(cand_embed, cand_labels, tgt_embed, tgt_labels):
    devices = lax.axis_size("row")
    top = devices.bit_length() - 1
    slots = devices // 2
    cand_rows, width = cand_embed.shape
    tgt_rows = tgt_embed.shape[0]
    cand_labels = cand_labels.reshape(1, cand_rows)
    block = (slots, CLASSES, tgt_rows)
    kept = (slots // 4, CLASSES, tgt_rows)
    image_type = ((CLASSES, cand_rows), F32)
    rounded_type = ((CLASSES, cand_rows), BF16)
    half_flops = 2 * cand_rows * slots * tgt_rows * 128

    def fill(held):
        columns = held.shape[0] // (tgt_rows + EXTRA) * tgt_rows
        return call(
            functools.partial(fill_body, tgt_rows=tgt_rows),
            [((cand_rows, columns), BF16), ((cand_rows, LANES), F32)],
            cand_unit, held, flops=4 * 2 * cand_rows * columns * 128,
        )

    held = piece = pack(tgt_embed, tgt_labels.reshape(1, tgt_rows), cand_labels)
    cand_unit = unit_rows(cand_embed)
    weight = 1.0 + 3.0 * hot(cand_labels)
    across = []
    for bits in list(zip(slot_bits(0, top), slot_bits(1, top)))[:-1]:
        turned = exchange(held, *[1 << bit for bit in bits])
        across.append(exchange(piece, 2))
        piece, across, cand_unit, weight = lax.optimization_barrier(
            (turned, across, cand_unit, weight)
        )
        held = jnp.concatenate([held, piece])
    later = exchange(piece, 2)
    near = [held, jnp.concatenate(across)]
    far = [swap(part) for part in near]
    filled = [[fill(part) for part in side] for side in (near, far)]
    later, filled = lax.optimization_barrier((later, filled))
    near.append(later)
    far.append(swap(later))
    for side, parts in zip((near, far), filled):
        parts.append(fill(side[-1]))
    near_kernels, near_sums = zip(*filled[0])
    far_kernels, far_sums = zip(*filled[1])

    cand_marg, scale_ub, far_column = call(
        functools.partial(first_body, parts=len(near)),
        [image_type, rounded_type, (block, BF16)],
        weight, *far_kernels, *near_sums, *far_sums, *near, *far, flops=half_flops,
    )
    (tgt_marg,) = call(target_body, [(block, F32)], *near, *far, flops=half_flops)
    for step in range(ITERS):
        last = step == ITERS - 1
        if step:
            scale_ub, far_column, *scale_u = call(
                functools.partial(step_body, parts=len(far)),
                [rounded_type, (block, BF16)] + [image_type] * last,
                far_vb, image, cand_marg, *far_kernels, flops=2 * half_flops,
            )
        got = swap(far_column)
        (column,) = call(
            column_body, [(block, F32)], scale_ub, *near_kernels, flops=half_flops
        )
        column, *sent = call(
            functools.partial(part_body, top=top),
            [(kept, F32)] + [(kept, BF16)] * 3, column, got,
        )
        found = [exchange(part, *flips) for part, flips in zip(sent, spread(top))]
        masks = [0] * 3
        for low in range(2, top - 1, 2):
            column, sent = call(
                functools.partial(sum_body, masks=masks),
                [(kept, F32), (kept, BF16)], column, *found,
            )
            turns = [flips_of(order(kind, top)[low : low + 2]) for kind in range(2)]
            found = [exchange(sent, *flips) for flips in zip(*turns)]
            masks = flips_of(list(range(low - 2, low - 2 + len(turns[0]).bit_length())))
        if last:
            potential = ENTROPY_TEMP * jnp.log(scale_u[0])
            found, potential = lax.optimization_barrier((found, potential))
        own_vb, *scale_v = call(
            functools.partial(scale_body, masks=masks, top=top),
            [(kept, BF16)] + [(kept, F32)] * last,
            column, tgt_marg, *found,
        )
        found = [exchange(own_vb, *flips) for flips in spread(top)]
        (scale_vb,) = call(functools.partial(join_body, top=top), [(block, BF16)], own_vb, *found)
        far_vb = swap(scale_vb)
        (image,) = call(image_body, [image_type], scale_vb, *near_kernels, flops=half_flops)
    space = pl.BlockSpec(memory_space=pltpu.VMEM)
    args = [far_vb, image, *scale_u, *scale_v, *far_kernels]
    mass, tgt_scaling = pl.pallas_call(
        functools.partial(last_body, candidates=float(cand_rows * devices)),
        out_shape=[
            jax.ShapeDtypeStruct(*image_type), jax.ShapeDtypeStruct((CLASSES, tgt_rows), F32)
        ],
        in_specs=[space] * len(args),
        out_specs=[space] * 2,
        compiler_params=pltpu.CompilerParams(vmem_limit_bytes=12 * 1024 * 1024),
    )(*[pltpu.with_memory_space_constraint(a, pltpu.VMEM) for a in args])
    return (potential, tgt_scaling, mass)


def solution(mesh):
    return jax.shard_map(
        shards,
        mesh=mesh,
        in_specs=(
            P(("grp", "row"), None),
            P(("grp", "row")),
            P(("grp", "row"), None),
            P(("grp", "row")),
        ),
        out_specs=(P(None, ("grp", "row")), P(None, ("grp", "row")), P(None, ("grp", "row"))),
        check_vma=False,
    )
```

```python
import functools
import math

import jax
import jax.numpy as jnp
from jax import lax
from jax.experimental import pallas as pl
from jax.experimental.pallas import tpu as pltpu
from jax.sharding import PartitionSpec as P

CLASSES = 32
ITERS = 3
INVERSE_TEMP = 20.0
ENTROPY_TEMP = 0.05
LANES = 128
EXTRA = 16
TILE = 256
F32 = jnp.float32
BF16 = jnp.bfloat16


def parity(index, top):
    return sum(index // (1 << bit) % 2 for bit in range(top)) % 2


def slot_bits(kind, top):
    layer = list(range(2, top))
    return (layer if kind else layer[::-1]) + [1]


def rounds(kind, top):
    bits = list(range(1, top))
    bits = bits[1 - kind :] + bits[: 1 - kind]
    return [bits[low : low + 2] for low in range(0, len(bits), 2)]


def flips_of(bits):
    flips = [0]
    for bit in bits:
        flips += [flip | 1 << bit for flip in flips]
    return flips[1:]


def exchange(block, *flips):
    devices = lax.axis_size("row")
    top = devices.bit_length() - 1
    pairs = []
    for d in range(devices):
        flip = flips[parity(d, top) % len(flips)]
        pairs.append((d, d ^ flip ^ parity(flip, top)))
    return lax.ppermute(block, "row", pairs)


def swap(block):
    devices = lax.axis_size("row")
    return lax.ppermute(block, "row", [(d, d ^ 1) for d in range(devices)])


def call(body, outs, *args, flops=0):
    space = pl.BlockSpec(memory_space=pltpu.VMEM)
    moved = sum(a.size * a.dtype.itemsize for a in args)
    return pl.pallas_call(
        body,
        out_shape=[pltpu.VMEM(shape, dtype) for shape, dtype in outs],
        in_specs=[space] * len(args),
        out_specs=[space] * len(outs),
        compiler_params=pltpu.CompilerParams(vmem_limit_bytes=12 * 1024 * 1024),
        cost_estimate=pl.CostEstimate(flops=flops, bytes_accessed=moved, transcendentals=0),
    )(*[pltpu.with_memory_space_constraint(a, pltpu.VMEM) for a in args])


def unit_rows(values):
    widened = values.astype(F32)
    meansq = jnp.mean(widened * widened, axis=1, keepdims=True)
    return (widened * lax.rsqrt(meansq + 1e-06) / math.sqrt(values.shape[1])).astype(BF16)


def hot(labels, classes=CLASSES):
    rows = lax.broadcasted_iota(jnp.int32, (classes, labels.shape[1]), 0)
    return (labels == rows).astype(F32)


def pack_body(embed_hbm, tgt_hbm, cand_hbm, out_ref, tgt_ref, cand_ref, sems):
    rows = embed_hbm.shape[0]
    copies = [
        pltpu.make_async_copy(cand_hbm, cand_ref, sems.at[0]),
        pltpu.make_async_copy(tgt_hbm, tgt_ref, sems.at[1]),
        pltpu.make_async_copy(embed_hbm, out_ref.at[pl.ds(0, rows)], sems.at[2]),
    ]
    for copy in copies:
        copy.start()
    copies[0].wait()
    counts = lax.dot_general(
        jnp.ones((EXTRA, cand_ref.shape[1]), BF16),
        hot(cand_ref[...]).astype(BF16),
        (((1,), (1,)), ((), ())),
        preferred_element_type=F32,
    )
    high = counts.astype(BF16).astype(F32)
    even = lax.broadcasted_iota(jnp.int32, counts.shape, 0) % 2 == 0
    out_ref[rows:, LANES:] = jnp.zeros((EXTRA, LANES), BF16)
    out_ref[rows:, LANES : LANES + CLASSES] = jnp.where(even, high, counts - high).astype(BF16)
    copies[1].wait()
    out_ref[rows:, :LANES] = jnp.broadcast_to(
        tgt_ref[...].astype(F32), (EXTRA, LANES)
    ).astype(BF16)
    copies[2].wait()


def pack(tgt_embed, tgt_labels, cand_labels):
    rows, width = tgt_embed.shape
    anywhere = pl.BlockSpec(memory_space=pl.ANY)
    return pl.pallas_call(
        pack_body,
        out_shape=pltpu.VMEM((rows + EXTRA, width), BF16),
        in_specs=[anywhere] * 3,
        out_specs=pl.BlockSpec(memory_space=pltpu.VMEM),
        scratch_shapes=[
            pltpu.VMEM(tgt_labels.shape, jnp.int32),
            pltpu.VMEM(cand_labels.shape, jnp.int32),
            pltpu.SemaphoreType.DMA((3,)),
        ],
        compiler_params=pltpu.CompilerParams(vmem_limit_bytes=12 * 1024 * 1024),
    )(*[
        pltpu.with_memory_space_constraint(a, pltpu.HBM)
        for a in (tgt_embed, tgt_labels, cand_labels)
    ])


def fill_body(own_ref, other_ref, held_ref, *out_refs, tgt_rows):
    rows = tgt_rows + EXTRA
    columns = out_refs[0].shape[1]
    per = min(TILE, columns) // tgt_rows
    tile = per * tgt_rows
    for col in range(0, columns, tile):
        first = col // tgt_rows
        block = jnp.concatenate(
            [held_ref[pl.ds((first + s) * rows, tgt_rows), :] for s in range(per)]
        )
        tgt_unit = unit_rows(block)
        for cand_ref, kernel_ref, sums_ref in zip((own_ref, other_ref), out_refs, out_refs[2:]):
            for row in range(0, cand_ref.shape[0], TILE):
                scores = lax.dot_general(
                    cand_ref[row : row + TILE, :],
                    tgt_unit,
                    (((1,), (1,)), ((), ())),
                    preferred_element_type=F32,
                )
                found = jnp.exp(INVERSE_TEMP * scores)
                kernel_ref[row : row + TILE, col : col + tile] = found.astype(BF16)
                sums = found[:, :LANES]
                for lane in range(LANES, tile, LANES):
                    sums += found[:, lane : lane + LANES]
                if col:
                    sums += sums_ref[row : row + TILE, :]
                sums_ref[row : row + TILE, :] = sums


def image_of(kernels, scale_ref):
    image = 0.0
    first = 0
    for kernel_ref in kernels:
        slots = kernel_ref.shape[1] // scale_ref.shape[2]
        scale_v = jnp.concatenate([scale_ref[s] for s in range(first, first + slots)], axis=1)
        image += lax.dot_general(
            kernel_ref[...], scale_v, (((1,), (1,)), ((), ())), preferred_element_type=F32
        )
        first += slots
    return image.T


def put_column(scale_ub, kernels, added, out_refs):
    width = out_refs[0].shape[2]
    first = 0
    for kernel_ref in kernels:
        part = jnp.dot(scale_ub, kernel_ref[...], preferred_element_type=F32)
        slots = kernel_ref.shape[1] // width
        for s in range(slots):
            piece = part[:, s * width : (s + 1) * width]
            if added is not None:
                piece += added[first + s]
            for out_ref in out_refs:
                out_ref[first + s] = piece.astype(out_ref.dtype)
        first += slots


def extras(refs, tgt_rows):
    rows = tgt_rows + EXTRA
    for ref in refs:
        for s in range(ref.shape[0] // rows):
            yield ref[pl.ds(s * rows + tgt_rows, EXTRA), :].astype(F32)


def sums_body(*refs, parts, tgt_rows):
    *refs, out_ref = refs
    each = (out_ref.shape[0] - 8) // 2
    for place in range(2):
        total = sum(ref[...] for ref in refs[place * parts : (place + 1) * parts])
        row = jnp.sum(total.T, axis=0, keepdims=True)
        for i in range(each):
            out_ref[pl.ds(place * each + i, 1), :] = row[:, i * LANES : (i + 1) * LANES]
    counts = jnp.zeros((EXTRA, LANES), F32)
    labels = jnp.zeros((LANES, tgt_rows), F32)
    for extra in extras(refs[2 * parts :], tgt_rows):
        counts += extra[:, LANES:]
        labels += hot(extra[:1, :LANES].astype(jnp.int32), LANES)
    out_ref[pl.ds(2 * each, 8), :] = counts[:8] + counts[1:9]
    out_ref[pl.ds(2 * each + 1, 1), :] = jnp.sum(labels.T, axis=0, keepdims=True)


def count_of(place, mine_ref, got_ref):
    row = mine_ref.shape[0] - 8 + place
    count = mine_ref[pl.ds(row, 1), :] + got_ref[pl.ds(row, 1), :]
    return jnp.broadcast_to(count, (LANES, LANES)).T[:CLASSES, :1]


def first_body(own_weight, other_weight, mine_ref, got_ref, *refs, candidates):
    *kernels, own_marg, other_marg, column_ref, sent_ref = refs
    parts = len(kernels) // 2
    each = (mine_ref.shape[0] - 8) // 2
    total = candidates + 3.0 * count_of(0, mine_ref, got_ref)
    for place, (weight_ref, marg_ref) in enumerate(
        ((own_weight, own_marg), (other_weight, other_marg))
    ):
        rows = [
            mine_ref[pl.ds(place * each + i, 1), :] + got_ref[pl.ds((1 - place) * each + i, 1), :]
            for i in range(each)
        ]
        marg = weight_ref[...] / total
        marg_ref[...] = marg
        scale_ub = (marg / jnp.concatenate(rows, axis=1)).astype(BF16)
        if place == 0:
            put_column(scale_ub, kernels[:parts], None, (column_ref,))
        else:
            put_column(scale_ub, kernels[parts:], column_ref, (column_ref, sent_ref))


def target_body(mine_ref, got_ref, *refs, targets):
    *held_refs, marg_ref = refs
    total = targets + 3.0 * count_of(1, mine_ref, got_ref)
    for s, extra in enumerate(extras(held_refs, marg_ref.shape[2])):
        marg_ref[s] = (1.0 + 3.0 * hot(extra[:1, :LANES].astype(jnp.int32))) / total


def image_body(scale_ref, *refs):
    refs[-1][...] = image_of(refs[:-1], scale_ref)


def own_body(image_ref, got_ref, marg_ref, *refs, parts):
    kernels, (column_ref, *out_refs) = refs[:parts], refs[parts:]
    scale_u = marg_ref[...] / (image_ref[...] + got_ref[...])
    for out_ref in out_refs:
        out_ref[...] = scale_u
    put_column(scale_u.astype(BF16), kernels, None, (column_ref,))


def other_body(image_ref, got_ref, marg_ref, added_ref, *refs):
    *kernels, column_ref, sent_ref = refs
    scale_u = marg_ref[...] / (image_ref[...] + got_ref[...])
    put_column(scale_u.astype(BF16), kernels, added_ref, (column_ref, sent_ref))


def last_body(image_ref, got_ref, u_ref, scale_v_ref, mass_ref, own_ref, *, candidates):
    own_ref[...] = scale_v_ref[0]
    mass_ref[...] = candidates * u_ref[...] * (image_ref[...] + got_ref[...])


def slot_of(slot, flips, slots):
    top = slots.bit_length()
    found = []
    for kind, flip in enumerate(flips):
        turned = sum(1 << i for i, bit in enumerate(slot_bits(kind, top)) if flip >> bit & 1)
        found.append(slot ^ turned)
    if found[0] == found[1]:
        return found[0]
    return found[0] + parity(lax.axis_index("row"), top) * (found[1] - found[0])


def total_of(slot, own_ref, got_refs, flips):
    total = own_ref[slot]
    for pair, got_ref in zip(flips, got_refs):
        total += got_ref[slot_of(slot, pair, own_ref.shape[0])].astype(F32)
    return total


def sum_body(own_ref, *refs, flips):
    *got_refs, total_ref, sent_ref = refs
    for slot in range(own_ref.shape[0]):
        total = total_of(slot, own_ref, got_refs, flips)
        total_ref[slot] = total
        sent_ref[slot] = total.astype(BF16)


def scale_body(own_ref, marg_ref, *refs, flips):
    got_refs, outs = refs[: len(flips)], refs[len(flips) :]
    for slot in range(own_ref.shape[0]):
        scale_v = marg_ref[slot] / total_of(slot, own_ref, got_refs, flips)
        for out_ref in outs:
            out_ref[slot] = scale_v.astype(out_ref.dtype)


def shards(cand_embed, cand_labels, tgt_embed, tgt_labels):
    devices = lax.axis_size("row")
    top = devices.bit_length() - 1
    slots = devices // 2
    cand_rows, width = cand_embed.shape
    tgt_rows = tgt_embed.shape[0]
    label_rows = cand_labels.reshape(cand_rows // LANES, LANES)
    cand_labels = cand_labels.reshape(1, cand_rows)
    block = (slots, CLASSES, tgt_rows)
    image_type = ((CLASSES, cand_rows), F32)
    half_flops = 2 * cand_rows * slots * tgt_rows * 128

    def fill(held):
        columns = held.shape[0] // (tgt_rows + EXTRA) * tgt_rows
        return call(
            functools.partial(fill_body, tgt_rows=tgt_rows),
            [((cand_rows, columns), BF16)] * 2 + [((cand_rows, LANES), F32)] * 2,
            cand_unit, other_unit, held, flops=8 * 2 * cand_rows * columns * 128,
        )

    held = piece = pack(tgt_embed, tgt_labels.reshape(1, tgt_rows), cand_labels)
    cand_unit = unit_rows(cand_embed)
    weight = 1.0 + 3.0 * hot(cand_labels)
    across = []
    other_unit = None
    for bits in list(zip(slot_bits(0, top), slot_bits(1, top)))[:-1]:
        turned = exchange(held, *[1 << bit for bit in bits])
        across.append(exchange(piece, 2))
        piece, across, cand_unit, weight, other_unit = lax.optimization_barrier(
            (turned, across, cand_unit, weight, other_unit)
        )
        held = jnp.concatenate([held, piece])
        if other_unit is None:
            other_unit = swap(cand_unit), swap(label_rows)
    later = exchange(piece, 2)
    other_unit, other_labels = other_unit
    other_weight = 1.0 + 3.0 * hot(other_labels.reshape(1, cand_rows))
    near = [held, jnp.concatenate(across)]
    filled = [fill(part) for part in near]
    later, filled, other_weight = lax.optimization_barrier((later, filled, other_weight))
    near.append(later)
    filled.append(fill(later))
    own_kernels, other_kernels, own_sums, other_sums = zip(*filled)

    (mine,) = call(
        functools.partial(sums_body, parts=len(near), tgt_rows=tgt_rows),
        [((2 * cand_rows // LANES + 8, LANES), F32)], *own_sums, *other_sums, *near,
    )
    got = swap(mine)
    own_marg, other_marg, column, sent = call(
        functools.partial(first_body, candidates=float(cand_rows * devices)),
        [image_type, image_type, (block, F32), (block, BF16)],
        weight, other_weight, mine, got, *own_kernels, *other_kernels, flops=2 * half_flops,
    )
    (tgt_marg,) = call(
        functools.partial(target_body, targets=float(tgt_rows * devices)),
        [(block, F32)], mine, got, *near,
    )
    for step in range(ITERS):
        last = step == ITERS - 1
        if step:
            column, *scale_u = call(
                functools.partial(own_body, parts=len(near)),
                [(block, F32)] + [image_type] * last,
                own_image, own_got, own_marg, *own_kernels, flops=half_flops,
            )
            column, sent = call(
                other_body, [(block, F32), (block, BF16)],
                other_image, other_got, other_marg, column, *other_kernels, flops=half_flops,
            )
        order = list(zip(rounds(0, top), rounds(1, top)))
        for place, pair in enumerate(order):
            flips = list(zip(*[flips_of(bits) for bits in pair]))
            found = [exchange(sent, *turn) for turn in flips]
            if place < len(order) - 1:
                column, sent = call(
                    functools.partial(sum_body, flips=flips),
                    [(block, F32), (block, BF16)], column, *found,
                )
        if last:
            potential = ENTROPY_TEMP * jnp.log(scale_u[0])
            found, potential = lax.optimization_barrier((found, potential))
        scale_vb, *scale_v = call(
            functools.partial(scale_body, flips=flips),
            [(block, BF16)] + [(block, F32)] * last,
            column, tgt_marg, *found,
        )
        (other_image,) = call(
            image_body, [image_type], scale_vb, *other_kernels, flops=half_flops
        )
        own_got = swap(other_image)
        (own_image,) = call(image_body, [image_type], scale_vb, *own_kernels, flops=half_flops)
        if not last:
            other_got = swap(own_image)
    space = pl.BlockSpec(memory_space=pltpu.VMEM)
    args = [own_image, own_got, *scale_u, *scale_v]
    mass, tgt_scaling = pl.pallas_call(
        functools.partial(last_body, candidates=float(cand_rows * devices)),
        out_shape=[
            jax.ShapeDtypeStruct(*image_type), jax.ShapeDtypeStruct((CLASSES, tgt_rows), F32)
        ],
        in_specs=[space] * len(args),
        out_specs=[space] * 2,
        compiler_params=pltpu.CompilerParams(vmem_limit_bytes=12 * 1024 * 1024),
    )(*[pltpu.with_memory_space_constraint(a, pltpu.VMEM) for a in args])
    return (potential, tgt_scaling, mass)


def solution(mesh):
    return jax.shard_map(
        shards,
        mesh=mesh,
        in_specs=(
            P(("grp", "row"), None),
            P(("grp", "row")),
            P(("grp", "row"), None),
            P(("grp", "row")),
        ),
        out_specs=(P(None, ("grp", "row")), P(None, ("grp", "row")), P(None, ("grp", "row"))),
        check_vma=False,
    )
```

```python
import functools
import math

import jax
import jax.numpy as jnp
from jax import lax
from jax.experimental import pallas as pl
from jax.experimental.pallas import tpu as pltpu
from jax.sharding import PartitionSpec as P

CLASSES = 32
ITERS = 3
INVERSE_TEMP = 20.0
ENTROPY_TEMP = 0.05
LANES = 128
EXTRA = 16
TILE = 256
F32 = jnp.float32
BF16 = jnp.bfloat16


def parity(index, top):
    return sum(index // (1 << bit) % 2 for bit in range(top)) % 2


def slot_bits(kind, top):
    layer = list(range(2, top))
    return (layer if kind else layer[::-1]) + [1]


def rounds(kind, top):
    bits = list(range(1, top))
    bits = bits[1 - kind :] + bits[: 1 - kind]
    return [bits[low : low + 2] for low in range(0, len(bits), 2)]


def flips_of(bits):
    flips = [0]
    for bit in bits:
        flips += [flip | 1 << bit for flip in flips]
    return flips[1:]


def exchange(block, *flips):
    devices = lax.axis_size("row")
    top = devices.bit_length() - 1
    pairs = []
    for d in range(devices):
        flip = flips[parity(d, top) % len(flips)]
        pairs.append((d, d ^ flip ^ parity(flip, top)))
    return lax.ppermute(block, "row", pairs)


def swap(block):
    devices = lax.axis_size("row")
    return lax.ppermute(block, "row", [(d, d ^ 1) for d in range(devices)])


def call(body, outs, *args, flops=0):
    space = pl.BlockSpec(memory_space=pltpu.VMEM)
    moved = sum(a.size * a.dtype.itemsize for a in args)
    return pl.pallas_call(
        body,
        out_shape=[pltpu.VMEM(shape, dtype) for shape, dtype in outs],
        in_specs=[space] * len(args),
        out_specs=[space] * len(outs),
        compiler_params=pltpu.CompilerParams(vmem_limit_bytes=12 * 1024 * 1024),
        cost_estimate=pl.CostEstimate(flops=flops, bytes_accessed=moved, transcendentals=0),
    )(*[pltpu.with_memory_space_constraint(a, pltpu.VMEM) for a in args])


def unit_rows(values):
    widened = values.astype(F32)
    meansq = jnp.mean(widened * widened, axis=1, keepdims=True)
    return (widened * lax.rsqrt(meansq + 1e-06) / math.sqrt(values.shape[1])).astype(BF16)


def hot(labels, classes=CLASSES):
    rows = lax.broadcasted_iota(jnp.int32, (classes, labels.shape[1]), 0)
    return (labels == rows).astype(F32)


def pack_body(embed_hbm, tgt_hbm, cand_hbm, out_ref, tgt_ref, cand_ref, sems):
    rows = embed_hbm.shape[0]
    copies = [
        pltpu.make_async_copy(cand_hbm, cand_ref, sems.at[0]),
        pltpu.make_async_copy(tgt_hbm, tgt_ref, sems.at[1]),
        pltpu.make_async_copy(embed_hbm, out_ref.at[pl.ds(0, rows)], sems.at[2]),
    ]
    for copy in copies:
        copy.start()
    copies[0].wait()
    counts = lax.dot_general(
        jnp.ones((EXTRA, cand_ref.shape[1]), BF16),
        hot(cand_ref[...]).astype(BF16),
        (((1,), (1,)), ((), ())),
        preferred_element_type=F32,
    )
    high = counts.astype(BF16).astype(F32)
    even = lax.broadcasted_iota(jnp.int32, counts.shape, 0) % 2 == 0
    out_ref[rows:, LANES:] = jnp.zeros((EXTRA, LANES), BF16)
    out_ref[rows:, LANES : LANES + CLASSES] = jnp.where(even, high, counts - high).astype(BF16)
    copies[1].wait()
    out_ref[rows:, :LANES] = jnp.broadcast_to(
        tgt_ref[...].astype(F32), (EXTRA, LANES)
    ).astype(BF16)
    copies[2].wait()


def pack(tgt_embed, tgt_labels, cand_labels):
    rows, width = tgt_embed.shape
    anywhere = pl.BlockSpec(memory_space=pl.ANY)
    return pl.pallas_call(
        pack_body,
        out_shape=pltpu.VMEM((rows + EXTRA, width), BF16),
        in_specs=[anywhere] * 3,
        out_specs=pl.BlockSpec(memory_space=pltpu.VMEM),
        scratch_shapes=[
            pltpu.VMEM(tgt_labels.shape, jnp.int32),
            pltpu.VMEM(cand_labels.shape, jnp.int32),
            pltpu.SemaphoreType.DMA((3,)),
        ],
        compiler_params=pltpu.CompilerParams(vmem_limit_bytes=12 * 1024 * 1024),
    )(*[
        pltpu.with_memory_space_constraint(a, pltpu.HBM)
        for a in (tgt_embed, tgt_labels, cand_labels)
    ])


def unit_body(*refs):
    for in_ref, out_ref in zip(refs, refs[2:]):
        for row in range(0, in_ref.shape[0], TILE):
            out_ref[row : row + TILE, :] = unit_rows(in_ref[row : row + TILE, :])


def block_of(refs, place, tgt_rows, extra=False):
    ref, first = refs[place[0]], place[1] * (tgt_rows + EXTRA)
    return ref[pl.ds(first + tgt_rows, EXTRA) if extra else pl.ds(first, tgt_rows), :]


def fill_body(own_ref, other_ref, *refs, places, tgt_rows):
    held_refs, out_refs = refs[:-4], refs[-4:]
    per = TILE // tgt_rows
    for first in range(0, len(places), per):
        block = jnp.concatenate(
            [block_of(held_refs, place, tgt_rows) for place in places[first : first + per]]
        )
        tgt_unit = unit_rows(block)
        col, tile = first * tgt_rows, block.shape[0]
        for cand_ref, kernel_ref, sums_ref in zip((own_ref, other_ref), out_refs, out_refs[2:]):
            for row in range(0, cand_ref.shape[0], TILE):
                scores = lax.dot_general(
                    cand_ref[row : row + TILE, :],
                    tgt_unit,
                    (((1,), (1,)), ((), ())),
                    preferred_element_type=F32,
                )
                found = jnp.exp(INVERSE_TEMP * scores)
                kernel_ref[row : row + TILE, col : col + tile] = found.astype(BF16)
                sums = found[:, :LANES]
                for lane in range(LANES, tile, LANES):
                    sums += found[:, lane : lane + LANES]
                if col:
                    sums += sums_ref[row : row + TILE, :]
                sums_ref[row : row + TILE, :] = sums


def image_of(kernels, scale_ref):
    image = 0.0
    first = 0
    for kernel_ref in kernels:
        slots = kernel_ref.shape[1] // scale_ref.shape[2]
        scale_v = jnp.concatenate([scale_ref[s] for s in range(first, first + slots)], axis=1)
        image += lax.dot_general(
            kernel_ref[...], scale_v, (((1,), (1,)), ((), ())), preferred_element_type=F32
        )
        first += slots
    return image.T


def put_column(scale_ub, kernels, added, out_refs):
    width = out_refs[0].shape[2]
    first = 0
    for kernel_ref in kernels:
        part = jnp.dot(scale_ub, kernel_ref[...], preferred_element_type=F32)
        slots = kernel_ref.shape[1] // width
        for s in range(slots):
            piece = part[:, s * width : (s + 1) * width]
            if added is not None:
                piece += added[first + s]
            for out_ref in out_refs:
                out_ref[first + s] = piece.astype(out_ref.dtype)
        first += slots


def sums_body(*refs, parts, places, tgt_rows):
    *refs, out_ref = refs
    each = (out_ref.shape[0] - 8) // 2
    for place in range(2):
        total = sum(ref[...] for ref in refs[place * parts : (place + 1) * parts])
        row = jnp.sum(total.T, axis=0, keepdims=True)
        for i in range(each):
            out_ref[pl.ds(place * each + i, 1), :] = row[:, i * LANES : (i + 1) * LANES]
    counts = jnp.zeros((EXTRA, LANES), F32)
    labels = jnp.zeros((LANES, tgt_rows), F32)
    for place in places:
        extra = block_of(refs[2 * parts :], place, tgt_rows, extra=True).astype(F32)
        counts += extra[:, LANES:]
        labels += hot(extra[:1, :LANES].astype(jnp.int32), LANES)
    out_ref[pl.ds(2 * each, 8), :] = counts[:8] + counts[1:9]
    out_ref[pl.ds(2 * each + 1, 1), :] = jnp.sum(labels.T, axis=0, keepdims=True)


def count_of(place, mine_ref, got_ref):
    row = mine_ref.shape[0] - 8 + place
    count = mine_ref[pl.ds(row, 1), :] + got_ref[pl.ds(row, 1), :]
    return jnp.broadcast_to(count, (LANES, LANES)).T[:CLASSES, :1]


def first_body(own_weight, other_weight, mine_ref, got_ref, *refs, candidates):
    *kernels, own_marg, other_marg, column_ref, sent_ref = refs
    parts = len(kernels) // 2
    each = (mine_ref.shape[0] - 8) // 2
    total = candidates + 3.0 * count_of(0, mine_ref, got_ref)
    for place, (weight_ref, marg_ref) in enumerate(
        ((own_weight, own_marg), (other_weight, other_marg))
    ):
        rows = [
            mine_ref[pl.ds(place * each + i, 1), :] + got_ref[pl.ds((1 - place) * each + i, 1), :]
            for i in range(each)
        ]
        marg = weight_ref[...] / total
        marg_ref[...] = marg
        scale_ub = (marg / jnp.concatenate(rows, axis=1)).astype(BF16)
        if place == 0:
            put_column(scale_ub, kernels[:parts], None, (column_ref,))
        else:
            put_column(scale_ub, kernels[parts:], column_ref, (column_ref, sent_ref))


def target_body(mine_ref, got_ref, *refs, places, targets):
    *held_refs, marg_ref = refs
    total = targets + 3.0 * count_of(1, mine_ref, got_ref)
    for s, place in enumerate(places):
        extra = block_of(held_refs, place, marg_ref.shape[2], extra=True).astype(F32)
        marg_ref[s] = (1.0 + 3.0 * hot(extra[:1, :LANES].astype(jnp.int32))) / total


def image_body(scale_ref, *refs):
    refs[-1][...] = image_of(refs[:-1], scale_ref)


def own_body(image_ref, got_ref, marg_ref, *refs, parts):
    kernels, (column_ref, *out_refs) = refs[:parts], refs[parts:]
    scale_u = marg_ref[...] / (image_ref[...] + got_ref[...])
    for out_ref in out_refs:
        out_ref[...] = scale_u
    put_column(scale_u.astype(BF16), kernels, None, (column_ref,))


def other_body(image_ref, got_ref, marg_ref, added_ref, *refs):
    *kernels, column_ref, sent_ref = refs
    scale_u = marg_ref[...] / (image_ref[...] + got_ref[...])
    put_column(scale_u.astype(BF16), kernels, added_ref, (column_ref, sent_ref))


def last_body(image_ref, got_ref, u_ref, scale_v_ref, mass_ref, own_ref, *, candidates):
    own_ref[...] = scale_v_ref[0]
    mass_ref[...] = candidates * u_ref[...] * (image_ref[...] + got_ref[...])


def slot_of(slot, flips, slots):
    top = slots.bit_length()
    found = []
    for kind, flip in enumerate(flips):
        turned = sum(1 << i for i, bit in enumerate(slot_bits(kind, top)) if flip >> bit & 1)
        found.append(slot ^ turned)
    if found[0] == found[1]:
        return found[0]
    return found[0] + parity(lax.axis_index("row"), top) * (found[1] - found[0])


def total_of(slot, own_ref, got_refs, flips):
    total = own_ref[slot]
    for pair, got_ref in zip(flips, got_refs):
        total += got_ref[slot_of(slot, pair, own_ref.shape[0])].astype(F32)
    return total


def sum_body(own_ref, *refs, flips):
    *got_refs, total_ref, sent_ref = refs
    for slot in range(own_ref.shape[0]):
        total = total_of(slot, own_ref, got_refs, flips)
        total_ref[slot] = total
        sent_ref[slot] = total.astype(BF16)


def scale_body(own_ref, marg_ref, *refs, flips):
    got_refs, outs = refs[: len(flips)], refs[len(flips) :]
    for slot in range(own_ref.shape[0]):
        scale_v = marg_ref[slot] / total_of(slot, own_ref, got_refs, flips)
        for out_ref in outs:
            out_ref[slot] = scale_v.astype(out_ref.dtype)


def shards(cand_embed, cand_labels, tgt_embed, tgt_labels):
    devices = lax.axis_size("row")
    top = devices.bit_length() - 1
    slots = devices // 2
    cand_rows, width = cand_embed.shape
    tgt_rows = tgt_embed.shape[0]
    label_rows = cand_labels.reshape(cand_rows // LANES, LANES)
    cand_labels = cand_labels.reshape(1, cand_rows)
    block = (slots, CLASSES, tgt_rows)
    image_type = ((CLASSES, cand_rows), F32)
    half_flops = 2 * cand_rows * slots * tgt_rows * 128

    def found_at(blocks):
        arrays = []
        for array, _ in blocks:
            if not any(array is known for known in arrays):
                arrays.append(array)
        number = {id(array): i for i, array in enumerate(arrays)}
        return arrays, [(number[id(array)], place) for array, place in blocks]

    def fill(blocks):
        arrays, places = found_at(blocks)
        columns = len(blocks) * tgt_rows
        return call(
            functools.partial(fill_body, places=places, tgt_rows=tgt_rows),
            [((cand_rows, columns), BF16)] * 2 + [((cand_rows, LANES), F32)] * 2,
            cand_unit, other_unit, *arrays, flops=8 * 2 * cand_rows * columns * 128,
        )

    held = pack(tgt_embed, tgt_labels.reshape(1, tgt_rows), cand_labels)
    piece, cand_embed, label_rows = lax.optimization_barrier((held, cand_embed, label_rows))
    swapped = swap(cand_embed), swap(label_rows)
    across = []
    stages = list(zip(slot_bits(0, top), slot_bits(1, top)))[:-1]
    for bits in stages[:-1]:
        turned = exchange(held, *[1 << bit for bit in bits])
        across.append(exchange(piece, 2))
        piece, across, swapped = lax.optimization_barrier((turned, across, swapped))
        held = jnp.concatenate([held, piece])
    height = tgt_rows + EXTRA
    half = held.shape[0] // height
    known = sum(part.shape[0] for part in across) // height
    sent = jnp.concatenate([held] + across)
    turned = exchange(sent, *[1 << bit for bit in stages[-1]])
    beside = exchange(piece, 2)
    cand_unit, other_unit = call(unit_body, [(cand_embed.shape, BF16)] * 2, cand_embed, swapped[0])
    weight = 1.0 + 3.0 * hot(cand_labels)
    other_weight = 1.0 + 3.0 * hot(swapped[1].reshape(1, cand_rows))
    turned, beside, cand_unit, other_unit, weight, other_weight = lax.optimization_barrier(
        (turned, beside, cand_unit, other_unit, weight, other_weight)
    )
    later = exchange(turned[known * height : half * height], 2)
    blocks = [(sent, i) for i in range(half)] + [(turned, i) for i in range(half)]
    blocks += [(sent, half + i) for i in range(known)]
    blocks += [(beside, i) for i in range(half - known)]
    filled = [fill(blocks[: 2 * half]), fill(blocks[2 * half :])]
    later, filled = lax.optimization_barrier((later, filled))
    blocks += [(turned, half + i) for i in range(known)]
    blocks += [(later, i) for i in range(half - known)]
    filled.append(fill(blocks[3 * half :]))
    own_kernels, other_kernels, own_sums, other_sums = zip(*filled)
    arrays, places = found_at(blocks)

    (mine,) = call(
        functools.partial(sums_body, parts=len(filled), places=places, tgt_rows=tgt_rows),
        [((2 * cand_rows // LANES + 8, LANES), F32)], *own_sums, *other_sums, *arrays,
    )
    got = swap(mine)
    own_marg, other_marg, column, sent = call(
        functools.partial(first_body, candidates=float(cand_rows * devices)),
        [image_type, image_type, (block, F32), (block, BF16)],
        weight, other_weight, mine, got, *own_kernels, *other_kernels, flops=2 * half_flops,
    )
    (tgt_marg,) = call(
        functools.partial(target_body, places=places, targets=float(tgt_rows * devices)),
        [(block, F32)], mine, got, *arrays,
    )
    for step in range(ITERS):
        last = step == ITERS - 1
        if step:
            column, *scale_u = call(
                functools.partial(own_body, parts=len(own_kernels)),
                [(block, F32)] + [image_type] * last,
                own_image, own_got, own_marg, *own_kernels, flops=half_flops,
            )
            column, sent = call(
                other_body, [(block, F32), (block, BF16)],
                other_image, other_got, other_marg, column, *other_kernels, flops=half_flops,
            )
        order = list(zip(rounds(0, top), rounds(1, top)))
        for place, pair in enumerate(order):
            flips = list(zip(*[flips_of(bits) for bits in pair]))
            found = [exchange(sent, *turn) for turn in flips]
            if place < len(order) - 1:
                column, sent = call(
                    functools.partial(sum_body, flips=flips),
                    [(block, F32), (block, BF16)], column, *found,
                )
        if last:
            potential = ENTROPY_TEMP * jnp.log(scale_u[0])
            found, potential = lax.optimization_barrier((found, potential))
        scale_vb, *scale_v = call(
            functools.partial(scale_body, flips=flips),
            [(block, BF16)] + [(block, F32)] * last,
            column, tgt_marg, *found,
        )
        (other_image,) = call(
            image_body, [image_type], scale_vb, *other_kernels, flops=half_flops
        )
        own_got = swap(other_image)
        (own_image,) = call(image_body, [image_type], scale_vb, *own_kernels, flops=half_flops)
        if not last:
            other_got = swap(own_image)
    space = pl.BlockSpec(memory_space=pltpu.VMEM)
    args = [own_image, own_got, *scale_u, *scale_v]
    mass, tgt_scaling = pl.pallas_call(
        functools.partial(last_body, candidates=float(cand_rows * devices)),
        out_shape=[
            jax.ShapeDtypeStruct(*image_type), jax.ShapeDtypeStruct((CLASSES, tgt_rows), F32)
        ],
        in_specs=[space] * len(args),
        out_specs=[space] * 2,
        compiler_params=pltpu.CompilerParams(vmem_limit_bytes=12 * 1024 * 1024),
    )(*[pltpu.with_memory_space_constraint(a, pltpu.VMEM) for a in args])
    return (potential, tgt_scaling, mass)


def solution(mesh):
    return jax.shard_map(
        shards,
        mesh=mesh,
        in_specs=(
            P(("grp", "row"), None),
            P(("grp", "row")),
            P(("grp", "row"), None),
            P(("grp", "row")),
        ),
        out_specs=(P(None, ("grp", "row")), P(None, ("grp", "row")), P(None, ("grp", "row"))),
        check_vma=False,
    )
```

```python
import functools
import math

import jax
import jax.numpy as jnp
from jax import lax
from jax.experimental import pallas as pl
from jax.experimental.pallas import tpu as pltpu
from jax.sharding import PartitionSpec as P

CLASSES = 32
ITERS = 3
INVERSE_TEMP = 20.0
ENTROPY_TEMP = 0.05
LANES = 128
EXTRA = 16
TILE = 256
F32 = jnp.float32
BF16 = jnp.bfloat16


def parity(index, top):
    return sum(index // (1 << bit) % 2 for bit in range(top)) % 2


def slot_bits(kind, top):
    layer = list(range(2, top))
    return (layer if kind else layer[::-1]) + [1]


def rounds(kind, top):
    bits = list(range(1, top))
    bits = bits[1 - kind :] + bits[: 1 - kind]
    return [bits[low : low + 2] for low in range(0, len(bits), 2)]


def flips_of(bits):
    flips = [0]
    for bit in bits:
        flips += [flip | 1 << bit for flip in flips]
    return flips[1:]


def exchange(block, *flips):
    devices = lax.axis_size("row")
    top = devices.bit_length() - 1
    pairs = []
    for d in range(devices):
        flip = flips[parity(d, top) % len(flips)]
        pairs.append((d, d ^ flip ^ parity(flip, top)))
    return lax.ppermute(block, "row", pairs)


def swap(block):
    devices = lax.axis_size("row")
    return lax.ppermute(block, "row", [(d, d ^ 1) for d in range(devices)])


def call(body, outs, *args, flops=0):
    space = pl.BlockSpec(memory_space=pltpu.VMEM)
    moved = sum(a.size * a.dtype.itemsize for a in args)
    return pl.pallas_call(
        body,
        out_shape=[pltpu.VMEM(shape, dtype) for shape, dtype in outs],
        in_specs=[space] * len(args),
        out_specs=[space] * len(outs),
        compiler_params=pltpu.CompilerParams(vmem_limit_bytes=12 * 1024 * 1024),
        cost_estimate=pl.CostEstimate(flops=flops, bytes_accessed=moved, transcendentals=0),
    )(*[pltpu.with_memory_space_constraint(a, pltpu.VMEM) for a in args])


def unit_rows(values):
    widened = values.astype(F32)
    meansq = jnp.mean(widened * widened, axis=1, keepdims=True)
    return (widened * lax.rsqrt(meansq + 1e-06) / math.sqrt(values.shape[1])).astype(BF16)


def hot(labels, classes=CLASSES):
    rows = lax.broadcasted_iota(jnp.int32, (classes, labels.shape[1]), 0)
    return (labels == rows).astype(F32)


def pack_body(embed_hbm, tgt_hbm, cand_hbm, out_ref, tgt_ref, cand_ref, sems):
    rows = embed_hbm.shape[0]
    copies = [
        pltpu.make_async_copy(cand_hbm, cand_ref, sems.at[0]),
        pltpu.make_async_copy(tgt_hbm, tgt_ref, sems.at[1]),
        pltpu.make_async_copy(embed_hbm, out_ref.at[pl.ds(0, rows)], sems.at[2]),
    ]
    for copy in copies:
        copy.start()
    copies[0].wait()
    counts = lax.dot_general(
        jnp.ones((EXTRA, cand_ref.shape[1]), BF16),
        hot(cand_ref[...]).astype(BF16),
        (((1,), (1,)), ((), ())),
        preferred_element_type=F32,
    )
    high = counts.astype(BF16).astype(F32)
    even = lax.broadcasted_iota(jnp.int32, counts.shape, 0) % 2 == 0
    out_ref[rows:, LANES:] = jnp.zeros((EXTRA, LANES), BF16)
    out_ref[rows:, LANES : LANES + CLASSES] = jnp.where(even, high, counts - high).astype(BF16)
    copies[1].wait()
    out_ref[rows:, :LANES] = jnp.broadcast_to(
        tgt_ref[...].astype(F32), (EXTRA, LANES)
    ).astype(BF16)
    copies[2].wait()


def pack(tgt_embed, tgt_labels, cand_labels):
    rows, width = tgt_embed.shape
    anywhere = pl.BlockSpec(memory_space=pl.ANY)
    return pl.pallas_call(
        pack_body,
        out_shape=pltpu.VMEM((rows + EXTRA, width), BF16),
        in_specs=[anywhere] * 3,
        out_specs=pl.BlockSpec(memory_space=pltpu.VMEM),
        scratch_shapes=[
            pltpu.VMEM(tgt_labels.shape, jnp.int32),
            pltpu.VMEM(cand_labels.shape, jnp.int32),
            pltpu.SemaphoreType.DMA((3,)),
        ],
        compiler_params=pltpu.CompilerParams(vmem_limit_bytes=12 * 1024 * 1024),
    )(*[
        pltpu.with_memory_space_constraint(a, pltpu.HBM)
        for a in (tgt_embed, tgt_labels, cand_labels)
    ])


def unit_body(in_ref, out_ref):
    for row in range(0, in_ref.shape[0], TILE):
        out_ref[row : row + TILE, :] = unit_rows(in_ref[row : row + TILE, :])


def fill_body(own_ref, other_ref, held_ref, *out_refs, tgt_rows):
    rows = tgt_rows + EXTRA
    columns = out_refs[0].shape[1]
    per = min(TILE, columns) // tgt_rows
    tile = per * tgt_rows
    for col in range(0, columns, tile):
        first = col // tgt_rows
        block = jnp.concatenate(
            [held_ref[pl.ds((first + s) * rows, tgt_rows), :] for s in range(per)]
        )
        tgt_unit = unit_rows(block)
        for cand_ref, kernel_ref, sums_ref in zip((own_ref, other_ref), out_refs, out_refs[2:]):
            for row in range(0, cand_ref.shape[0], TILE):
                scores = lax.dot_general(
                    cand_ref[row : row + TILE, :],
                    tgt_unit,
                    (((1,), (1,)), ((), ())),
                    preferred_element_type=F32,
                )
                found = jnp.exp(INVERSE_TEMP * scores)
                kernel_ref[row : row + TILE, col : col + tile] = found.astype(BF16)
                sums = found[:, :LANES]
                for lane in range(LANES, tile, LANES):
                    sums += found[:, lane : lane + LANES]
                if col:
                    sums += sums_ref[row : row + TILE, :]
                sums_ref[row : row + TILE, :] = sums


def image_of(kernels, scale_ref):
    image = 0.0
    first = 0
    for kernel_ref in kernels:
        slots = kernel_ref.shape[1] // scale_ref.shape[2]
        scale_v = jnp.concatenate([scale_ref[s] for s in range(first, first + slots)], axis=1)
        image += lax.dot_general(
            kernel_ref[...], scale_v, (((1,), (1,)), ((), ())), preferred_element_type=F32
        )
        first += slots
    return image.T


def put_column(scale_ub, kernels, added, out_refs):
    width = out_refs[0].shape[2]
    first = 0
    for kernel_ref in kernels:
        part = jnp.dot(scale_ub, kernel_ref[...], preferred_element_type=F32)
        slots = kernel_ref.shape[1] // width
        for s in range(slots):
            piece = part[:, s * width : (s + 1) * width]
            if added is not None:
                piece += added[first + s]
            for out_ref in out_refs:
                out_ref[first + s] = piece.astype(out_ref.dtype)
        first += slots


def extras(refs, tgt_rows):
    rows = tgt_rows + EXTRA
    for ref in refs:
        for s in range(ref.shape[0] // rows):
            yield ref[pl.ds(s * rows + tgt_rows, EXTRA), :].astype(F32)


def sums_body(*refs, parts, tgt_rows):
    *refs, out_ref = refs
    each = (out_ref.shape[0] - 8) // 2
    for place in range(2):
        total = sum(ref[...] for ref in refs[place * parts : (place + 1) * parts])
        row = jnp.sum(total.T, axis=0, keepdims=True)
        for i in range(each):
            out_ref[pl.ds(place * each + i, 1), :] = row[:, i * LANES : (i + 1) * LANES]
    counts = jnp.zeros((EXTRA, LANES), F32)
    labels = jnp.zeros((LANES, tgt_rows), F32)
    for extra in extras(refs[2 * parts :], tgt_rows):
        counts += extra[:, LANES:]
        labels += hot(extra[:1, :LANES].astype(jnp.int32), LANES)
    out_ref[pl.ds(2 * each, 8), :] = counts[:8] + counts[1:9]
    out_ref[pl.ds(2 * each + 1, 1), :] = jnp.sum(labels.T, axis=0, keepdims=True)


def count_of(place, mine_ref, got_ref):
    row = mine_ref.shape[0] - 8 + place
    count = mine_ref[pl.ds(row, 1), :] + got_ref[pl.ds(row, 1), :]
    return jnp.broadcast_to(count, (LANES, LANES)).T[:CLASSES, :1]


def first_body(own_weight, other_weight, mine_ref, got_ref, *refs, candidates):
    *kernels, own_marg, other_marg, column_ref, sent_ref = refs
    parts = len(kernels) // 2
    each = (mine_ref.shape[0] - 8) // 2
    total = candidates + 3.0 * count_of(0, mine_ref, got_ref)
    for place, (weight_ref, marg_ref) in enumerate(
        ((own_weight, own_marg), (other_weight, other_marg))
    ):
        rows = [
            mine_ref[pl.ds(place * each + i, 1), :] + got_ref[pl.ds((1 - place) * each + i, 1), :]
            for i in range(each)
        ]
        marg = weight_ref[...] / total
        marg_ref[...] = marg
        scale_ub = (marg / jnp.concatenate(rows, axis=1)).astype(BF16)
        if place == 0:
            put_column(scale_ub, kernels[:parts], None, (column_ref,))
        else:
            put_column(scale_ub, kernels[parts:], column_ref, (column_ref, sent_ref))


def target_body(mine_ref, got_ref, *refs, targets):
    *held_refs, marg_ref = refs
    total = targets + 3.0 * count_of(1, mine_ref, got_ref)
    for s, extra in enumerate(extras(held_refs, marg_ref.shape[2])):
        marg_ref[s] = (1.0 + 3.0 * hot(extra[:1, :LANES].astype(jnp.int32))) / total


def image_body(scale_ref, *refs):
    refs[-1][...] = image_of(refs[:-1], scale_ref)


def own_body(image_ref, got_ref, marg_ref, *refs, parts):
    kernels, (column_ref, *out_refs) = refs[:parts], refs[parts:]
    scale_u = marg_ref[...] / (image_ref[...] + got_ref[...])
    for out_ref in out_refs:
        out_ref[...] = scale_u
    put_column(scale_u.astype(BF16), kernels, None, (column_ref,))


def other_body(image_ref, got_ref, marg_ref, added_ref, *refs):
    *kernels, column_ref, sent_ref = refs
    scale_u = marg_ref[...] / (image_ref[...] + got_ref[...])
    put_column(scale_u.astype(BF16), kernels, added_ref, (column_ref, sent_ref))


def last_body(image_ref, got_ref, u_ref, scale_v_ref, mass_ref, own_ref, *, candidates):
    own_ref[...] = scale_v_ref[0]
    mass_ref[...] = candidates * u_ref[...] * (image_ref[...] + got_ref[...])


def slot_of(slot, flips, slots):
    top = slots.bit_length()
    found = []
    for kind, flip in enumerate(flips):
        turned = sum(1 << i for i, bit in enumerate(slot_bits(kind, top)) if flip >> bit & 1)
        found.append(slot ^ turned)
    if found[0] == found[1]:
        return found[0]
    return found[0] + parity(lax.axis_index("row"), top) * (found[1] - found[0])


def total_of(slot, own_ref, got_refs, flips):
    total = own_ref[slot]
    for pair, got_ref in zip(flips, got_refs):
        total += got_ref[slot_of(slot, pair, own_ref.shape[0])].astype(F32)
    return total


def sum_body(own_ref, *refs, flips):
    *got_refs, total_ref, sent_ref = refs
    for slot in range(own_ref.shape[0]):
        total = total_of(slot, own_ref, got_refs, flips)
        total_ref[slot] = total
        sent_ref[slot] = total.astype(BF16)


def scale_body(own_ref, marg_ref, *refs, flips):
    got_refs, outs = refs[: len(flips)], refs[len(flips) :]
    for slot in range(own_ref.shape[0]):
        scale_v = marg_ref[slot] / total_of(slot, own_ref, got_refs, flips)
        for out_ref in outs:
            out_ref[slot] = scale_v.astype(out_ref.dtype)


def shards(cand_embed, cand_labels, tgt_embed, tgt_labels):
    devices = lax.axis_size("row")
    top = devices.bit_length() - 1
    slots = devices // 2
    cand_rows, width = cand_embed.shape
    tgt_rows = tgt_embed.shape[0]
    label_rows = cand_labels.reshape(cand_rows // LANES, LANES)
    cand_labels = cand_labels.reshape(1, cand_rows)
    block = (slots, CLASSES, tgt_rows)
    image_type = ((CLASSES, cand_rows), F32)
    half_flops = 2 * cand_rows * slots * tgt_rows * 128

    def fill(held):
        columns = held.shape[0] // (tgt_rows + EXTRA) * tgt_rows
        return call(
            functools.partial(fill_body, tgt_rows=tgt_rows),
            [((cand_rows, columns), BF16)] * 2 + [((cand_rows, LANES), F32)] * 2,
            cand_unit, other_unit, held, flops=8 * 2 * cand_rows * columns * 128,
        )

    held = piece = pack(tgt_embed, tgt_labels.reshape(1, tgt_rows), cand_labels)
    across = []
    stages = list(zip(slot_bits(0, top), slot_bits(1, top)))[:-1]
    for place, bits in enumerate(stages):
        turned = exchange(held, *[1 << bit for bit in bits])
        across.append(exchange(piece, 2))
        if place == len(stages) - 1:
            (cand_unit,) = call(unit_body, [(cand_embed.shape, BF16)], cand_embed)
            other_unit, other_labels = swap(cand_unit), swap(label_rows)
            weight = 1.0 + 3.0 * hot(cand_labels)
            turned, across, weight = lax.optimization_barrier((turned, across, weight))
        else:
            turned, across, cand_embed, cand_labels, label_rows = lax.optimization_barrier(
                (turned, across, cand_embed, cand_labels, label_rows)
            )
        piece = turned
        held = jnp.concatenate([held, piece])
    later = exchange(piece, 2)
    other_weight = 1.0 + 3.0 * hot(other_labels.reshape(1, cand_rows))
    near = [held, jnp.concatenate(across)]
    filled = [fill(part) for part in near]
    later, filled, other_weight = lax.optimization_barrier((later, filled, other_weight))
    near.append(later)
    filled.append(fill(later))
    own_kernels, other_kernels, own_sums, other_sums = zip(*filled)

    (mine,) = call(
        functools.partial(sums_body, parts=len(near), tgt_rows=tgt_rows),
        [((2 * cand_rows // LANES + 8, LANES), F32)], *own_sums, *other_sums, *near,
    )
    got = swap(mine)
    own_marg, other_marg, column, sent = call(
        functools.partial(first_body, candidates=float(cand_rows * devices)),
        [image_type, image_type, (block, F32), (block, BF16)],
        weight, other_weight, mine, got, *own_kernels, *other_kernels, flops=2 * half_flops,
    )
    (tgt_marg,) = call(
        functools.partial(target_body, targets=float(tgt_rows * devices)),
        [(block, F32)], mine, got, *near,
    )
    for step in range(ITERS):
        last = step == ITERS - 1
        if step:
            column, *scale_u = call(
                functools.partial(own_body, parts=len(near)),
                [(block, F32)] + [image_type] * last,
                own_image, own_got, own_marg, *own_kernels, flops=half_flops,
            )
            column, sent = call(
                other_body, [(block, F32), (block, BF16)],
                other_image, other_got, other_marg, column, *other_kernels, flops=half_flops,
            )
        order = list(zip(rounds(0, top), rounds(1, top)))
        for place, pair in enumerate(order):
            flips = list(zip(*[flips_of(bits) for bits in pair]))
            found = [exchange(sent, *turn) for turn in flips]
            if place < len(order) - 1:
                column, sent = call(
                    functools.partial(sum_body, flips=flips),
                    [(block, F32), (block, BF16)], column, *found,
                )
        if last:
            potential = ENTROPY_TEMP * jnp.log(scale_u[0])
            found, potential = lax.optimization_barrier((found, potential))
        scale_vb, *scale_v = call(
            functools.partial(scale_body, flips=flips),
            [(block, BF16)] + [(block, F32)] * last,
            column, tgt_marg, *found,
        )
        (other_image,) = call(
            image_body, [image_type], scale_vb, *other_kernels, flops=half_flops
        )
        own_got = swap(other_image)
        (own_image,) = call(image_body, [image_type], scale_vb, *own_kernels, flops=half_flops)
        if not last:
            other_got = swap(own_image)
    space = pl.BlockSpec(memory_space=pltpu.VMEM)
    args = [own_image, own_got, *scale_u, *scale_v]
    mass, tgt_scaling = pl.pallas_call(
        functools.partial(last_body, candidates=float(cand_rows * devices)),
        out_shape=[
            jax.ShapeDtypeStruct(*image_type), jax.ShapeDtypeStruct((CLASSES, tgt_rows), F32)
        ],
        in_specs=[space] * len(args),
        out_specs=[space] * 2,
        compiler_params=pltpu.CompilerParams(vmem_limit_bytes=12 * 1024 * 1024),
    )(*[pltpu.with_memory_space_constraint(a, pltpu.VMEM) for a in args])
    return (potential, tgt_scaling, mass)


def solution(mesh):
    return jax.shard_map(
        shards,
        mesh=mesh,
        in_specs=(
            P(("grp", "row"), None),
            P(("grp", "row")),
            P(("grp", "row"), None),
            P(("grp", "row")),
        ),
        out_specs=(P(None, ("grp", "row")), P(None, ("grp", "row")), P(None, ("grp", "row"))),
        check_vma=False,
    )
```

```python
import functools
import math

import jax
import jax.numpy as jnp
from jax import lax
from jax.experimental import pallas as pl
from jax.experimental.pallas import tpu as pltpu
from jax.sharding import PartitionSpec as P

CLASSES = 32
ITERS = 3
INVERSE_TEMP = 20.0
ENTROPY_TEMP = 0.05
LANES = 128
EXTRA = 16
TILE = 256
F32 = jnp.float32
BF16 = jnp.bfloat16


def parity(index, top):
    return sum(index // (1 << bit) % 2 for bit in range(top)) % 2


def slot_bits(kind, top):
    layer = list(range(2, top))
    return (layer if kind else layer[::-1]) + [1]


def rounds(kind, top):
    bits = list(range(1, top))
    bits = bits[1 - kind :] + bits[: 1 - kind]
    return [bits[low : low + 2] for low in range(0, len(bits), 2)]


def flips_of(bits):
    flips = [0]
    for bit in bits:
        flips += [flip | 1 << bit for flip in flips]
    return flips[1:]


def exchange(block, *flips):
    devices = lax.axis_size("row")
    top = devices.bit_length() - 1
    pairs = []
    for d in range(devices):
        flip = flips[parity(d, top) % len(flips)]
        pairs.append((d, d ^ flip ^ parity(flip, top)))
    return lax.ppermute(block, "row", pairs)


def swap(block):
    devices = lax.axis_size("row")
    return lax.ppermute(block, "row", [(d, d ^ 1) for d in range(devices)])


def call(body, outs, *args, flops=0):
    space = pl.BlockSpec(memory_space=pltpu.VMEM)
    moved = sum(a.size * a.dtype.itemsize for a in args)
    return pl.pallas_call(
        body,
        out_shape=[pltpu.VMEM(shape, dtype) for shape, dtype in outs],
        in_specs=[space] * len(args),
        out_specs=[space] * len(outs),
        compiler_params=pltpu.CompilerParams(vmem_limit_bytes=12 * 1024 * 1024),
        cost_estimate=pl.CostEstimate(flops=flops, bytes_accessed=moved, transcendentals=0),
    )(*[pltpu.with_memory_space_constraint(a, pltpu.VMEM) for a in args])


def unit_rows(values):
    widened = values.astype(F32)
    meansq = jnp.mean(widened * widened, axis=1, keepdims=True)
    return (widened * lax.rsqrt(meansq + 1e-06) / math.sqrt(values.shape[1])).astype(BF16)


def hot(labels, classes=CLASSES):
    rows = lax.broadcasted_iota(jnp.int32, (classes, labels.shape[1]), 0)
    return (labels == rows).astype(F32)


def pack_body(embed_hbm, tgt_hbm, cand_hbm, out_ref, tgt_ref, cand_ref, sems):
    rows = embed_hbm.shape[0]
    copies = [
        pltpu.make_async_copy(cand_hbm, cand_ref, sems.at[0]),
        pltpu.make_async_copy(tgt_hbm, tgt_ref, sems.at[1]),
        pltpu.make_async_copy(embed_hbm, out_ref.at[pl.ds(0, rows)], sems.at[2]),
    ]
    for copy in copies:
        copy.start()
    copies[0].wait()
    counts = lax.dot_general(
        jnp.ones((EXTRA, cand_ref.shape[1]), BF16),
        hot(cand_ref[...]).astype(BF16),
        (((1,), (1,)), ((), ())),
        preferred_element_type=F32,
    )
    high = counts.astype(BF16).astype(F32)
    even = lax.broadcasted_iota(jnp.int32, counts.shape, 0) % 2 == 0
    out_ref[rows:, LANES:] = jnp.zeros((EXTRA, LANES), BF16)
    out_ref[rows:, LANES : LANES + CLASSES] = jnp.where(even, high, counts - high).astype(BF16)
    copies[1].wait()
    out_ref[rows:, :LANES] = jnp.broadcast_to(
        tgt_ref[...].astype(F32), (EXTRA, LANES)
    ).astype(BF16)
    copies[2].wait()


def pack(tgt_embed, tgt_labels, cand_labels):
    rows, width = tgt_embed.shape
    anywhere = pl.BlockSpec(memory_space=pl.ANY)
    return pl.pallas_call(
        pack_body,
        out_shape=pltpu.VMEM((rows + EXTRA, width), BF16),
        in_specs=[anywhere] * 3,
        out_specs=pl.BlockSpec(memory_space=pltpu.VMEM),
        scratch_shapes=[
            pltpu.VMEM(tgt_labels.shape, jnp.int32),
            pltpu.VMEM(cand_labels.shape, jnp.int32),
            pltpu.SemaphoreType.DMA((3,)),
        ],
        compiler_params=pltpu.CompilerParams(vmem_limit_bytes=12 * 1024 * 1024),
    )(*[
        pltpu.with_memory_space_constraint(a, pltpu.HBM)
        for a in (tgt_embed, tgt_labels, cand_labels)
    ])


def fill_body(own_ref, other_ref, held_ref, *out_refs, tgt_rows):
    rows = tgt_rows + EXTRA
    columns = out_refs[0].shape[1]
    per = min(TILE, columns) // tgt_rows
    tile = per * tgt_rows
    for col in range(0, columns, tile):
        first = col // tgt_rows
        block = jnp.concatenate(
            [held_ref[pl.ds((first + s) * rows, tgt_rows), :] for s in range(per)]
        )
        tgt_unit = unit_rows(block)
        for cand_ref, kernel_ref, sums_ref in zip((own_ref, other_ref), out_refs, out_refs[2:]):
            for row in range(0, cand_ref.shape[0], TILE):
                scores = lax.dot_general(
                    cand_ref[row : row + TILE, :],
                    tgt_unit,
                    (((1,), (1,)), ((), ())),
                    preferred_element_type=F32,
                )
                found = jnp.exp(INVERSE_TEMP * scores)
                kernel_ref[row : row + TILE, col : col + tile] = found.astype(BF16)
                sums = found[:, :LANES]
                for lane in range(LANES, tile, LANES):
                    sums += found[:, lane : lane + LANES]
                if col:
                    sums += sums_ref[row : row + TILE, :]
                sums_ref[row : row + TILE, :] = sums


def put_column(scale_ub, kernels, added, out_refs):
    width = out_refs[0].shape[2]
    first = 0
    for kernel_ref in kernels:
        part = jnp.dot(scale_ub, kernel_ref[...], preferred_element_type=F32)
        slots = kernel_ref.shape[1] // width
        for s in range(slots):
            piece = part[:, s * width : (s + 1) * width]
            if added is not None:
                piece += added[first + s]
            for out_ref in out_refs:
                out_ref[first + s] = piece.astype(out_ref.dtype)
        first += slots


def extras(refs, tgt_rows):
    rows = tgt_rows + EXTRA
    for ref in refs:
        for s in range(ref.shape[0] // rows):
            yield ref[pl.ds(s * rows + tgt_rows, EXTRA), :].astype(F32)


def sums_body(*refs, parts, tgt_rows):
    *refs, out_ref = refs
    each = (out_ref.shape[0] - 8) // 2
    for place in range(2):
        total = sum(ref[...] for ref in refs[place * parts : (place + 1) * parts])
        row = jnp.sum(total.T, axis=0, keepdims=True)
        for i in range(each):
            out_ref[pl.ds(place * each + i, 1), :] = row[:, i * LANES : (i + 1) * LANES]
    counts = jnp.zeros((EXTRA, LANES), F32)
    labels = jnp.zeros((LANES, tgt_rows), F32)
    for extra in extras(refs[2 * parts :], tgt_rows):
        counts += extra[:, LANES:]
        labels += hot(extra[:1, :LANES].astype(jnp.int32), LANES)
    out_ref[pl.ds(2 * each, 8), :] = counts[:8] + counts[1:9]
    out_ref[pl.ds(2 * each + 1, 1), :] = jnp.sum(labels.T, axis=0, keepdims=True)


def count_of(place, mine_ref, got_ref):
    row = mine_ref.shape[0] - 8 + place
    count = mine_ref[pl.ds(row, 1), :] + got_ref[pl.ds(row, 1), :]
    return jnp.broadcast_to(count, (LANES, LANES)).T[:CLASSES, :1]


def first_body(own_weight, other_weight, mine_ref, got_ref, *refs, candidates):
    *kernels, own_marg, other_marg, column_ref, sent_ref = refs
    parts = len(kernels) // 2
    each = (mine_ref.shape[0] - 8) // 2
    total = candidates + 3.0 * count_of(0, mine_ref, got_ref)
    for place, (weight_ref, marg_ref) in enumerate(
        ((own_weight, own_marg), (other_weight, other_marg))
    ):
        rows = [
            mine_ref[pl.ds(place * each + i, 1), :] + got_ref[pl.ds((1 - place) * each + i, 1), :]
            for i in range(each)
        ]
        marg = weight_ref[...] / total
        marg_ref[...] = marg
        scale_ub = (marg / jnp.concatenate(rows, axis=1)).astype(BF16)
        if place == 0:
            put_column(scale_ub, kernels[:parts], None, (column_ref,))
        else:
            put_column(scale_ub, kernels[parts:], column_ref, (column_ref, sent_ref))


def target_body(mine_ref, got_ref, *refs, targets):
    *held_refs, marg_ref = refs
    total = targets + 3.0 * count_of(1, mine_ref, got_ref)
    for s, extra in enumerate(extras(held_refs, marg_ref.shape[2])):
        marg_ref[s] = (1.0 + 3.0 * hot(extra[:1, :LANES].astype(jnp.int32))) / total


def image_body(scale_ref, *refs):
    *kernels, image_ref = refs
    step = min(512, image_ref.shape[1])
    for row in range(0, image_ref.shape[1], step):
        image = 0.0
        first = 0
        for kernel_ref in kernels:
            slots = kernel_ref.shape[1] // scale_ref.shape[2]
            scale_v = jnp.concatenate([scale_ref[s] for s in range(first, first + slots)], axis=1)
            image += lax.dot_general(
                kernel_ref[row : row + step, :],
                scale_v,
                (((1,), (1,)), ((), ())),
                preferred_element_type=F32,
            )
            first += slots
        image_ref[:, row : row + step] = image.T


def own_body(image_ref, got_ref, marg_ref, *refs, parts):
    kernels, (column_ref, *out_refs) = refs[:parts], refs[parts:]
    scale_u = marg_ref[...] / (image_ref[...] + got_ref[...])
    for out_ref in out_refs:
        out_ref[...] = scale_u
    put_column(scale_u.astype(BF16), kernels, None, (column_ref,))


def other_body(image_ref, got_ref, marg_ref, added_ref, *refs):
    *kernels, column_ref, sent_ref = refs
    scale_u = marg_ref[...] / (image_ref[...] + got_ref[...])
    put_column(scale_u.astype(BF16), kernels, added_ref, (column_ref, sent_ref))


def last_body(image_ref, got_ref, u_ref, scale_v_ref, mass_ref, own_ref, *, candidates):
    own_ref[...] = scale_v_ref[0]
    mass_ref[...] = candidates * u_ref[...] * (image_ref[...] + got_ref[...])


def slot_of(slot, flips, slots):
    top = slots.bit_length()
    found = []
    for kind, flip in enumerate(flips):
        turned = sum(1 << i for i, bit in enumerate(slot_bits(kind, top)) if flip >> bit & 1)
        found.append(slot ^ turned)
    if found[0] == found[1]:
        return found[0]
    return found[0] + parity(lax.axis_index("row"), top) * (found[1] - found[0])


def total_of(slot, own_ref, got_refs, flips):
    total = own_ref[slot]
    for pair, got_ref in zip(flips, got_refs):
        total += got_ref[slot_of(slot, pair, own_ref.shape[0])].astype(F32)
    return total


def sum_body(own_ref, *refs, flips):
    *got_refs, total_ref, sent_ref = refs
    for slot in range(own_ref.shape[0]):
        total = total_of(slot, own_ref, got_refs, flips)
        total_ref[slot] = total
        sent_ref[slot] = total.astype(BF16)


def scale_body(own_ref, marg_ref, *refs, flips):
    got_refs, outs = refs[: len(flips)], refs[len(flips) :]
    for slot in range(own_ref.shape[0]):
        scale_v = marg_ref[slot] / total_of(slot, own_ref, got_refs, flips)
        for out_ref in outs:
            out_ref[slot] = scale_v.astype(out_ref.dtype)


def shards(cand_embed, cand_labels, tgt_embed, tgt_labels):
    devices = lax.axis_size("row")
    top = devices.bit_length() - 1
    slots = devices // 2
    cand_rows, width = cand_embed.shape
    tgt_rows = tgt_embed.shape[0]
    label_rows = cand_labels.reshape(cand_rows // LANES, LANES)
    cand_labels = cand_labels.reshape(1, cand_rows)
    block = (slots, CLASSES, tgt_rows)
    image_type = ((CLASSES, cand_rows), F32)
    half_flops = 2 * cand_rows * slots * tgt_rows * 128

    def fill(held):
        columns = held.shape[0] // (tgt_rows + EXTRA) * tgt_rows
        return call(
            functools.partial(fill_body, tgt_rows=tgt_rows),
            [((cand_rows, columns), BF16)] * 2 + [((cand_rows, LANES), F32)] * 2,
            cand_unit, other_unit, held, flops=8 * 2 * cand_rows * columns * 128,
        )

    held = piece = pack(tgt_embed, tgt_labels.reshape(1, tgt_rows), cand_labels)
    cand_unit = unit_rows(cand_embed)
    weight = 1.0 + 3.0 * hot(cand_labels)
    across = []
    other_unit = None
    for bits in list(zip(slot_bits(0, top), slot_bits(1, top)))[:-1]:
        turned = exchange(held, *[1 << bit for bit in bits])
        across.append(exchange(piece, 2))
        piece, across, cand_unit, weight, other_unit = lax.optimization_barrier(
            (turned, across, cand_unit, weight, other_unit)
        )
        held = jnp.concatenate([held, piece])
        if other_unit is None:
            other_unit = swap(cand_unit), swap(label_rows)
    later = exchange(piece, 2)
    other_unit, other_labels = other_unit
    other_weight = 1.0 + 3.0 * hot(other_labels.reshape(1, cand_rows))
    near = [held, jnp.concatenate(across)]
    filled = [fill(part) for part in near]
    later, filled, other_weight = lax.optimization_barrier((later, filled, other_weight))
    near.append(later)
    filled.append(fill(later))
    own_kernels, other_kernels, own_sums, other_sums = zip(*filled)

    (mine,) = call(
        functools.partial(sums_body, parts=len(near), tgt_rows=tgt_rows),
        [((2 * cand_rows // LANES + 8, LANES), F32)], *own_sums, *other_sums, *near,
    )
    got = swap(mine)
    own_marg, other_marg, column, sent = call(
        functools.partial(first_body, candidates=float(cand_rows * devices)),
        [image_type, image_type, (block, F32), (block, BF16)],
        weight, other_weight, mine, got, *own_kernels, *other_kernels, flops=2 * half_flops,
    )
    (tgt_marg,) = call(
        functools.partial(target_body, targets=float(tgt_rows * devices)),
        [(block, F32)], mine, got, *near,
    )
    for step in range(ITERS):
        last = step == ITERS - 1
        if step:
            column, *scale_u = call(
                functools.partial(own_body, parts=len(near)),
                [(block, F32)] + [image_type] * last,
                own_image, own_got, own_marg, *own_kernels, flops=half_flops,
            )
            column, sent = call(
                other_body, [(block, F32), (block, BF16)],
                other_image, other_got, other_marg, column, *other_kernels, flops=half_flops,
            )
        order = list(zip(rounds(0, top), rounds(1, top)))
        for place, pair in enumerate(order):
            flips = list(zip(*[flips_of(bits) for bits in pair]))
            found = [exchange(sent, *turn) for turn in flips]
            if place < len(order) - 1:
                column, sent = call(
                    functools.partial(sum_body, flips=flips),
                    [(block, F32), (block, BF16)], column, *found,
                )
        if last:
            potential = ENTROPY_TEMP * jnp.log(scale_u[0])
            found, potential = lax.optimization_barrier((found, potential))
        scale_vb, *scale_v = call(
            functools.partial(scale_body, flips=flips),
            [(block, BF16)] + [(block, F32)] * last,
            column, tgt_marg, *found,
        )
        (other_image,) = call(
            image_body, [image_type], scale_vb, *other_kernels, flops=half_flops
        )
        own_got = swap(other_image)
        (own_image,) = call(image_body, [image_type], scale_vb, *own_kernels, flops=half_flops)
        if not last:
            other_got = swap(own_image)
    space = pl.BlockSpec(memory_space=pltpu.VMEM)
    args = [own_image, own_got, *scale_u, *scale_v]
    mass, tgt_scaling = pl.pallas_call(
        functools.partial(last_body, candidates=float(cand_rows * devices)),
        out_shape=[
            jax.ShapeDtypeStruct(*image_type), jax.ShapeDtypeStruct((CLASSES, tgt_rows), F32)
        ],
        in_specs=[space] * len(args),
        out_specs=[space] * 2,
        compiler_params=pltpu.CompilerParams(vmem_limit_bytes=12 * 1024 * 1024),
    )(*[pltpu.with_memory_space_constraint(a, pltpu.VMEM) for a in args])
    return (potential, tgt_scaling, mass)


def solution(mesh):
    return jax.shard_map(
        shards,
        mesh=mesh,
        in_specs=(
            P(("grp", "row"), None),
            P(("grp", "row")),
            P(("grp", "row"), None),
            P(("grp", "row")),
        ),
        out_specs=(P(None, ("grp", "row")), P(None, ("grp", "row")), P(None, ("grp", "row"))),
        check_vma=False,
    )
```

```python
import functools
import math

import jax
import jax.numpy as jnp
from jax import lax
from jax.experimental import pallas as pl
from jax.experimental.pallas import tpu as pltpu
from jax.sharding import PartitionSpec as P

CLASSES = 32
ITERS = 3
INVERSE_TEMP = 20.0
ENTROPY_TEMP = 0.05
LANES = 128
EXTRA = 16
TILE = 256
F32 = jnp.float32
BF16 = jnp.bfloat16


def parity(index, top):
    return sum(index // (1 << bit) % 2 for bit in range(top)) % 2


def slot_bits(kind, top):
    layer = list(range(2, top))
    return (layer if kind else layer[::-1]) + [1]


def rounds(kind, top):
    bits = list(range(1, top))
    bits = bits[1 - kind :] + bits[: 1 - kind]
    return [bits[low : low + 2] for low in range(0, len(bits), 2)]


def flips_of(bits):
    flips = [0]
    for bit in bits:
        flips += [flip | 1 << bit for flip in flips]
    return flips[1:]


def exchange(block, *flips):
    devices = lax.axis_size("row")
    top = devices.bit_length() - 1
    pairs = []
    for d in range(devices):
        flip = flips[parity(d, top) % len(flips)]
        pairs.append((d, d ^ flip ^ parity(flip, top)))
    return lax.ppermute(block, "row", pairs)


def swap(block):
    devices = lax.axis_size("row")
    return lax.ppermute(block, "row", [(d, d ^ 1) for d in range(devices)])


def call(body, outs, *args, flops=0):
    space = pl.BlockSpec(memory_space=pltpu.VMEM)
    moved = sum(a.size * a.dtype.itemsize for a in args)
    return pl.pallas_call(
        body,
        out_shape=[pltpu.VMEM(shape, dtype) for shape, dtype in outs],
        in_specs=[space] * len(args),
        out_specs=[space] * len(outs),
        compiler_params=pltpu.CompilerParams(vmem_limit_bytes=12 * 1024 * 1024),
        cost_estimate=pl.CostEstimate(flops=flops, bytes_accessed=moved, transcendentals=0),
    )(*[pltpu.with_memory_space_constraint(a, pltpu.VMEM) for a in args])


def unit_rows(values):
    widened = values.astype(F32)
    meansq = jnp.mean(widened * widened, axis=1, keepdims=True)
    return (widened * lax.rsqrt(meansq + 1e-06) / math.sqrt(values.shape[1])).astype(BF16)


def hot(labels, classes=CLASSES):
    rows = lax.broadcasted_iota(jnp.int32, (classes, labels.shape[1]), 0)
    return (labels == rows).astype(F32)


def pack_body(embed_hbm, tgt_hbm, cand_hbm, out_ref, tgt_ref, cand_ref, sems):
    rows = embed_hbm.shape[0]
    copies = [
        pltpu.make_async_copy(cand_hbm, cand_ref, sems.at[0]),
        pltpu.make_async_copy(tgt_hbm, tgt_ref, sems.at[1]),
        pltpu.make_async_copy(embed_hbm, out_ref.at[pl.ds(0, rows)], sems.at[2]),
    ]
    for copy in copies:
        copy.start()
    copies[0].wait()
    counts = lax.dot_general(
        jnp.ones((EXTRA, cand_ref.shape[1]), BF16),
        hot(cand_ref[...]).astype(BF16),
        (((1,), (1,)), ((), ())),
        preferred_element_type=F32,
    )
    high = counts.astype(BF16).astype(F32)
    even = lax.broadcasted_iota(jnp.int32, counts.shape, 0) % 2 == 0
    out_ref[rows:, LANES:] = jnp.zeros((EXTRA, LANES), BF16)
    out_ref[rows:, LANES : LANES + CLASSES] = jnp.where(even, high, counts - high).astype(BF16)
    copies[1].wait()
    out_ref[rows:, :LANES] = jnp.broadcast_to(
        tgt_ref[...].astype(F32), (EXTRA, LANES)
    ).astype(BF16)
    copies[2].wait()


def pack(tgt_embed, tgt_labels, cand_labels):
    rows, width = tgt_embed.shape
    anywhere = pl.BlockSpec(memory_space=pl.ANY)
    return pl.pallas_call(
        pack_body,
        out_shape=pltpu.VMEM((rows + EXTRA, width), BF16),
        in_specs=[anywhere] * 3,
        out_specs=pl.BlockSpec(memory_space=pltpu.VMEM),
        scratch_shapes=[
            pltpu.VMEM(tgt_labels.shape, jnp.int32),
            pltpu.VMEM(cand_labels.shape, jnp.int32),
            pltpu.SemaphoreType.DMA((3,)),
        ],
        compiler_params=pltpu.CompilerParams(vmem_limit_bytes=12 * 1024 * 1024),
    )(*[
        pltpu.with_memory_space_constraint(a, pltpu.HBM)
        for a in (tgt_embed, tgt_labels, cand_labels)
    ])


def fill_body(own_ref, other_ref, held_ref, *out_refs, tgt_rows):
    rows = tgt_rows + EXTRA
    columns = out_refs[0].shape[1]
    per = min(TILE, columns) // tgt_rows
    tile = per * tgt_rows
    for col in range(0, columns, tile):
        first = col // tgt_rows
        block = jnp.concatenate(
            [held_ref[pl.ds((first + s) * rows, tgt_rows), :] for s in range(per)]
        )
        tgt_unit = unit_rows(block)
        for cand_ref, kernel_ref, sums_ref in zip((own_ref, other_ref), out_refs, out_refs[2:]):
            for row in range(0, cand_ref.shape[0], TILE):
                scores = lax.dot_general(
                    cand_ref[row : row + TILE, :],
                    tgt_unit,
                    (((1,), (1,)), ((), ())),
                    preferred_element_type=F32,
                )
                found = jnp.exp(INVERSE_TEMP * scores)
                kernel_ref[row : row + TILE, col : col + tile] = found.astype(BF16)
                sums = found[:, :LANES]
                for lane in range(LANES, tile, LANES):
                    sums += found[:, lane : lane + LANES]
                if col:
                    sums += sums_ref[row : row + TILE, :]
                sums_ref[row : row + TILE, :] = sums


def turned_body(own_ref, other_ref, held_ref, *out_refs, tgt_rows):
    rows = tgt_rows + EXTRA
    for s in range(held_ref.shape[0] // rows):
        tgt_unit = unit_rows(held_ref[pl.ds(s * rows, tgt_rows), :])
        for cand_ref, out_ref in zip((own_ref, other_ref), out_refs):
            for row in range(0, cand_ref.shape[0], TILE):
                scores = lax.dot_general(
                    tgt_unit,
                    cand_ref[row : row + TILE, :],
                    (((1,), (1,)), ((), ())),
                    preferred_element_type=F32,
                )
                out_ref[s * tgt_rows : (s + 1) * tgt_rows, row : row + TILE] = jnp.exp(
                    INVERSE_TEMP * scores
                ).astype(BF16)


def put_column(scale_ub, kernels, added, out_refs):
    width = out_refs[0].shape[2]
    first = 0
    for kernel_ref in kernels:
        part = jnp.dot(scale_ub, kernel_ref[...], preferred_element_type=F32)
        slots = kernel_ref.shape[1] // width
        for s in range(slots):
            piece = part[:, s * width : (s + 1) * width]
            if added is not None:
                piece += added[first + s]
            for out_ref in out_refs:
                out_ref[first + s] = piece.astype(out_ref.dtype)
        first += slots


def extras(refs, tgt_rows):
    rows = tgt_rows + EXTRA
    for ref in refs:
        for s in range(ref.shape[0] // rows):
            yield ref[pl.ds(s * rows + tgt_rows, EXTRA), :].astype(F32)


def sums_body(*refs, parts, tgt_rows):
    *refs, out_ref = refs
    each = (out_ref.shape[0] - 8) // 2
    for place in range(2):
        total = sum(ref[...] for ref in refs[place * parts : (place + 1) * parts])
        row = jnp.sum(total.T, axis=0, keepdims=True)
        for i in range(each):
            out_ref[pl.ds(place * each + i, 1), :] = row[:, i * LANES : (i + 1) * LANES]
    counts = jnp.zeros((EXTRA, LANES), F32)
    labels = jnp.zeros((LANES, tgt_rows), F32)
    for extra in extras(refs[2 * parts :], tgt_rows):
        counts += extra[:, LANES:]
        labels += hot(extra[:1, :LANES].astype(jnp.int32), LANES)
    out_ref[pl.ds(2 * each, 8), :] = counts[:8] + counts[1:9]
    out_ref[pl.ds(2 * each + 1, 1), :] = jnp.sum(labels.T, axis=0, keepdims=True)


def count_of(place, mine_ref, got_ref):
    row = mine_ref.shape[0] - 8 + place
    count = mine_ref[pl.ds(row, 1), :] + got_ref[pl.ds(row, 1), :]
    return jnp.broadcast_to(count, (LANES, LANES)).T[:CLASSES, :1]


def first_body(own_weight, other_weight, mine_ref, got_ref, *refs, candidates):
    *kernels, own_marg, other_marg, column_ref, sent_ref = refs
    parts = len(kernels) // 2
    each = (mine_ref.shape[0] - 8) // 2
    total = candidates + 3.0 * count_of(0, mine_ref, got_ref)
    for place, (weight_ref, marg_ref) in enumerate(
        ((own_weight, own_marg), (other_weight, other_marg))
    ):
        rows = [
            mine_ref[pl.ds(place * each + i, 1), :] + got_ref[pl.ds((1 - place) * each + i, 1), :]
            for i in range(each)
        ]
        marg = weight_ref[...] / total
        marg_ref[...] = marg
        scale_ub = (marg / jnp.concatenate(rows, axis=1)).astype(BF16)
        if place == 0:
            put_column(scale_ub, kernels[:parts], None, (column_ref,))
        else:
            put_column(scale_ub, kernels[parts:], column_ref, (column_ref, sent_ref))


def target_body(mine_ref, got_ref, *refs, targets):
    *held_refs, marg_ref = refs
    total = targets + 3.0 * count_of(1, mine_ref, got_ref)
    for s, extra in enumerate(extras(held_refs, marg_ref.shape[2])):
        marg_ref[s] = (1.0 + 3.0 * hot(extra[:1, :LANES].astype(jnp.int32))) / total


def image_body(scale_ref, *refs):
    *turned, image_ref = refs
    image = 0.0
    first = 0
    for turned_ref in turned:
        slots = turned_ref.shape[0] // scale_ref.shape[2]
        scale_v = jnp.concatenate([scale_ref[s] for s in range(first, first + slots)], axis=1)
        image += jnp.dot(scale_v, turned_ref[...], preferred_element_type=F32)
        first += slots
    image_ref[...] = image


def own_body(image_ref, got_ref, marg_ref, *refs, parts):
    kernels, (column_ref, *out_refs) = refs[:parts], refs[parts:]
    scale_u = marg_ref[...] / (image_ref[...] + got_ref[...])
    for out_ref in out_refs:
        out_ref[...] = scale_u
    put_column(scale_u.astype(BF16), kernels, None, (column_ref,))


def other_body(image_ref, got_ref, marg_ref, added_ref, *refs):
    *kernels, column_ref, sent_ref = refs
    scale_u = marg_ref[...] / (image_ref[...] + got_ref[...])
    put_column(scale_u.astype(BF16), kernels, added_ref, (column_ref, sent_ref))


def last_body(image_ref, got_ref, u_ref, scale_v_ref, mass_ref, own_ref, *, candidates):
    own_ref[...] = scale_v_ref[0]
    mass_ref[...] = candidates * u_ref[...] * (image_ref[...] + got_ref[...])


def slot_of(slot, flips, slots):
    top = slots.bit_length()
    found = []
    for kind, flip in enumerate(flips):
        turned = sum(1 << i for i, bit in enumerate(slot_bits(kind, top)) if flip >> bit & 1)
        found.append(slot ^ turned)
    if found[0] == found[1]:
        return found[0]
    return found[0] + parity(lax.axis_index("row"), top) * (found[1] - found[0])


def total_of(slot, own_ref, got_refs, flips):
    total = own_ref[slot]
    for pair, got_ref in zip(flips, got_refs):
        total += got_ref[slot_of(slot, pair, own_ref.shape[0])].astype(F32)
    return total


def sum_body(own_ref, *refs, flips):
    *got_refs, total_ref, sent_ref = refs
    for slot in range(own_ref.shape[0]):
        total = total_of(slot, own_ref, got_refs, flips)
        total_ref[slot] = total
        sent_ref[slot] = total.astype(BF16)


def scale_body(own_ref, marg_ref, *refs, flips):
    got_refs, outs = refs[: len(flips)], refs[len(flips) :]
    for slot in range(own_ref.shape[0]):
        scale_v = marg_ref[slot] / total_of(slot, own_ref, got_refs, flips)
        for out_ref in outs:
            out_ref[slot] = scale_v.astype(out_ref.dtype)


def shards(cand_embed, cand_labels, tgt_embed, tgt_labels):
    devices = lax.axis_size("row")
    top = devices.bit_length() - 1
    slots = devices // 2
    cand_rows, width = cand_embed.shape
    tgt_rows = tgt_embed.shape[0]
    label_rows = cand_labels.reshape(cand_rows // LANES, LANES)
    cand_labels = cand_labels.reshape(1, cand_rows)
    block = (slots, CLASSES, tgt_rows)
    image_type = ((CLASSES, cand_rows), F32)
    half_flops = 2 * cand_rows * slots * tgt_rows * 128

    def fill(held):
        columns = held.shape[0] // (tgt_rows + EXTRA) * tgt_rows
        return call(
            functools.partial(fill_body, tgt_rows=tgt_rows),
            [((cand_rows, columns), BF16)] * 2 + [((cand_rows, LANES), F32)] * 2,
            cand_unit, other_unit, held, flops=8 * 2 * cand_rows * columns * 128,
        )

    held = piece = pack(tgt_embed, tgt_labels.reshape(1, tgt_rows), cand_labels)
    cand_unit = unit_rows(cand_embed)
    weight = 1.0 + 3.0 * hot(cand_labels)
    across = []
    other_unit = None
    for bits in list(zip(slot_bits(0, top), slot_bits(1, top)))[:-1]:
        turned = exchange(held, *[1 << bit for bit in bits])
        across.append(exchange(piece, 2))
        piece, across, cand_unit, weight, other_unit = lax.optimization_barrier(
            (turned, across, cand_unit, weight, other_unit)
        )
        held = jnp.concatenate([held, piece])
        if other_unit is None:
            other_unit = swap(cand_unit), swap(label_rows)
    later = exchange(piece, 2)
    other_unit, other_labels = other_unit
    other_weight = 1.0 + 3.0 * hot(other_labels.reshape(1, cand_rows))
    near = [held, jnp.concatenate(across)]
    filled = [fill(part) for part in near]
    later, filled, other_weight = lax.optimization_barrier((later, filled, other_weight))
    near.append(later)
    filled.append(fill(later))
    own_kernels, other_kernels, own_sums, other_sums = zip(*filled)

    (mine,) = call(
        functools.partial(sums_body, parts=len(near), tgt_rows=tgt_rows),
        [((2 * cand_rows // LANES + 8, LANES), F32)], *own_sums, *other_sums, *near,
    )
    got = swap(mine)
    own_marg, other_marg, column, sent = call(
        functools.partial(first_body, candidates=float(cand_rows * devices)),
        [image_type, image_type, (block, F32), (block, BF16)],
        weight, other_weight, mine, got, *own_kernels, *other_kernels, flops=2 * half_flops,
    )
    sent, cand_unit, other_unit, near = lax.optimization_barrier(
        (sent, cand_unit, other_unit, near)
    )
    turned = []
    for part in near:
        columns = part.shape[0] // (tgt_rows + EXTRA) * tgt_rows
        turned.append(
            call(
                functools.partial(turned_body, tgt_rows=tgt_rows),
                [((columns, cand_rows), BF16)] * 2,
                cand_unit, other_unit, part, flops=8 * 2 * cand_rows * columns * 128,
            )
        )
    own_turned, other_turned = zip(*turned)
    (tgt_marg,) = call(
        functools.partial(target_body, targets=float(tgt_rows * devices)),
        [(block, F32)], mine, got, *near,
    )
    for step in range(ITERS):
        last = step == ITERS - 1
        if step:
            column, *scale_u = call(
                functools.partial(own_body, parts=len(near)),
                [(block, F32)] + [image_type] * last,
                own_image, own_got, own_marg, *own_kernels, flops=half_flops,
            )
            column, sent = call(
                other_body, [(block, F32), (block, BF16)],
                other_image, other_got, other_marg, column, *other_kernels, flops=half_flops,
            )
        order = list(zip(rounds(0, top), rounds(1, top)))
        for place, pair in enumerate(order):
            flips = list(zip(*[flips_of(bits) for bits in pair]))
            found = [exchange(sent, *turn) for turn in flips]
            if place < len(order) - 1:
                column, sent = call(
                    functools.partial(sum_body, flips=flips),
                    [(block, F32), (block, BF16)], column, *found,
                )
        if last:
            potential = ENTROPY_TEMP * jnp.log(scale_u[0])
            found, potential = lax.optimization_barrier((found, potential))
        scale_vb, *scale_v = call(
            functools.partial(scale_body, flips=flips),
            [(block, BF16)] + [(block, F32)] * last,
            column, tgt_marg, *found,
        )
        (other_image,) = call(
            image_body, [image_type], scale_vb, *other_turned, flops=half_flops
        )
        own_got = swap(other_image)
        (own_image,) = call(image_body, [image_type], scale_vb, *own_turned, flops=half_flops)
        if not last:
            other_got = swap(own_image)
    space = pl.BlockSpec(memory_space=pltpu.VMEM)
    args = [own_image, own_got, *scale_u, *scale_v]
    mass, tgt_scaling = pl.pallas_call(
        functools.partial(last_body, candidates=float(cand_rows * devices)),
        out_shape=[
            jax.ShapeDtypeStruct(*image_type), jax.ShapeDtypeStruct((CLASSES, tgt_rows), F32)
        ],
        in_specs=[space] * len(args),
        out_specs=[space] * 2,
        compiler_params=pltpu.CompilerParams(vmem_limit_bytes=12 * 1024 * 1024),
    )(*[pltpu.with_memory_space_constraint(a, pltpu.VMEM) for a in args])
    return (potential, tgt_scaling, mass)


def solution(mesh):
    return jax.shard_map(
        shards,
        mesh=mesh,
        in_specs=(
            P(("grp", "row"), None),
            P(("grp", "row")),
            P(("grp", "row"), None),
            P(("grp", "row")),
        ),
        out_specs=(P(None, ("grp", "row")), P(None, ("grp", "row")), P(None, ("grp", "row"))),
        check_vma=False,
    )
```

```python
import functools
import math

import jax
import jax.numpy as jnp
from jax import lax
from jax.experimental import pallas as pl
from jax.experimental.pallas import tpu as pltpu
from jax.sharding import PartitionSpec as P

CLASSES = 32
ITERS = 3
INVERSE_TEMP = 20.0
ENTROPY_TEMP = 0.05
LANES = 128
EXTRA = 16
TILE = 256
F32 = jnp.float32
BF16 = jnp.bfloat16


def parity(index, top):
    return sum(index // (1 << bit) % 2 for bit in range(top)) % 2


def slot_bits(kind, top):
    layer = list(range(2, top))
    return (layer if kind else layer[::-1]) + [1]


def rounds(kind, top):
    bits = list(range(1, top))
    bits = bits[1 - kind :] + bits[: 1 - kind]
    return [bits[low : low + 2] for low in range(0, len(bits), 2)]


def flips_of(bits):
    flips = [0]
    for bit in bits:
        flips += [flip | 1 << bit for flip in flips]
    return flips[1:]


def exchange(block, *flips):
    devices = lax.axis_size("row")
    top = devices.bit_length() - 1
    pairs = []
    for d in range(devices):
        flip = flips[parity(d, top) % len(flips)]
        pairs.append((d, d ^ flip ^ parity(flip, top)))
    return lax.ppermute(block, "row", pairs)


def swap(block):
    devices = lax.axis_size("row")
    return lax.ppermute(block, "row", [(d, d ^ 1) for d in range(devices)])


def call(body, outs, *args, flops=0):
    space = pl.BlockSpec(memory_space=pltpu.VMEM)
    moved = sum(a.size * a.dtype.itemsize for a in args)
    return pl.pallas_call(
        body,
        out_shape=[pltpu.VMEM(shape, dtype) for shape, dtype in outs],
        in_specs=[space] * len(args),
        out_specs=[space] * len(outs),
        compiler_params=pltpu.CompilerParams(vmem_limit_bytes=12 * 1024 * 1024),
        cost_estimate=pl.CostEstimate(flops=flops, bytes_accessed=moved, transcendentals=0),
    )(*[pltpu.with_memory_space_constraint(a, pltpu.VMEM) for a in args])


def unit_rows(values):
    widened = values.astype(F32)
    meansq = jnp.mean(widened * widened, axis=1, keepdims=True)
    return (widened * lax.rsqrt(meansq + 1e-06) / math.sqrt(values.shape[1])).astype(BF16)


def hot(labels, classes=CLASSES):
    rows = lax.broadcasted_iota(jnp.int32, (classes, labels.shape[1]), 0)
    return (labels == rows).astype(F32)


def pack_body(embed_hbm, tgt_hbm, cand_hbm, out_ref, tgt_ref, cand_ref, sems):
    rows = embed_hbm.shape[0]
    copies = [
        pltpu.make_async_copy(cand_hbm, cand_ref, sems.at[0]),
        pltpu.make_async_copy(tgt_hbm, tgt_ref, sems.at[1]),
        pltpu.make_async_copy(embed_hbm, out_ref.at[pl.ds(0, rows)], sems.at[2]),
    ]
    for copy in copies:
        copy.start()
    copies[0].wait()
    counts = lax.dot_general(
        jnp.ones((EXTRA, cand_ref.shape[1]), BF16),
        hot(cand_ref[...]).astype(BF16),
        (((1,), (1,)), ((), ())),
        preferred_element_type=F32,
    )
    high = counts.astype(BF16).astype(F32)
    even = lax.broadcasted_iota(jnp.int32, counts.shape, 0) % 2 == 0
    out_ref[rows:, LANES:] = jnp.zeros((EXTRA, LANES), BF16)
    out_ref[rows:, LANES : LANES + CLASSES] = jnp.where(even, high, counts - high).astype(BF16)
    copies[1].wait()
    out_ref[rows:, :LANES] = jnp.broadcast_to(
        tgt_ref[...].astype(F32), (EXTRA, LANES)
    ).astype(BF16)
    copies[2].wait()


def pack(tgt_embed, tgt_labels, cand_labels):
    rows, width = tgt_embed.shape
    anywhere = pl.BlockSpec(memory_space=pl.ANY)
    return pl.pallas_call(
        pack_body,
        out_shape=pltpu.VMEM((rows + EXTRA, width), BF16),
        in_specs=[anywhere] * 3,
        out_specs=pl.BlockSpec(memory_space=pltpu.VMEM),
        scratch_shapes=[
            pltpu.VMEM(tgt_labels.shape, jnp.int32),
            pltpu.VMEM(cand_labels.shape, jnp.int32),
            pltpu.SemaphoreType.DMA((3,)),
        ],
        compiler_params=pltpu.CompilerParams(vmem_limit_bytes=12 * 1024 * 1024),
    )(*[
        pltpu.with_memory_space_constraint(a, pltpu.HBM)
        for a in (tgt_embed, tgt_labels, cand_labels)
    ])


def fill_body(own_ref, other_ref, held_ref, *out_refs, tgt_rows):
    rows = tgt_rows + EXTRA
    columns = out_refs[0].shape[1]
    per = min(TILE, columns) // tgt_rows
    tile = per * tgt_rows
    for col in range(0, columns, tile):
        first = col // tgt_rows
        block = jnp.concatenate(
            [held_ref[pl.ds((first + s) * rows, tgt_rows), :] for s in range(per)]
        )
        tgt_unit = unit_rows(block)
        for cand_ref, kernel_ref, sums_ref in zip((own_ref, other_ref), out_refs, out_refs[2:]):
            for row in range(0, cand_ref.shape[0], TILE):
                scores = lax.dot_general(
                    cand_ref[row : row + TILE, :],
                    tgt_unit,
                    (((1,), (1,)), ((), ())),
                    preferred_element_type=F32,
                )
                found = jnp.exp(INVERSE_TEMP * scores)
                kernel_ref[row : row + TILE, col : col + tile] = found.astype(BF16)
                sums = found[:, :LANES]
                for lane in range(LANES, tile, LANES):
                    sums += found[:, lane : lane + LANES]
                if col:
                    sums += sums_ref[row : row + TILE, :]
                sums_ref[row : row + TILE, :] = sums


def turned_body(own_ref, other_ref, held_ref, *out_refs, tgt_rows):
    rows = tgt_rows + EXTRA
    columns = out_refs[0].shape[0]
    per = min(TILE, columns) // tgt_rows
    tile = per * tgt_rows
    for col in range(0, columns, tile):
        first = col // tgt_rows
        tgt_unit = unit_rows(
            jnp.concatenate(
                [held_ref[pl.ds((first + s) * rows, tgt_rows), :] for s in range(per)]
            )
        )
        for cand_ref, out_ref in zip((own_ref, other_ref), out_refs):
            for row in range(0, cand_ref.shape[0], TILE):
                scores = lax.dot_general(
                    tgt_unit,
                    cand_ref[row : row + TILE, :],
                    (((1,), (1,)), ((), ())),
                    preferred_element_type=F32,
                )
                out_ref[col : col + tile, row : row + TILE] = jnp.exp(
                    INVERSE_TEMP * scores
                ).astype(BF16)


def put_column(scale_ub, kernels, added, out_refs):
    width = out_refs[0].shape[2]
    first = 0
    for kernel_ref in kernels:
        part = jnp.dot(scale_ub, kernel_ref[...], preferred_element_type=F32)
        slots = kernel_ref.shape[1] // width
        for s in range(slots):
            piece = part[:, s * width : (s + 1) * width]
            if added is not None:
                piece += added[first + s]
            for out_ref in out_refs:
                out_ref[first + s] = piece.astype(out_ref.dtype)
        first += slots


def extras(refs, tgt_rows):
    rows = tgt_rows + EXTRA
    for ref in refs:
        for s in range(ref.shape[0] // rows):
            yield ref[pl.ds(s * rows + tgt_rows, EXTRA), :].astype(F32)


def sums_body(*refs, parts, tgt_rows):
    *refs, out_ref = refs
    each = (out_ref.shape[0] - 8) // 2
    for place in range(2):
        total = sum(ref[...] for ref in refs[place * parts : (place + 1) * parts])
        row = jnp.sum(total.T, axis=0, keepdims=True)
        for i in range(each):
            out_ref[pl.ds(place * each + i, 1), :] = row[:, i * LANES : (i + 1) * LANES]
    counts = jnp.zeros((EXTRA, LANES), F32)
    labels = jnp.zeros((LANES, tgt_rows), F32)
    for extra in extras(refs[2 * parts :], tgt_rows):
        counts += extra[:, LANES:]
        labels += hot(extra[:1, :LANES].astype(jnp.int32), LANES)
    out_ref[pl.ds(2 * each, 8), :] = counts[:8] + counts[1:9]
    out_ref[pl.ds(2 * each + 1, 1), :] = jnp.sum(labels.T, axis=0, keepdims=True)


def count_of(place, mine_ref, got_ref):
    row = mine_ref.shape[0] - 8 + place
    count = mine_ref[pl.ds(row, 1), :] + got_ref[pl.ds(row, 1), :]
    return jnp.broadcast_to(count, (LANES, LANES)).T[:CLASSES, :1]


def first_body(own_weight, other_weight, mine_ref, got_ref, *refs, candidates):
    *kernels, own_marg, other_marg, column_ref, sent_ref = refs
    parts = len(kernels) // 2
    each = (mine_ref.shape[0] - 8) // 2
    total = candidates + 3.0 * count_of(0, mine_ref, got_ref)
    for place, (weight_ref, marg_ref) in enumerate(
        ((own_weight, own_marg), (other_weight, other_marg))
    ):
        rows = [
            mine_ref[pl.ds(place * each + i, 1), :] + got_ref[pl.ds((1 - place) * each + i, 1), :]
            for i in range(each)
        ]
        marg = weight_ref[...] / total
        marg_ref[...] = marg
        scale_ub = (marg / jnp.concatenate(rows, axis=1)).astype(BF16)
        if place == 0:
            put_column(scale_ub, kernels[:parts], None, (column_ref,))
        else:
            put_column(scale_ub, kernels[parts:], column_ref, (column_ref, sent_ref))


def target_body(mine_ref, got_ref, *refs, targets):
    *held_refs, marg_ref = refs
    total = targets + 3.0 * count_of(1, mine_ref, got_ref)
    for s, extra in enumerate(extras(held_refs, marg_ref.shape[2])):
        marg_ref[s] = (1.0 + 3.0 * hot(extra[:1, :LANES].astype(jnp.int32))) / total


def image_body(scale_ref, *refs):
    *turned, image_ref = refs
    image = 0.0
    first = 0
    for turned_ref in turned:
        slots = turned_ref.shape[0] // scale_ref.shape[2]
        scale_v = jnp.concatenate([scale_ref[s] for s in range(first, first + slots)], axis=1)
        image += jnp.dot(scale_v, turned_ref[...], preferred_element_type=F32)
        first += slots
    image_ref[...] = image


def own_body(image_ref, got_ref, marg_ref, *refs, parts):
    kernels, (column_ref, *out_refs) = refs[:parts], refs[parts:]
    scale_u = marg_ref[...] / (image_ref[...] + got_ref[...])
    for out_ref in out_refs:
        out_ref[...] = scale_u
    put_column(scale_u.astype(BF16), kernels, None, (column_ref,))


def other_body(image_ref, got_ref, marg_ref, added_ref, *refs):
    *kernels, column_ref, sent_ref = refs
    scale_u = marg_ref[...] / (image_ref[...] + got_ref[...])
    put_column(scale_u.astype(BF16), kernels, added_ref, (column_ref, sent_ref))


def last_body(image_ref, got_ref, u_ref, scale_v_ref, mass_ref, own_ref, *, candidates):
    own_ref[...] = scale_v_ref[0]
    mass_ref[...] = candidates * u_ref[...] * (image_ref[...] + got_ref[...])


def slot_of(slot, flips, slots):
    top = slots.bit_length()
    found = []
    for kind, flip in enumerate(flips):
        turned = sum(1 << i for i, bit in enumerate(slot_bits(kind, top)) if flip >> bit & 1)
        found.append(slot ^ turned)
    if found[0] == found[1]:
        return found[0]
    return found[0] + parity(lax.axis_index("row"), top) * (found[1] - found[0])


def total_of(slot, own_ref, got_refs, flips):
    total = own_ref[slot]
    for pair, got_ref in zip(flips, got_refs):
        total += got_ref[slot_of(slot, pair, own_ref.shape[0])].astype(F32)
    return total


def sum_body(own_ref, *refs, flips):
    *got_refs, total_ref, sent_ref = refs
    for slot in range(own_ref.shape[0]):
        total = total_of(slot, own_ref, got_refs, flips)
        total_ref[slot] = total
        sent_ref[slot] = total.astype(BF16)


def scale_body(own_ref, marg_ref, *refs, flips):
    got_refs, outs = refs[: len(flips)], refs[len(flips) :]
    for slot in range(own_ref.shape[0]):
        scale_v = marg_ref[slot] / total_of(slot, own_ref, got_refs, flips)
        for out_ref in outs:
            out_ref[slot] = scale_v.astype(out_ref.dtype)


def shards(cand_embed, cand_labels, tgt_embed, tgt_labels):
    devices = lax.axis_size("row")
    top = devices.bit_length() - 1
    slots = devices // 2
    cand_rows, width = cand_embed.shape
    tgt_rows = tgt_embed.shape[0]
    label_rows = cand_labels.reshape(cand_rows // LANES, LANES)
    cand_labels = cand_labels.reshape(1, cand_rows)
    block = (slots, CLASSES, tgt_rows)
    image_type = ((CLASSES, cand_rows), F32)
    half_flops = 2 * cand_rows * slots * tgt_rows * 128

    def fill(held):
        columns = held.shape[0] // (tgt_rows + EXTRA) * tgt_rows
        return call(
            functools.partial(fill_body, tgt_rows=tgt_rows),
            [((cand_rows, columns), BF16)] * 2 + [((cand_rows, LANES), F32)] * 2,
            cand_unit, other_unit, held, flops=8 * 2 * cand_rows * columns * 128,
        )

    held = piece = pack(tgt_embed, tgt_labels.reshape(1, tgt_rows), cand_labels)
    cand_unit = unit_rows(cand_embed)
    weight = 1.0 + 3.0 * hot(cand_labels)
    across = []
    other_unit = None
    for bits in list(zip(slot_bits(0, top), slot_bits(1, top)))[:-1]:
        turned = exchange(held, *[1 << bit for bit in bits])
        across.append(exchange(piece, 2))
        piece, across, cand_unit, weight, other_unit = lax.optimization_barrier(
            (turned, across, cand_unit, weight, other_unit)
        )
        held = jnp.concatenate([held, piece])
        if other_unit is None:
            other_unit = swap(cand_unit), swap(label_rows)
    later = exchange(piece, 2)
    other_unit, other_labels = other_unit
    other_weight = 1.0 + 3.0 * hot(other_labels.reshape(1, cand_rows))
    near = [held, jnp.concatenate(across)]
    filled = [fill(part) for part in near]
    later, filled, other_weight = lax.optimization_barrier((later, filled, other_weight))
    near.append(later)
    filled.append(fill(later))
    own_kernels, other_kernels, own_sums, other_sums = zip(*filled)

    (mine,) = call(
        functools.partial(sums_body, parts=len(near), tgt_rows=tgt_rows),
        [((2 * cand_rows // LANES + 8, LANES), F32)], *own_sums, *other_sums, *near,
    )
    got = swap(mine)
    own_marg, other_marg, column, sent = call(
        functools.partial(first_body, candidates=float(cand_rows * devices)),
        [image_type, image_type, (block, F32), (block, BF16)],
        weight, other_weight, mine, got, *own_kernels, *other_kernels, flops=2 * half_flops,
    )
    sent, cand_unit, other_unit, near = lax.optimization_barrier(
        (sent, cand_unit, other_unit, near)
    )
    turned = []
    for part in near:
        columns = part.shape[0] // (tgt_rows + EXTRA) * tgt_rows
        turned.append(
            call(
                functools.partial(turned_body, tgt_rows=tgt_rows),
                [((columns, cand_rows), BF16)] * 2,
                cand_unit, other_unit, part, flops=8 * 2 * cand_rows * columns * 128,
            )
        )
    own_turned, other_turned = zip(*turned)
    (tgt_marg,) = call(
        functools.partial(target_body, targets=float(tgt_rows * devices)),
        [(block, F32)], mine, got, *near,
    )
    for step in range(ITERS):
        last = step == ITERS - 1
        if step:
            column, *scale_u = call(
                functools.partial(own_body, parts=len(near)),
                [(block, F32)] + [image_type] * last,
                own_image, own_got, own_marg, *own_kernels, flops=half_flops,
            )
            column, sent = call(
                other_body, [(block, F32), (block, BF16)],
                other_image, other_got, other_marg, column, *other_kernels, flops=half_flops,
            )
        order = list(zip(rounds(0, top), rounds(1, top)))
        for place, pair in enumerate(order):
            flips = list(zip(*[flips_of(bits) for bits in pair]))
            found = [exchange(sent, *turn) for turn in flips]
            if place < len(order) - 1:
                column, sent = call(
                    functools.partial(sum_body, flips=flips),
                    [(block, F32), (block, BF16)], column, *found,
                )
        if last:
            potential = ENTROPY_TEMP * jnp.log(scale_u[0])
            found, potential = lax.optimization_barrier((found, potential))
        scale_vb, *scale_v = call(
            functools.partial(scale_body, flips=flips),
            [(block, BF16)] + [(block, F32)] * last,
            column, tgt_marg, *found,
        )
        (other_image,) = call(
            image_body, [image_type], scale_vb, *other_turned, flops=half_flops
        )
        own_got = swap(other_image)
        (own_image,) = call(image_body, [image_type], scale_vb, *own_turned, flops=half_flops)
        if not last:
            other_got = swap(own_image)
    space = pl.BlockSpec(memory_space=pltpu.VMEM)
    args = [own_image, own_got, *scale_u, *scale_v]
    mass, tgt_scaling = pl.pallas_call(
        functools.partial(last_body, candidates=float(cand_rows * devices)),
        out_shape=[
            jax.ShapeDtypeStruct(*image_type), jax.ShapeDtypeStruct((CLASSES, tgt_rows), F32)
        ],
        in_specs=[space] * len(args),
        out_specs=[space] * 2,
        compiler_params=pltpu.CompilerParams(vmem_limit_bytes=12 * 1024 * 1024),
    )(*[pltpu.with_memory_space_constraint(a, pltpu.VMEM) for a in args])
    return (potential, tgt_scaling, mass)


def solution(mesh):
    return jax.shard_map(
        shards,
        mesh=mesh,
        in_specs=(
            P(("grp", "row"), None),
            P(("grp", "row")),
            P(("grp", "row"), None),
            P(("grp", "row")),
        ),
        out_specs=(P(None, ("grp", "row")), P(None, ("grp", "row")), P(None, ("grp", "row"))),
        check_vma=False,
    )
```

```python
import functools
import math

import jax
import jax.numpy as jnp
from jax import lax
from jax.experimental import pallas as pl
from jax.experimental.pallas import tpu as pltpu
from jax.sharding import PartitionSpec as P

CLASSES = 32
ITERS = 3
INVERSE_TEMP = 20.0
ENTROPY_TEMP = 0.05
LANES = 128
EXTRA = 16
TILE = 256
F32 = jnp.float32
BF16 = jnp.bfloat16


def parity(index, top):
    return sum(index // (1 << bit) % 2 for bit in range(top)) % 2


def slot_bits(kind, top):
    layer = list(range(2, top))
    return (layer if kind else layer[::-1]) + [1]


def rounds(kind, top):
    bits = list(range(1, top))
    bits = bits[1 - kind :] + bits[: 1 - kind]
    return [bits[low : low + 2] for low in range(0, len(bits), 2)]


def flips_of(bits):
    flips = [0]
    for bit in bits:
        flips += [flip | 1 << bit for flip in flips]
    return flips[1:]


def exchange(block, *flips):
    devices = lax.axis_size("row")
    top = devices.bit_length() - 1
    pairs = []
    for d in range(devices):
        flip = flips[parity(d, top) % len(flips)]
        pairs.append((d, d ^ flip ^ parity(flip, top)))
    return lax.ppermute(block, "row", pairs)


def swap(block):
    devices = lax.axis_size("row")
    return lax.ppermute(block, "row", [(d, d ^ 1) for d in range(devices)])


def call(body, outs, *args, flops=0):
    space = pl.BlockSpec(memory_space=pltpu.VMEM)
    moved = sum(a.size * a.dtype.itemsize for a in args)
    return pl.pallas_call(
        body,
        out_shape=[pltpu.VMEM(shape, dtype) for shape, dtype in outs],
        in_specs=[space] * len(args),
        out_specs=[space] * len(outs),
        compiler_params=pltpu.CompilerParams(vmem_limit_bytes=12 * 1024 * 1024),
        cost_estimate=pl.CostEstimate(flops=flops, bytes_accessed=moved, transcendentals=0),
    )(*[pltpu.with_memory_space_constraint(a, pltpu.VMEM) for a in args])


def unit_rows(values):
    widened = values.astype(F32)
    meansq = jnp.mean(widened * widened, axis=1, keepdims=True)
    return (widened * lax.rsqrt(meansq + 1e-06) / math.sqrt(values.shape[1])).astype(BF16)


def hot(labels, classes=CLASSES):
    rows = lax.broadcasted_iota(jnp.int32, (classes, labels.shape[1]), 0)
    return (labels == rows).astype(F32)


def pack_body(embed_hbm, tgt_hbm, cand_hbm, out_ref, tgt_ref, cand_ref, sems):
    rows = embed_hbm.shape[0]
    copies = [
        pltpu.make_async_copy(cand_hbm, cand_ref, sems.at[0]),
        pltpu.make_async_copy(tgt_hbm, tgt_ref, sems.at[1]),
        pltpu.make_async_copy(embed_hbm, out_ref.at[pl.ds(0, rows)], sems.at[2]),
    ]
    for copy in copies:
        copy.start()
    copies[0].wait()
    counts = lax.dot_general(
        jnp.ones((EXTRA, cand_ref.shape[1]), BF16),
        hot(cand_ref[...]).astype(BF16),
        (((1,), (1,)), ((), ())),
        preferred_element_type=F32,
    )
    high = counts.astype(BF16).astype(F32)
    even = lax.broadcasted_iota(jnp.int32, counts.shape, 0) % 2 == 0
    out_ref[rows:, LANES:] = jnp.zeros((EXTRA, LANES), BF16)
    out_ref[rows:, LANES : LANES + CLASSES] = jnp.where(even, high, counts - high).astype(BF16)
    copies[1].wait()
    out_ref[rows:, :LANES] = jnp.broadcast_to(
        tgt_ref[...].astype(F32), (EXTRA, LANES)
    ).astype(BF16)
    copies[2].wait()


def pack(tgt_embed, tgt_labels, cand_labels):
    rows, width = tgt_embed.shape
    anywhere = pl.BlockSpec(memory_space=pl.ANY)
    return pl.pallas_call(
        pack_body,
        out_shape=pltpu.VMEM((rows + EXTRA, width), BF16),
        in_specs=[anywhere] * 3,
        out_specs=pl.BlockSpec(memory_space=pltpu.VMEM),
        scratch_shapes=[
            pltpu.VMEM(tgt_labels.shape, jnp.int32),
            pltpu.VMEM(cand_labels.shape, jnp.int32),
            pltpu.SemaphoreType.DMA((3,)),
        ],
        compiler_params=pltpu.CompilerParams(vmem_limit_bytes=12 * 1024 * 1024),
    )(*[
        pltpu.with_memory_space_constraint(a, pltpu.HBM)
        for a in (tgt_embed, tgt_labels, cand_labels)
    ])


def fill_body(own_ref, other_ref, held_ref, *out_refs, tgt_rows):
    rows = tgt_rows + EXTRA
    columns = out_refs[0].shape[1]
    per = min(TILE, columns) // tgt_rows
    tile = per * tgt_rows
    for col in range(0, columns, tile):
        first = col // tgt_rows
        block = jnp.concatenate(
            [held_ref[pl.ds((first + s) * rows, tgt_rows), :] for s in range(per)]
        )
        tgt_unit = unit_rows(block)
        for cand_ref, kernel_ref, sums_ref in zip((own_ref, other_ref), out_refs, out_refs[2:]):
            for row in range(0, cand_ref.shape[0], TILE):
                scores = lax.dot_general(
                    cand_ref[row : row + TILE, :],
                    tgt_unit,
                    (((1,), (1,)), ((), ())),
                    preferred_element_type=F32,
                )
                found = jnp.exp(INVERSE_TEMP * scores)
                kernel_ref[row : row + TILE, col : col + tile] = found.astype(BF16)
                sums = found[:, :LANES]
                for lane in range(LANES, tile, LANES):
                    sums += found[:, lane : lane + LANES]
                if col:
                    sums += sums_ref[row : row + TILE, :]
                sums_ref[row : row + TILE, :] = sums


def turned_body(own_ref, other_ref, held_ref, *out_refs, tgt_rows):
    rows = tgt_rows + EXTRA
    columns = out_refs[0].shape[0]
    per = min(TILE, columns) // tgt_rows
    tile = per * tgt_rows
    for col in range(0, columns, tile):
        first = col // tgt_rows
        tgt_unit = unit_rows(
            jnp.concatenate(
                [held_ref[pl.ds((first + s) * rows, tgt_rows), :] for s in range(per)]
            )
        )
        for cand_ref, out_ref in zip((own_ref, other_ref), out_refs):
            for row in range(0, cand_ref.shape[0], TILE):
                scores = lax.dot_general(
                    tgt_unit,
                    cand_ref[row : row + TILE, :],
                    (((1,), (1,)), ((), ())),
                    preferred_element_type=F32,
                )
                out_ref[col : col + tile, row : row + TILE] = jnp.exp(
                    INVERSE_TEMP * scores
                ).astype(BF16)


def put_column(scale_ub, kernels, added, out_refs):
    width = out_refs[0].shape[2]
    first = 0
    for kernel_ref in kernels:
        part = jnp.dot(scale_ub, kernel_ref[...], preferred_element_type=F32)
        slots = kernel_ref.shape[1] // width
        for s in range(slots):
            piece = part[:, s * width : (s + 1) * width]
            if added is not None:
                piece += added[first + s]
            for out_ref in out_refs:
                out_ref[first + s] = piece.astype(out_ref.dtype)
        first += slots


def extras(refs, tgt_rows):
    rows = tgt_rows + EXTRA
    for ref in refs:
        for s in range(ref.shape[0] // rows):
            yield ref[pl.ds(s * rows + tgt_rows, EXTRA), :].astype(F32)


def sums_body(*refs, parts, tgt_rows):
    *refs, out_ref = refs
    each = (out_ref.shape[0] - 8) // 2
    for place in range(2):
        total = sum(ref[...] for ref in refs[place * parts : (place + 1) * parts])
        row = jnp.sum(total.T, axis=0, keepdims=True)
        for i in range(each):
            out_ref[pl.ds(place * each + i, 1), :] = row[:, i * LANES : (i + 1) * LANES]
    counts = jnp.zeros((EXTRA, LANES), F32)
    labels = jnp.zeros((LANES, tgt_rows), F32)
    for extra in extras(refs[2 * parts :], tgt_rows):
        counts += extra[:, LANES:]
        labels += hot(extra[:1, :LANES].astype(jnp.int32), LANES)
    out_ref[pl.ds(2 * each, 8), :] = counts[:8] + counts[1:9]
    out_ref[pl.ds(2 * each + 1, 1), :] = jnp.sum(labels.T, axis=0, keepdims=True)


def count_of(place, mine_ref, got_ref):
    row = mine_ref.shape[0] - 8 + place
    count = mine_ref[pl.ds(row, 1), :] + got_ref[pl.ds(row, 1), :]
    return jnp.broadcast_to(count, (LANES, LANES)).T[:CLASSES, :1]


def first_body(own_weight, other_weight, mine_ref, got_ref, *refs, candidates):
    *kernels, own_marg, other_marg, column_ref, sent_ref = refs
    parts = len(kernels) // 2
    each = (mine_ref.shape[0] - 8) // 2
    total = candidates + 3.0 * count_of(0, mine_ref, got_ref)
    for place, (weight_ref, marg_ref) in enumerate(
        ((own_weight, own_marg), (other_weight, other_marg))
    ):
        rows = [
            mine_ref[pl.ds(place * each + i, 1), :] + got_ref[pl.ds((1 - place) * each + i, 1), :]
            for i in range(each)
        ]
        marg = weight_ref[...] / total
        marg_ref[...] = marg
        scale_ub = (marg / jnp.concatenate(rows, axis=1)).astype(BF16)
        if place == 0:
            put_column(scale_ub, kernels[:parts], None, (column_ref,))
        else:
            put_column(scale_ub, kernels[parts:], column_ref, (column_ref, sent_ref))


def target_body(mine_ref, got_ref, *refs, targets):
    *held_refs, marg_ref = refs
    total = targets + 3.0 * count_of(1, mine_ref, got_ref)
    for s, extra in enumerate(extras(held_refs, marg_ref.shape[2])):
        marg_ref[s] = (1.0 + 3.0 * hot(extra[:1, :LANES].astype(jnp.int32))) / total


def image_body(scale_ref, *refs):
    *turned, image_ref, sent_ref = refs
    image = 0.0
    first = 0
    for turned_ref in turned:
        slots = turned_ref.shape[0] // scale_ref.shape[2]
        scale_v = jnp.concatenate([scale_ref[s] for s in range(first, first + slots)], axis=1)
        image += jnp.dot(scale_v, turned_ref[...], preferred_element_type=F32)
        first += slots
    image_ref[...] = image
    sent_ref[...] = image.astype(BF16)


def own_body(image_ref, got_ref, marg_ref, *refs, parts):
    kernels, (column_ref, *out_refs) = refs[:parts], refs[parts:]
    scale_u = marg_ref[...] / (image_ref[...] + got_ref[...].astype(F32))
    for out_ref in out_refs:
        out_ref[...] = scale_u
    put_column(scale_u.astype(BF16), kernels, None, (column_ref,))


def other_body(image_ref, got_ref, marg_ref, added_ref, *refs):
    *kernels, column_ref, sent_ref = refs
    scale_u = marg_ref[...] / (image_ref[...] + got_ref[...].astype(F32))
    put_column(scale_u.astype(BF16), kernels, added_ref, (column_ref, sent_ref))


def last_body(image_ref, got_ref, u_ref, scale_v_ref, mass_ref, own_ref, *, candidates):
    own_ref[...] = scale_v_ref[0]
    mass_ref[...] = candidates * u_ref[...] * (image_ref[...] + got_ref[...].astype(F32))


def slot_of(slot, flips, slots):
    top = slots.bit_length()
    found = []
    for kind, flip in enumerate(flips):
        turned = sum(1 << i for i, bit in enumerate(slot_bits(kind, top)) if flip >> bit & 1)
        found.append(slot ^ turned)
    if found[0] == found[1]:
        return found[0]
    return found[0] + parity(lax.axis_index("row"), top) * (found[1] - found[0])


def total_of(slot, own_ref, got_refs, flips):
    total = own_ref[slot]
    for pair, got_ref in zip(flips, got_refs):
        total += got_ref[slot_of(slot, pair, own_ref.shape[0])].astype(F32)
    return total


def sum_body(own_ref, *refs, flips):
    *got_refs, total_ref, sent_ref = refs
    for slot in range(own_ref.shape[0]):
        total = total_of(slot, own_ref, got_refs, flips)
        total_ref[slot] = total
        sent_ref[slot] = total.astype(BF16)


def scale_body(own_ref, marg_ref, *refs, flips):
    got_refs, outs = refs[: len(flips)], refs[len(flips) :]
    for slot in range(own_ref.shape[0]):
        scale_v = marg_ref[slot] / total_of(slot, own_ref, got_refs, flips)
        for out_ref in outs:
            out_ref[slot] = scale_v.astype(out_ref.dtype)


def shards(cand_embed, cand_labels, tgt_embed, tgt_labels):
    devices = lax.axis_size("row")
    top = devices.bit_length() - 1
    slots = devices // 2
    cand_rows, width = cand_embed.shape
    tgt_rows = tgt_embed.shape[0]
    label_rows = cand_labels.reshape(cand_rows // LANES, LANES)
    cand_labels = cand_labels.reshape(1, cand_rows)
    block = (slots, CLASSES, tgt_rows)
    image_type = ((CLASSES, cand_rows), F32)
    half_flops = 2 * cand_rows * slots * tgt_rows * 128

    def fill(held):
        columns = held.shape[0] // (tgt_rows + EXTRA) * tgt_rows
        return call(
            functools.partial(fill_body, tgt_rows=tgt_rows),
            [((cand_rows, columns), BF16)] * 2 + [((cand_rows, LANES), F32)] * 2,
            cand_unit, other_unit, held, flops=8 * 2 * cand_rows * columns * 128,
        )

    held = piece = pack(tgt_embed, tgt_labels.reshape(1, tgt_rows), cand_labels)
    cand_unit = unit_rows(cand_embed)
    weight = 1.0 + 3.0 * hot(cand_labels)
    across = []
    other_unit = None
    for bits in list(zip(slot_bits(0, top), slot_bits(1, top)))[:-1]:
        turned = exchange(held, *[1 << bit for bit in bits])
        across.append(exchange(piece, 2))
        piece, across, cand_unit, weight, other_unit = lax.optimization_barrier(
            (turned, across, cand_unit, weight, other_unit)
        )
        held = jnp.concatenate([held, piece])
        if other_unit is None:
            other_unit = swap(cand_unit), swap(label_rows)
    later = exchange(piece, 2)
    other_unit, other_labels = other_unit
    other_weight = 1.0 + 3.0 * hot(other_labels.reshape(1, cand_rows))
    near = [held, jnp.concatenate(across)]
    filled = [fill(part) for part in near]
    later, filled, other_weight = lax.optimization_barrier((later, filled, other_weight))
    near.append(later)
    filled.append(fill(later))
    own_kernels, other_kernels, own_sums, other_sums = zip(*filled)

    (mine,) = call(
        functools.partial(sums_body, parts=len(near), tgt_rows=tgt_rows),
        [((2 * cand_rows // LANES + 8, LANES), F32)], *own_sums, *other_sums, *near,
    )
    got = swap(mine)
    own_marg, other_marg, column, sent = call(
        functools.partial(first_body, candidates=float(cand_rows * devices)),
        [image_type, image_type, (block, F32), (block, BF16)],
        weight, other_weight, mine, got, *own_kernels, *other_kernels, flops=2 * half_flops,
    )
    sent, cand_unit, other_unit, near = lax.optimization_barrier(
        (sent, cand_unit, other_unit, near)
    )
    turned = []
    for part in near:
        columns = part.shape[0] // (tgt_rows + EXTRA) * tgt_rows
        turned.append(
            call(
                functools.partial(turned_body, tgt_rows=tgt_rows),
                [((columns, cand_rows), BF16)] * 2,
                cand_unit, other_unit, part, flops=8 * 2 * cand_rows * columns * 128,
            )
        )
    own_turned, other_turned = zip(*turned)
    (tgt_marg,) = call(
        functools.partial(target_body, targets=float(tgt_rows * devices)),
        [(block, F32)], mine, got, *near,
    )
    for step in range(ITERS):
        last = step == ITERS - 1
        if step:
            column, *scale_u = call(
                functools.partial(own_body, parts=len(near)),
                [(block, F32)] + [image_type] * last,
                own_image, own_got, own_marg, *own_kernels, flops=half_flops,
            )
            column, sent = call(
                other_body, [(block, F32), (block, BF16)],
                other_image, other_got, other_marg, column, *other_kernels, flops=half_flops,
            )
        order = list(zip(rounds(0, top), rounds(1, top)))
        for place, pair in enumerate(order):
            flips = list(zip(*[flips_of(bits) for bits in pair]))
            found = [exchange(sent, *turn) for turn in flips]
            if place < len(order) - 1:
                column, sent = call(
                    functools.partial(sum_body, flips=flips),
                    [(block, F32), (block, BF16)], column, *found,
                )
        if last:
            potential = ENTROPY_TEMP * jnp.log(scale_u[0])
            found, potential = lax.optimization_barrier((found, potential))
        scale_vb, *scale_v = call(
            functools.partial(scale_body, flips=flips),
            [(block, BF16)] + [(block, F32)] * last,
            column, tgt_marg, *found,
        )
        both = [image_type, ((CLASSES, cand_rows), BF16)]
        other_image, sent = call(image_body, both, scale_vb, *other_turned, flops=half_flops)
        own_got = swap(sent)
        own_image, sent = call(image_body, both, scale_vb, *own_turned, flops=half_flops)
        if not last:
            other_got = swap(sent)
    space = pl.BlockSpec(memory_space=pltpu.VMEM)
    args = [own_image, own_got, *scale_u, *scale_v]
    mass, tgt_scaling = pl.pallas_call(
        functools.partial(last_body, candidates=float(cand_rows * devices)),
        out_shape=[
            jax.ShapeDtypeStruct(*image_type), jax.ShapeDtypeStruct((CLASSES, tgt_rows), F32)
        ],
        in_specs=[space] * len(args),
        out_specs=[space] * 2,
        compiler_params=pltpu.CompilerParams(vmem_limit_bytes=12 * 1024 * 1024),
    )(*[pltpu.with_memory_space_constraint(a, pltpu.VMEM) for a in args])
    return (potential, tgt_scaling, mass)


def solution(mesh):
    return jax.shard_map(
        shards,
        mesh=mesh,
        in_specs=(
            P(("grp", "row"), None),
            P(("grp", "row")),
            P(("grp", "row"), None),
            P(("grp", "row")),
        ),
        out_specs=(P(None, ("grp", "row")), P(None, ("grp", "row")), P(None, ("grp", "row"))),
        check_vma=False,
    )
```

```python
import functools
import math

import jax
import jax.numpy as jnp
from jax import lax
from jax.experimental import pallas as pl
from jax.experimental.pallas import tpu as pltpu
from jax.sharding import PartitionSpec as P

CLASSES = 32
ITERS = 3
INVERSE_TEMP = 20.0
ENTROPY_TEMP = 0.05
LANES = 128
EXTRA = 16
TILE = 256
F32 = jnp.float32
BF16 = jnp.bfloat16


def parity(index, top):
    return sum(index // (1 << bit) % 2 for bit in range(top)) % 2


def slot_bits(kind, top):
    layer = list(range(2, top))
    return (layer if kind else layer[::-1]) + [1]


def rounds(kind, top):
    bits = list(range(1, top))
    bits = bits[kind:] + bits[:kind]
    return [bits[low : low + 2] for low in range(0, len(bits), 2)]


def flips_of(bits):
    flips = [0]
    for bit in bits:
        flips += [flip | 1 << bit for flip in flips]
    return flips[1:]


def exchange(block, *flips):
    devices = lax.axis_size("row")
    top = devices.bit_length() - 1
    pairs = []
    for d in range(devices):
        flip = flips[parity(d, top) % len(flips)]
        pairs.append((d, d ^ flip ^ parity(flip, top)))
    return lax.ppermute(block, "row", pairs)


def swap(block):
    devices = lax.axis_size("row")
    return lax.ppermute(block, "row", [(d, d ^ 1) for d in range(devices)])


def call(body, outs, *args, flops=0):
    space = pl.BlockSpec(memory_space=pltpu.VMEM)
    moved = sum(a.size * a.dtype.itemsize for a in args)
    return pl.pallas_call(
        body,
        out_shape=[pltpu.VMEM(shape, dtype) for shape, dtype in outs],
        in_specs=[space] * len(args),
        out_specs=[space] * len(outs),
        compiler_params=pltpu.CompilerParams(vmem_limit_bytes=12 * 1024 * 1024),
        cost_estimate=pl.CostEstimate(flops=flops, bytes_accessed=moved, transcendentals=0),
    )(*[pltpu.with_memory_space_constraint(a, pltpu.VMEM) for a in args])


def unit_rows(values):
    widened = values.astype(F32)
    meansq = jnp.mean(widened * widened, axis=1, keepdims=True)
    return (widened * lax.rsqrt(meansq + 1e-06) / math.sqrt(values.shape[1])).astype(BF16)


def hot(labels, classes=CLASSES):
    rows = lax.broadcasted_iota(jnp.int32, (classes, labels.shape[1]), 0)
    return (labels == rows).astype(F32)


def pack_body(embed_hbm, tgt_hbm, cand_hbm, out_ref, tgt_ref, cand_ref, sems):
    rows = embed_hbm.shape[0]
    copies = [
        pltpu.make_async_copy(cand_hbm, cand_ref, sems.at[0]),
        pltpu.make_async_copy(tgt_hbm, tgt_ref, sems.at[1]),
        pltpu.make_async_copy(embed_hbm, out_ref.at[pl.ds(0, rows)], sems.at[2]),
    ]
    for copy in copies:
        copy.start()
    copies[0].wait()
    counts = lax.dot_general(
        jnp.ones((EXTRA, cand_ref.shape[1]), BF16),
        hot(cand_ref[...]).astype(BF16),
        (((1,), (1,)), ((), ())),
        preferred_element_type=F32,
    )
    high = counts.astype(BF16).astype(F32)
    even = lax.broadcasted_iota(jnp.int32, counts.shape, 0) % 2 == 0
    out_ref[rows:, LANES:] = jnp.zeros((EXTRA, LANES), BF16)
    out_ref[rows:, LANES : LANES + CLASSES] = jnp.where(even, high, counts - high).astype(BF16)
    copies[1].wait()
    out_ref[rows:, :LANES] = jnp.broadcast_to(
        tgt_ref[...].astype(F32), (EXTRA, LANES)
    ).astype(BF16)
    copies[2].wait()


def pack(tgt_embed, tgt_labels, cand_labels):
    rows, width = tgt_embed.shape
    anywhere = pl.BlockSpec(memory_space=pl.ANY)
    return pl.pallas_call(
        pack_body,
        out_shape=pltpu.VMEM((rows + EXTRA, width), BF16),
        in_specs=[anywhere] * 3,
        out_specs=pl.BlockSpec(memory_space=pltpu.VMEM),
        scratch_shapes=[
            pltpu.VMEM(tgt_labels.shape, jnp.int32),
            pltpu.VMEM(cand_labels.shape, jnp.int32),
            pltpu.SemaphoreType.DMA((3,)),
        ],
        compiler_params=pltpu.CompilerParams(vmem_limit_bytes=12 * 1024 * 1024),
    )(*[
        pltpu.with_memory_space_constraint(a, pltpu.HBM)
        for a in (tgt_embed, tgt_labels, cand_labels)
    ])


def fill_body(own_ref, other_ref, held_ref, *out_refs, tgt_rows):
    rows = tgt_rows + EXTRA
    columns = out_refs[0].shape[1]
    per = min(TILE, columns) // tgt_rows
    tile = per * tgt_rows
    for col in range(0, columns, tile):
        first = col // tgt_rows
        block = jnp.concatenate(
            [held_ref[pl.ds((first + s) * rows, tgt_rows), :] for s in range(per)]
        )
        tgt_unit = unit_rows(block)
        for cand_ref, kernel_ref, sums_ref in zip((own_ref, other_ref), out_refs, out_refs[2:]):
            for row in range(0, cand_ref.shape[0], TILE):
                scores = lax.dot_general(
                    cand_ref[row : row + TILE, :],
                    tgt_unit,
                    (((1,), (1,)), ((), ())),
                    preferred_element_type=F32,
                )
                found = jnp.exp(INVERSE_TEMP * scores)
                kernel_ref[row : row + TILE, col : col + tile] = found.astype(BF16)
                sums = found[:, :LANES]
                for lane in range(LANES, tile, LANES):
                    sums += found[:, lane : lane + LANES]
                if col:
                    sums += sums_ref[row : row + TILE, :]
                sums_ref[row : row + TILE, :] = sums


def turned_body(own_ref, other_ref, held_ref, *out_refs, tgt_rows):
    rows = tgt_rows + EXTRA
    columns = out_refs[0].shape[0]
    per = min(TILE, columns) // tgt_rows
    tile = per * tgt_rows
    for col in range(0, columns, tile):
        first = col // tgt_rows
        tgt_unit = unit_rows(
            jnp.concatenate(
                [held_ref[pl.ds((first + s) * rows, tgt_rows), :] for s in range(per)]
            )
        )
        for cand_ref, out_ref in zip((own_ref, other_ref), out_refs):
            for row in range(0, cand_ref.shape[0], TILE):
                scores = lax.dot_general(
                    tgt_unit,
                    cand_ref[row : row + TILE, :],
                    (((1,), (1,)), ((), ())),
                    preferred_element_type=F32,
                )
                out_ref[col : col + tile, row : row + TILE] = jnp.exp(
                    INVERSE_TEMP * scores
                ).astype(BF16)


def put_column(scale_ub, kernels, added, out_refs):
    width = out_refs[0].shape[2]
    first = 0
    for kernel_ref in kernels:
        part = jnp.dot(scale_ub, kernel_ref[...], preferred_element_type=F32)
        slots = kernel_ref.shape[1] // width
        for s in range(slots):
            piece = part[:, s * width : (s + 1) * width]
            if added is not None:
                piece += added[first + s]
            for out_ref in out_refs:
                out_ref[first + s] = piece.astype(out_ref.dtype)
        first += slots


def extras(refs, tgt_rows):
    rows = tgt_rows + EXTRA
    for ref in refs:
        for s in range(ref.shape[0] // rows):
            yield ref[pl.ds(s * rows + tgt_rows, EXTRA), :].astype(F32)


def sums_body(*refs, parts, tgt_rows):
    *refs, out_ref = refs
    each = (out_ref.shape[0] - 8) // 2
    for place in range(2):
        total = sum(ref[...] for ref in refs[place * parts : (place + 1) * parts])
        row = jnp.sum(total.T, axis=0, keepdims=True)
        for i in range(each):
            out_ref[pl.ds(place * each + i, 1), :] = row[:, i * LANES : (i + 1) * LANES]
    counts = jnp.zeros((EXTRA, LANES), F32)
    labels = jnp.zeros((LANES, tgt_rows), F32)
    for extra in extras(refs[2 * parts :], tgt_rows):
        counts += extra[:, LANES:]
        labels += hot(extra[:1, :LANES].astype(jnp.int32), LANES)
    out_ref[pl.ds(2 * each, 8), :] = counts[:8] + counts[1:9]
    out_ref[pl.ds(2 * each + 1, 1), :] = jnp.sum(labels.T, axis=0, keepdims=True)


def count_of(place, mine_ref, got_ref):
    row = mine_ref.shape[0] - 8 + place
    count = mine_ref[pl.ds(row, 1), :] + got_ref[pl.ds(row, 1), :]
    return jnp.broadcast_to(count, (LANES, LANES)).T[:CLASSES, :1]


def first_body(own_weight, other_weight, mine_ref, got_ref, *refs, candidates):
    *kernels, own_marg, other_marg, column_ref, sent_ref = refs
    parts = len(kernels) // 2
    each = (mine_ref.shape[0] - 8) // 2
    total = candidates + 3.0 * count_of(0, mine_ref, got_ref)
    for place, (weight_ref, marg_ref) in enumerate(
        ((own_weight, own_marg), (other_weight, other_marg))
    ):
        rows = [
            mine_ref[pl.ds(place * each + i, 1), :] + got_ref[pl.ds((1 - place) * each + i, 1), :]
            for i in range(each)
        ]
        marg = weight_ref[...] / total
        marg_ref[...] = marg
        scale_ub = (marg / jnp.concatenate(rows, axis=1)).astype(BF16)
        if place == 0:
            put_column(scale_ub, kernels[:parts], None, (column_ref,))
        else:
            put_column(scale_ub, kernels[parts:], column_ref, (column_ref, sent_ref))


def target_body(mine_ref, got_ref, *refs, targets):
    *held_refs, marg_ref = refs
    total = targets + 3.0 * count_of(1, mine_ref, got_ref)
    for s, extra in enumerate(extras(held_refs, marg_ref.shape[2])):
        marg_ref[s] = (1.0 + 3.0 * hot(extra[:1, :LANES].astype(jnp.int32))) / total


def image_body(scale_ref, *refs):
    *turned, image_ref = refs
    image = 0.0
    first = 0
    for turned_ref in turned:
        slots = turned_ref.shape[0] // scale_ref.shape[2]
        scale_v = jnp.concatenate([scale_ref[s] for s in range(first, first + slots)], axis=1)
        image += jnp.dot(scale_v, turned_ref[...], preferred_element_type=F32)
        first += slots
    image_ref[...] = image


def own_body(image_ref, got_ref, marg_ref, *refs, parts):
    kernels, (column_ref, *out_refs) = refs[:parts], refs[parts:]
    scale_u = marg_ref[...] / (image_ref[...] + got_ref[...])
    for out_ref in out_refs:
        out_ref[...] = scale_u
    put_column(scale_u.astype(BF16), kernels, None, (column_ref,))


def other_body(image_ref, got_ref, marg_ref, added_ref, *refs):
    *kernels, column_ref, sent_ref = refs
    scale_u = marg_ref[...] / (image_ref[...] + got_ref[...])
    put_column(scale_u.astype(BF16), kernels, added_ref, (column_ref, sent_ref))


def last_body(image_ref, got_ref, u_ref, scale_v_ref, mass_ref, own_ref, *, candidates):
    own_ref[...] = scale_v_ref[0]
    mass_ref[...] = candidates * u_ref[...] * (image_ref[...] + got_ref[...])


def slot_of(slot, flips, slots):
    top = slots.bit_length()
    found = []
    for kind, flip in enumerate(flips):
        turned = sum(1 << i for i, bit in enumerate(slot_bits(kind, top)) if flip >> bit & 1)
        found.append(slot ^ turned)
    if found[0] == found[1]:
        return found[0]
    return found[0] + parity(lax.axis_index("row"), top) * (found[1] - found[0])


def total_of(slot, own_ref, got_refs, flips):
    total = own_ref[slot]
    for pair, got_ref in zip(flips, got_refs):
        total += got_ref[slot_of(slot, pair, own_ref.shape[0])].astype(F32)
    return total


def sum_body(own_ref, *refs, flips):
    *got_refs, total_ref, sent_ref = refs
    for slot in range(own_ref.shape[0]):
        total = total_of(slot, own_ref, got_refs, flips)
        total_ref[slot] = total
        sent_ref[slot] = total.astype(BF16)


def scale_body(own_ref, marg_ref, *refs, flips):
    got_refs, outs = refs[: len(flips)], refs[len(flips) :]
    for slot in range(own_ref.shape[0]):
        scale_v = marg_ref[slot] / total_of(slot, own_ref, got_refs, flips)
        for out_ref in outs:
            out_ref[slot] = scale_v.astype(out_ref.dtype)


def shards(cand_embed, cand_labels, tgt_embed, tgt_labels):
    devices = lax.axis_size("row")
    top = devices.bit_length() - 1
    slots = devices // 2
    cand_rows, width = cand_embed.shape
    tgt_rows = tgt_embed.shape[0]
    label_rows = cand_labels.reshape(cand_rows // LANES, LANES)
    cand_labels = cand_labels.reshape(1, cand_rows)
    block = (slots, CLASSES, tgt_rows)
    image_type = ((CLASSES, cand_rows), F32)
    half_flops = 2 * cand_rows * slots * tgt_rows * 128

    def fill(held):
        columns = held.shape[0] // (tgt_rows + EXTRA) * tgt_rows
        return call(
            functools.partial(fill_body, tgt_rows=tgt_rows),
            [((cand_rows, columns), BF16)] * 2 + [((cand_rows, LANES), F32)] * 2,
            cand_unit, other_unit, held, flops=8 * 2 * cand_rows * columns * 128,
        )

    held = piece = pack(tgt_embed, tgt_labels.reshape(1, tgt_rows), cand_labels)
    cand_unit = unit_rows(cand_embed)
    weight = 1.0 + 3.0 * hot(cand_labels)
    across = []
    other_unit = None
    for bits in list(zip(slot_bits(0, top), slot_bits(1, top)))[:-1]:
        turned = exchange(held, *[1 << bit for bit in bits])
        across.append(exchange(piece, 2))
        piece, across, cand_unit, weight, other_unit = lax.optimization_barrier(
            (turned, across, cand_unit, weight, other_unit)
        )
        held = jnp.concatenate([held, piece])
        if other_unit is None:
            other_unit = swap(cand_unit), swap(label_rows)
    later = exchange(piece, 2)
    other_unit, other_labels = other_unit
    other_weight = 1.0 + 3.0 * hot(other_labels.reshape(1, cand_rows))
    near = [held, jnp.concatenate(across)]
    filled = [fill(part) for part in near]
    later, filled, other_weight = lax.optimization_barrier((later, filled, other_weight))
    near.append(later)
    filled.append(fill(later))
    own_kernels, other_kernels, own_sums, other_sums = zip(*filled)

    (mine,) = call(
        functools.partial(sums_body, parts=len(near), tgt_rows=tgt_rows),
        [((2 * cand_rows // LANES + 8, LANES), F32)], *own_sums, *other_sums, *near,
    )
    got = swap(mine)
    own_marg, other_marg, column, sent = call(
        functools.partial(first_body, candidates=float(cand_rows * devices)),
        [image_type, image_type, (block, F32), (block, BF16)],
        weight, other_weight, mine, got, *own_kernels, *other_kernels, flops=2 * half_flops,
    )
    sent, cand_unit, other_unit, near = lax.optimization_barrier(
        (sent, cand_unit, other_unit, near)
    )
    turned = []
    for part in near:
        columns = part.shape[0] // (tgt_rows + EXTRA) * tgt_rows
        turned.append(
            call(
                functools.partial(turned_body, tgt_rows=tgt_rows),
                [((columns, cand_rows), BF16)] * 2,
                cand_unit, other_unit, part, flops=8 * 2 * cand_rows * columns * 128,
            )
        )
    own_turned, other_turned = zip(*turned)
    (tgt_marg,) = call(
        functools.partial(target_body, targets=float(tgt_rows * devices)),
        [(block, F32)], mine, got, *near,
    )
    for step in range(ITERS):
        last = step == ITERS - 1
        if step:
            column, *scale_u = call(
                functools.partial(own_body, parts=len(near)),
                [(block, F32)] + [image_type] * last,
                own_image, own_got, own_marg, *own_kernels, flops=half_flops,
            )
            column, sent = call(
                other_body, [(block, F32), (block, BF16)],
                other_image, other_got, other_marg, column, *other_kernels, flops=half_flops,
            )
        order = list(zip(rounds(0, top), rounds(1, top)))
        for place, pair in enumerate(order):
            flips = list(zip(*[flips_of(bits) for bits in pair]))
            found = [exchange(sent, *turn) for turn in flips]
            if place < len(order) - 1:
                column, sent = call(
                    functools.partial(sum_body, flips=flips),
                    [(block, F32), (block, BF16)], column, *found,
                )
        if last:
            potential = ENTROPY_TEMP * jnp.log(scale_u[0])
            found, potential = lax.optimization_barrier((found, potential))
        scale_vb, *scale_v = call(
            functools.partial(scale_body, flips=flips),
            [(block, BF16)] + [(block, F32)] * last,
            column, tgt_marg, *found,
        )
        (other_image,) = call(
            image_body, [image_type], scale_vb, *other_turned, flops=half_flops
        )
        own_got = swap(other_image)
        (own_image,) = call(image_body, [image_type], scale_vb, *own_turned, flops=half_flops)
        if not last:
            other_got = swap(own_image)
    space = pl.BlockSpec(memory_space=pltpu.VMEM)
    args = [own_image, own_got, *scale_u, *scale_v]
    mass, tgt_scaling = pl.pallas_call(
        functools.partial(last_body, candidates=float(cand_rows * devices)),
        out_shape=[
            jax.ShapeDtypeStruct(*image_type), jax.ShapeDtypeStruct((CLASSES, tgt_rows), F32)
        ],
        in_specs=[space] * len(args),
        out_specs=[space] * 2,
        compiler_params=pltpu.CompilerParams(vmem_limit_bytes=12 * 1024 * 1024),
    )(*[pltpu.with_memory_space_constraint(a, pltpu.VMEM) for a in args])
    return (potential, tgt_scaling, mass)


def solution(mesh):
    return jax.shard_map(
        shards,
        mesh=mesh,
        in_specs=(
            P(("grp", "row"), None),
            P(("grp", "row")),
            P(("grp", "row"), None),
            P(("grp", "row")),
        ),
        out_specs=(P(None, ("grp", "row")), P(None, ("grp", "row")), P(None, ("grp", "row"))),
        check_vma=False,
    )
```
